32 devices in a mesh: dp: 16 (over z, x, core), tensor: 2 (over y).
Axes of the slice: x: 2, y: 2, z: 4, core: 2. Of those that a mesh axis runs over, the one named last changes fastest.
Arguments:
- inputs: bfloat16 [32, 1024, 768], P(('dp', 'tensor')), may hold values from -6 to 6
- prenorm: float32 [768], replicated, may hold values from 0.5 to 1.5
- gate_weight: bfloat16 [768, 1536], P('dp', 'tensor'), may hold values from -0.21875 to 0.21875
- value_weight: bfloat16 [768, 1536], P('dp', 'tensor'), may hold values from -0.21875 to 0.21875
- state_weight: bfloat16 [768, 256], P('dp'), may hold values from -0.21875 to 0.21875
- step_weight: bfloat16 [768, 24], P('dp', 'tensor'), may hold values from -0.21875 to 0.21875
- value_conv: float32 [4, 1536], P(None, 'tensor'), may hold values from -3 to 3
- value_shift: float32 [1536], P('tensor'), may hold values from -3 to 3
- state_conv: float32 [4, 256], replicated, may hold values from -3 to 3
- state_shift: float32 [256], replicated, may hold values from -3 to 3
- step_shift: float32 [24], P('tensor'), may hold values from -6.5 to -2.5
- decay_log: float32 [24], P('tensor'), may hold values from 0 to 2.7
- skip_scale: float32 [24], P('tensor'), may hold values from 0.5 to 1.5
- gated_gain: float32 [1536], P('tensor'), may hold values from 0.5 to 1.5
- output_matrix: bfloat16 [1536, 768], P('tensor', 'dp'), may hold values from -0.15625 to 0.15625
- cotangent: bfloat16 [32, 1024, 768], P(('dp', 'tensor')), may hold values from -6 to 6
Outputs:
- result: bfloat16 [32, 1024, 768], P(('dp', 'tensor'))
- input_grad: float32 [32, 1024, 768], P(('dp', 'tensor'))
- prenorm_grad: float32 [768], replicated
- gate_grad: float32 [768, 1536], P('dp', 'tensor')
- value_grad: float32 [768, 1536], P('dp', 'tensor')
- state_grad: float32 [768, 256], P('dp')
- step_grad: float32 [768, 24], P('dp', 'tensor')
- valueconv_grad: float32 [4, 1536], P(None, 'tensor')
- valueshift_grad: float32 [1536], P('tensor')
- stateconv_grad: float32 [4, 256], replicated
- stateshift_grad: float32 [256], replicated
- stepshift_grad: float32 [24], P('tensor')
- decay_grad: float32 [24], P('tensor')
- skip_grad: float32 [24], P('tensor')
- gated_grad: float32 [1536], P('tensor')
- out_grad: float32 [1536, 768], P('tensor', 'dp')
The draws below stay inside these ranges and needn't reach their ends.
All inputs are finite; a program needn't handle non-finite values.
Results may differ from the reference program's by a relative error of at most 0.0078.
Values may be sent and summed in bfloat16 or wider, within the bound.
No kernel may reach another device: no remote copies, remote signals or barrier semaphores. Data moves between devices by JAX's collectives and lax.ppermute only.
A program may use at most 192 MiB of HBM per device.

```python
import math
import jax
import jax.numpy as jnp
from jax import lax

D = 768
HEADS = 24
STATE = 128
KCONV = 4
BLOCK = 256
LEN = 1024
INNER = 1536
SEQS = 32


def steps_of(key, dims, shards, smallest, largest):
    gain = 1.0
    for position, parts in shards:
        draws = jax.random.uniform(jax.random.fold_in(jax.random.fold_in(key, 6), position), (parts,), jnp.float32, smallest / len(shards), largest / len(shards))
        gain = gain * jnp.repeat(jnp.exp(draws), dims[position] // parts).reshape((-1,) + (1,) * (len(dims) - 1 - position))
    return gain


def centred(rng, shape, deviation, limit, pieces=(), dtype=jnp.bfloat16):
    values = deviation * jax.random.normal(rng, shape, jnp.float32)
    if pieces:
        values = values * steps_of(rng, shape, pieces, -0.22, 0.18)
    return jnp.clip(values, -limit, limit).astype(dtype)


def setup_inputs(seed: int = 0) -> dict:
    key_of = jax.random.split(jax.random.key(seed), 17)
    return {
        "inputs": centred(key_of[0], (SEQS, LEN, D), 1.0, 6.0, ((0, 32),)),
        "prenorm": jnp.clip(1.0 + 0.1 * jax.random.normal(key_of[1], (D,), jnp.float32), 0.5, 1.5),
        "gate_weight": centred(key_of[2], (D, INNER), D ** -0.5, 0.21875, ((0, 16), (1, 2))),
        "value_weight": centred(key_of[3], (D, INNER), D ** -0.5, 0.21875, ((0, 16), (1, 2))),
        "state_weight": centred(key_of[4], (D, 2 * STATE), D ** -0.5, 0.21875, ((0, 16),)),
        "step_weight": centred(key_of[5], (D, HEADS), D ** -0.5, 0.21875, ((0, 16), (1, 2))),
        "value_conv": centred(key_of[6], (KCONV, INNER), KCONV ** -0.5, 3.0, ((1, 2),), jnp.float32),
        "value_shift": centred(key_of[7], (INNER,), 0.5, 3.0, ((0, 2),), jnp.float32),
        "state_conv": centred(key_of[8], (KCONV, 2 * STATE), KCONV ** -0.5, 3.0, (), jnp.float32),
        "state_shift": centred(key_of[9], (2 * STATE,), 0.5, 3.0, (), jnp.float32),
        "step_shift": jnp.clip(-6.5 + 4.0 * jax.random.uniform(key_of[10], (HEADS,), jnp.float32) ** steps_of(key_of[10], (HEADS,), ((0, 2),), -0.2, 0.2), -6.5, -2.5),
        "decay_log": jnp.clip(2.7 * jax.random.uniform(key_of[11], (HEADS,), jnp.float32) ** steps_of(key_of[11], (HEADS,), ((0, 2),), -0.2, 0.2), 0.0, 2.7),
        "skip_scale": jnp.clip(0.5 + 1.0 * jax.random.uniform(key_of[12], (HEADS,), jnp.float32) ** steps_of(key_of[12], (HEADS,), ((0, 2),), -0.2, 0.2), 0.5, 1.5),
        "gated_gain": jnp.clip(1.0 + 0.1 * jax.random.normal(key_of[13], (INNER,), jnp.float32), 0.5, 1.5),
        "output_matrix": centred(key_of[14], (INNER, D), INNER ** -0.5, 0.15625, ((0, 2), (1, 16))),
        "cotangent": centred(key_of[15], (SEQS, LEN, D), 1.0, 6.0, ((0, 32),)),
    }


exact_precision = lax.Precision.HIGHEST
epsilon = 1e-05

@jax.custom_vjp
def low(v):
    return lax.optimization_barrier(v.astype(jnp.bfloat16)).astype(jnp.float32)

@jax.custom_vjp
def reduced_backward(v):
    return v

def low_keep(v):
    return (low(v), None)

def low_pass(kept, grad):
    return (grad,)

def back_keep(v):
    return (v, None)

def back_low(kept, grad):
    return (low(grad),)
low.defvjp(low_keep, low_pass)
reduced_backward.defvjp(back_keep, back_low)

def causal_conv(signal, kernel, shift):
    taps = kernel.shape[0]
    length = signal.shape[1]
    padded = jnp.pad(signal, ((0, 0), (taps - 1, 0), (0, 0)))
    total = shift + jnp.zeros_like(signal)
    for offset in range(taps):
        total = total + kernel[offset] * padded[:, offset:offset + length, :]
    return total

def ssd_scan(values, step_sizes, decay_rates, write_map, read_map, skip_scale):
    sequences, positions, head_count, head_width = values.shape
    blocks = positions // BLOCK

    def split(array):
        return jnp.moveaxis(array.reshape((sequences, blocks, BLOCK) + array.shape[2:]), 1, 0)
    causal = (jnp.arange(BLOCK)[:, None] >= jnp.arange(BLOCK)[None, :])[None, None]

    def advance(state, block):
        value_blk, step_blk, write_blk, read_blk = block
        logged = jnp.cumsum(jnp.swapaxes(step_blk * decay_rates, 1, 2), axis=2)
        grams = jnp.einsum('sqn,skn->sqk', read_blk, write_blk, precision=exact_precision)
        spread_log = logged[:, :, :, None] - logged[:, :, None, :]
        decay = jnp.where(causal, jnp.exp(jnp.where(causal, spread_log, 0.0)), 0.0)
        mixing = grams[:, None] * decay * jnp.swapaxes(step_blk, 1, 2)[:, :, None, :]
        within = jnp.einsum('shqk,skhp->sqhp', mixing, value_blk, precision=exact_precision)
        carried = jnp.einsum('sqn,shpn->sqhp', read_blk, state, precision=exact_precision)
        carried = carried * jnp.swapaxes(jnp.exp(logged), 1, 2)[..., None]
        remain = jnp.swapaxes(jnp.exp(logged[:, :, -1:] - logged), 1, 2) * step_blk
        update = jnp.einsum('skn,skhp->shpn', write_blk, value_blk * remain[..., None], precision=exact_precision)
        state = state * jnp.exp(logged[:, :, -1])[:, :, None, None] + update
        return (state, within + carried)
    initial = jnp.zeros((sequences, head_count, head_width, write_map.shape[-1]), jnp.float32)
    _, mixed = lax.scan(jax.checkpoint(advance), initial, (split(values), split(step_sizes), split(write_map), split(read_map)))
    mixed = jnp.moveaxis(mixed, 0, 1).reshape(values.shape)
    return mixed + skip_scale[:, None] * values

def head_mixer(value_in, write_map, read_map, step_raw, gate_in, value_conv, value_shift, step_shift, decay_log, skip_scale):
    values = jax.nn.silu(causal_conv(value_in, value_conv, value_shift))
    step_sizes = jax.nn.softplus(step_raw + step_shift)
    sequences, positions, channels = values.shape
    head_count = step_sizes.shape[-1]
    mixed = ssd_scan(values.reshape(sequences, positions, head_count, channels // head_count), step_sizes, -jnp.exp(decay_log), write_map, read_map, skip_scale)
    return mixed.reshape(values.shape) * jax.nn.silu(gate_in)

def state_inputs(state_in, state_conv, state_shift):
    active = jax.nn.silu(causal_conv(state_in, state_conv, state_shift))
    half = active.shape[-1] // 2
    return (active[..., :half], active[..., half:])

def forward(token_rows, prenorm, gate_weight, value_weight, state_weight, step_weight, value_conv, value_shift, state_conv, state_shift, step_shift, decay_log, skip_scale, gated_gain, output_matrix):
    inv_rms = lax.rsqrt(lax.optimization_barrier(jnp.mean(token_rows * token_rows, axis=-1, keepdims=True)) + epsilon)
    normalized_input = low(token_rows * inv_rms * prenorm)

    def project(weight_matrix):
        return reduced_backward(jnp.einsum('bzj,jf->bzf', normalized_input, weight_matrix, precision=exact_precision))
    gate_in = project(gate_weight)
    value_in = project(value_weight)
    state_in = project(state_weight)
    step_raw = project(step_weight)
    write_map, read_map = state_inputs(state_in, state_conv, state_shift)
    mixed = head_mixer(value_in, write_map, read_map, step_raw, gate_in, value_conv, value_shift, step_shift, decay_log, skip_scale)
    gate_rms = lax.rsqrt(lax.optimization_barrier(jnp.mean(mixed * mixed, axis=-1, keepdims=True)) + epsilon)
    gated_result = low(mixed * gate_rms * gated_gain)
    return token_rows + jnp.einsum('kmt,tz->kmz', gated_result, output_matrix, precision=exact_precision)

def reference(inputs, prenorm, gate_weight, value_weight, state_weight, step_weight, value_conv, value_shift, state_conv, state_shift, step_shift, decay_log, skip_scale, gated_gain, output_matrix, cotangent):
    params = tuple((array.astype(jnp.float32) for array in (prenorm, gate_weight, value_weight, state_weight, step_weight, value_conv, value_shift, state_conv, state_shift, step_shift, decay_log, skip_scale, gated_gain, output_matrix)))
    sequences, positions, width = inputs.shape
    group = math.gcd(sequences, max(1, 4096 // positions))
    shape = (sequences // group, group, positions, width)

    def one_group(totals, pair):
        token_rows, grad_out = pair
        value, pullback = jax.vjp(forward, token_rows.astype(jnp.float32), *params)
        grads = pullback(grad_out.astype(jnp.float32))
        totals = tuple((summed + added for summed, added in zip(totals, grads[1:])))
        return (totals, (value.astype(jnp.bfloat16), grads[0]))
    start_sums = tuple((jnp.zeros_like(param) for param in params))
    totals, (results, input_grads) = lax.scan(one_group, start_sums, (inputs.reshape(shape), cotangent.reshape(shape)))
    return (results.reshape(inputs.shape), input_grads.reshape(inputs.shape), totals[0], totals[1], totals[2], totals[3], totals[4], totals[5], totals[6], totals[7], totals[8], totals[9], totals[10], totals[11], totals[12], totals[13])
```

```python
import functools

import jax
import jax.numpy as jnp
from jax import lax
from jax.experimental import pallas as pl
from jax.experimental.pallas import tpu as pltpu
from jax.sharding import PartitionSpec as P

BLOCK = 256
HALVES = 2
PAD = 128
EPS = 1e-05
NEG = -1e30
F32 = jnp.float32
BF16 = jnp.bfloat16
VMEM_BYTES = 56 * 1024 * 1024


def dot(a, b):
    return jnp.dot(a, b, preferred_element_type=F32)


def dot_nt(a, b):
    return lax.dot_general(a, b, (((1,), (1,)), ((), ())), preferred_element_type=F32)


def dot_tn(a, b):
    return lax.dot_general(a, b, (((0,), (0,)), ((), ())), preferred_element_type=F32)


def split3(v):
    high = v.astype(BF16)
    rest = v - high.astype(F32)
    mid = rest.astype(BF16)
    low = (rest - mid.astype(F32)).astype(BF16)
    return high, mid, low


def dot_exact(mask, v):
    high, mid, low = split3(v)
    return dot(mask, high) + dot(mask, mid) + dot(mask, low)


def sigmoid(v):
    return 1.0 / (1.0 + jnp.exp(-v))


def spread(cols, pair, lane_low):
    rows = cols.shape[0]
    left = jnp.broadcast_to(cols[:, 2 * pair : 2 * pair + 1], (rows, 128))
    right = jnp.broadcast_to(cols[:, 2 * pair + 1 : 2 * pair + 2], (rows, 128))
    return jnp.where(lane_low, left, right)


def conv_taps(buf, taps_ref, shift_ref, first, rows):
    total = shift_ref[...] + taps_ref[0:1, :] * buf[pl.ds(first, rows), :]
    for j in range(1, 4):
        total = total + taps_ref[j : j + 1, :] * buf[pl.ds(first + j, rows), :]
    return total


def maps_kernel(
    x_ref, gain_ref, ws_ref, wt0_ref, wt1_ref, taps_ref, shift_ref, tshift_ref, rate_ref,
    normed_ref, statein_ref, statec_ref, maps_ref, mapst_ref, cumc_ref, dtc_ref, sgc_ref, cumr_ref,
    buf,
):
    step = pl.program_id(0)

    @pl.when(step == 0)
    def _():
        buf[pl.ds(0, 8), :] = jnp.zeros((8, buf.shape[1]), F32)

    x = x_ref[0].astype(F32)
    inv = lax.rsqrt(jnp.mean(x * x, axis=-1, keepdims=True) + EPS)
    normed = (x * inv * gain_ref[...]).astype(BF16)
    normed_ref[...] = normed
    state_in = dot(normed, ws_ref[0])
    statein_ref[...] = state_in
    buf[pl.ds(8, BLOCK), :] = state_in
    c = conv_taps(buf, taps_ref, shift_ref, 5, BLOCK)
    buf[pl.ds(0, 8), :] = buf[pl.ds(BLOCK, 8), :]
    statec_ref[...] = c
    maps = c * sigmoid(c)
    maps_ref[...] = maps.astype(BF16)
    mapst_ref[...] = maps.T.astype(BF16)
    row = lax.broadcasted_iota(jnp.int32, (BLOCK, BLOCK), 0)
    col = lax.broadcasted_iota(jnp.int32, (BLOCK, BLOCK), 1)
    lower = jnp.where(row >= col, 1.0, 0.0).astype(BF16)
    for half, wt_ref in enumerate((wt0_ref, wt1_ref)):
        raw = dot(normed, wt_ref[0]) + tshift_ref[half : half + 1, :]
        soft = jnp.exp(-jnp.abs(raw))
        dt = jnp.maximum(raw, 0.0) + jnp.log1p(soft)
        dtc_ref[half] = dt
        sgc_ref[half] = jnp.where(raw >= 0, 1.0, soft) / (1.0 + soft)
        cum = dot_exact(lower, dt * rate_ref[half : half + 1, :])
        cumc_ref[half] = cum
        cumr_ref[half] = cum.T[0:16, :]


def forward_kernel(
    normed_ref, wv_ref, taps_ref, shift_ref, skip_ref, maps_ref, mapst_ref, cumc_ref, dtc_ref, cumr_ref,
    vin_ref, c_ref, y_ref, state_ref,
    buf, state,
):
    step = pl.program_id(1)
    width = buf.shape[1]
    n = state.shape[0]

    @pl.when(step == 0)
    def _():
        buf[pl.ds(0, 8), :] = jnp.zeros((8, width), F32)
        state[...] = jnp.zeros(state.shape, F32)

    value_in = dot(normed_ref[...], wv_ref[0])
    vin_ref[0] = value_in.astype(BF16)
    buf[pl.ds(8, BLOCK), :] = value_in
    c = conv_taps(buf, taps_ref, shift_ref, 5, BLOCK)
    buf[pl.ds(0, 8), :] = buf[pl.ds(BLOCK, 8), :]
    c_ref[0] = c
    state_ref[0, 0] = state[...]
    write = maps_ref[:, 0:n]
    read = maps_ref[:, n : 2 * n]
    write_t = mapst_ref[0:n, :]
    grams = dot_nt(read, write)
    carried = dot(read, state[...].astype(BF16))
    cumc = cumc_ref[0]
    dtc = dtc_ref[0]
    ecum = jnp.exp(cumc)
    rem = jnp.exp(cumc[BLOCK - 1 : BLOCK, :] - cumc) * dtc
    lane_low = lax.broadcasted_iota(jnp.int32, (BLOCK, 128), 1) < 64
    hb = BLOCK // 2
    tri = lax.broadcasted_iota(jnp.int32, (hb, hb), 0) >= lax.broadcasted_iota(jnp.int32, (hb, hb), 1)
    zeros = jnp.zeros((hb, hb), BF16)
    g00 = grams[0:hb, 0:hb]
    g10 = grams[hb:, 0:hb]
    g11 = grams[hb:, hb:]
    for pair in range(width // 128):
        lanes = slice(pair * 128, pair * 128 + 128)
        cp = c[:, lanes]
        v = cp * sigmoid(cp)
        vdt = (v * spread(dtc, pair, lane_low)).astype(BF16)
        outs = []
        for j in range(2):
            h = 2 * pair + j
            cq = jnp.broadcast_to(cumc[:, h : h + 1], (BLOCK, hb))
            ck = cumr_ref[0, h : h + 1, :]
            d00 = jnp.exp(jnp.where(tri, cq[0:hb] - ck[:, 0:hb], NEG))
            d10 = jnp.exp(cq[hb:] - ck[:, 0:hb])
            d11 = jnp.exp(jnp.where(tri, cq[hb:] - ck[:, hb:], NEG))
            top = jnp.concatenate([(g00 * d00).astype(BF16), zeros], axis=1)
            bot = jnp.concatenate([(g10 * d10).astype(BF16), (g11 * d11).astype(BF16)], axis=1)
            outs.append(dot(jnp.concatenate([top, bot], axis=0), vdt))
        ec = spread(ecum, pair, lane_low)
        y = jnp.where(lane_low, outs[0], outs[1]) + ec * carried[:, lanes] + skip_ref[:, lanes] * v
        y_ref[0, :, lanes] = y
        vrem = (v * spread(rem, pair, lane_low)).astype(BF16)
        state[:, lanes] = state[:, lanes] * ec[BLOCK - 1 : BLOCK, :] + dot(write_t, vrem)


def gated_kernel(
    x_ref, cot_ref, normed_ref, y_ref, wg_ref, wo_ref, gain_ref,
    result_ref, dy_ref, dgate_ref, outg_ref, gateg_ref, gaing_ref,
):
    step = pl.program_id(0)

    @pl.when(step == 0)
    def _():
        outg_ref[...] = jnp.zeros(outg_ref.shape, F32)
        gateg_ref[...] = jnp.zeros(gateg_ref.shape, F32)
        gaing_ref[...] = jnp.zeros(gaing_ref.shape, F32)

    width = wg_ref.shape[2]
    normed = normed_ref[...]
    cot = cot_ref[0]
    gates, mixes = [], []
    squares = 0.0
    for half in range(HALVES):
        gate = dot(normed, wg_ref[half])
        mixed = y_ref[half] * (gate * sigmoid(gate))
        squares = squares + jnp.sum(mixed * mixed, axis=-1, keepdims=True)
        gates.append(gate)
        mixes.append(mixed)
    rms = lax.rsqrt(squares / (HALVES * width) + EPS)
    total = x_ref[0].astype(F32)
    inner = 0.0
    scaled = []
    for half in range(HALVES):
        gain = gain_ref[half : half + 1, :]
        gated = (mixes[half] * rms * gain).astype(BF16)
        total = total + dot_nt(gated, wo_ref[half])
        outg_ref[half] += dot_tn(cot, gated)
        grad = dot(cot, wo_ref[half])
        gaing_ref[half : half + 1, :] += jnp.sum(grad * mixes[half] * rms, axis=0, keepdims=True)
        grad = grad * gain
        inner = inner + jnp.sum(grad * mixes[half], axis=-1, keepdims=True)
        scaled.append(grad)
    result_ref[0] = total.astype(BF16)
    factor = rms * rms * rms * (inner / (HALVES * width))
    for half in range(HALVES):
        grad_mixed = rms * scaled[half] - mixes[half] * factor
        gate = gates[half]
        sg = sigmoid(gate)
        dy_ref[half] = (grad_mixed * (gate * sg)).astype(BF16)
        dgate = (grad_mixed * y_ref[half] * (sg * (1.0 + gate * (1.0 - sg)))).astype(BF16)
        dgate_ref[half] = dgate
        gateg_ref[half] += dot_tn(normed, dgate)


def backward_kernel(
    c_ref, vin_ref, dy_ref, state_ref, maps_ref, mapst_ref, cumc_ref, dtc_ref, sgc_ref, cumr_ref,
    taps_ref, skip_ref, rate_ref,
    dvin_ref, dmaps_ref, dstep_ref, tapsg_ref, headg_ref,
    buf, dstate, dgt, uacc, vacc,
):
    step = pl.program_id(1)
    width = buf.shape[1]
    n = dstate.shape[0]
    hb = BLOCK // 2

    @pl.when(step == 0)
    def _():
        buf[pl.ds(BLOCK, 8), :] = jnp.zeros((8, width), F32)
        dstate[...] = jnp.zeros(dstate.shape, F32)
        tapsg_ref[...] = jnp.zeros(tapsg_ref.shape, F32)
        headg_ref[...] = jnp.zeros(headg_ref.shape, F32)

    write = maps_ref[:, 0:n]
    read = maps_ref[:, n : 2 * n]
    read_t = mapst_ref[n : 2 * n, :]
    gt = dot_nt(write, read)
    state = state_ref[0, 0]
    ds = dstate[...]
    ds_b = ds.astype(BF16)
    carried = dot(read, state.astype(BF16))
    wds = dot(write, ds_b)
    cumc = cumc_ref[0]
    dtc = dtc_ref[0]
    ecum = jnp.exp(cumc)
    last = jnp.exp(cumc[BLOCK - 1 : BLOCK, :] - cumc)
    rem = last * dtc
    lane = lax.broadcasted_iota(jnp.int32, (BLOCK, 128), 1)
    lane_low = lane < 64
    sub = lax.broadcasted_iota(jnp.int32, (16, BLOCK), 0)
    tri = lax.broadcasted_iota(jnp.int32, (hb, hb), 1) >= lax.broadcasted_iota(jnp.int32, (hb, hb), 0)
    zeros = jnp.zeros((hb, hb), BF16)
    g00 = gt[0:hb, 0:hb]
    g01 = gt[0:hb, hb:]
    g11 = gt[hb:, hb:]
    dgt[...] = jnp.zeros(dgt.shape, F32)
    to_k = jnp.zeros((BLOCK, 128), F32)
    to_q = jnp.zeros((16, BLOCK), F32)
    for pair in range(width // 128):
        lanes = slice(pair * 128, pair * 128 + 128)
        cp = c_ref[0, :, lanes]
        v = cp * sigmoid(cp)
        vacc[:, lanes] = v
        dt_s = spread(dtc, pair, lane_low)
        vdt = (v * dt_s).astype(BF16)
        dyp = dy_ref[0, :, lanes]
        us = []
        for j in range(2):
            h = 2 * pair + j
            ck = jnp.broadcast_to(cumc[:, h : h + 1], (BLOCK, hb))
            cq = cumr_ref[0, h : h + 1, :]
            d00 = jnp.exp(jnp.where(tri, cq[:, 0:hb] - ck[0:hb], NEG))
            d01 = jnp.exp(cq[:, hb:] - ck[0:hb])
            d11 = jnp.exp(jnp.where(tri, cq[:, hb:] - ck[hb:], NEG))
            mine = jnp.where(lane_low if j == 0 else jnp.logical_not(lane_low), dyp, jnp.zeros_like(dyp))
            qt = dot_nt(vdt, mine)
            e00 = d00 * qt[0:hb, 0:hb]
            e01 = d01 * qt[0:hb, hb:]
            e11 = d11 * qt[hb:, hb:]
            dgt[0:hb, 0:hb] += e00
            dgt[0:hb, hb:] += e01
            dgt[hb:, hb:] += e11
            a = jnp.concatenate(
                [
                    jnp.concatenate([(g00 * d00).astype(BF16), (g01 * d01).astype(BF16)], axis=1),
                    jnp.concatenate([zeros, (g11 * d11).astype(BF16)], axis=1),
                ],
                axis=0,
            )
            z = jnp.concatenate(
                [
                    jnp.concatenate([(g00 * e00).astype(BF16), (g01 * e01).astype(BF16)], axis=1),
                    jnp.concatenate([zeros, (g11 * e11).astype(BF16)], axis=1),
                ],
                axis=0,
            )
            us.append(dot(a, dyp))
            to_k = to_k + dot(z, jnp.where(lane == h, 1.0, 0.0).astype(BF16))
            to_q = to_q + dot(jnp.where(sub == h, 1.0, 0.0).astype(BF16), z)
        uacc[:, lanes] = jnp.where(lane_low, us[0], us[1])
        ec = spread(ecum, pair, lane_low)
        dye = (dyp.astype(F32) * ec).astype(BF16)
        u = uacc[:, lanes]
        dv = dt_s * u + skip_ref[:, lanes] * dyp.astype(F32) + spread(rem, pair, lane_low) * wds[:, lanes]
        sg = sigmoid(cp)
        buf[0:BLOCK, lanes] = dv * (sg * (1.0 + cp * (1.0 - sg)))
        dstate[:, lanes] = ds[:, lanes] * ec[BLOCK - 1 : BLOCK, :] + dot(read_t, dye)
        vrem = (v * spread(rem, pair, lane_low)).astype(BF16)
        dmw = dot_nt(vrem, ds_b[:, lanes])
        dmr = dot_nt(dye, state[:, lanes].astype(BF16))
        if pair == 0:
            dmaps_w, dmaps_r = dmw, dmr
        else:
            dmaps_w, dmaps_r = dmaps_w + dmw, dmaps_r + dmr
    dg_b = dgt[...].astype(BF16)
    dmaps_ref[0, :, 0:n] = dmaps_w + dot(dg_b, read)
    dmaps_ref[0, :, n : 2 * n] = dmaps_r + dot_tn(dg_b, write)

    row = lax.broadcasted_iota(jnp.int32, (width, 128), 0)
    col = lax.broadcasted_iota(jnp.int32, (width, 128), 1)
    pick = jnp.where(row // 64 == col, 1.0, 0.0).astype(BF16)

    def per_head(values):
        high = values.astype(BF16)
        low = (values - high.astype(F32)).astype(BF16)
        return dot(high, pick) + dot(low, pick)

    v = vacc[...]
    dy = dy_ref[0].astype(F32)
    v_u = per_head(v * uacc[...])
    v_wds = per_head(v * wds)
    dy_c = per_head(dy * carried)
    skip_sum = jnp.sum(dy * v, axis=0, keepdims=True)
    ss = per_head(jnp.broadcast_to(jnp.sum(ds * state, axis=0, keepdims=True), (8, width)))
    sent = rem * v_wds
    d_last = ecum[BLOCK - 1 : BLOCK, :] * ss[0:1, :] + jnp.sum(sent, axis=0, keepdims=True)
    dcum = jnp.concatenate([to_q, jnp.zeros((112, BLOCK), F32)], axis=0).T - to_k + ecum * dy_c - sent
    token = lax.broadcasted_iota(jnp.int32, (BLOCK, 128), 0)
    dcum = dcum + jnp.where(token == BLOCK - 1, d_last, 0.0)
    row = lax.broadcasted_iota(jnp.int32, (BLOCK, BLOCK), 0)
    col = lax.broadcasted_iota(jnp.int32, (BLOCK, BLOCK), 1)
    upper = jnp.where(row <= col, 1.0, 0.0).astype(BF16)
    dlog = dot_exact(upper, dcum)
    rate = rate_ref[0]
    ddt = v_u + last * v_wds + dlog * rate
    draw = ddt * sgc_ref[0]
    dstep_ref[0] = draw.astype(BF16)
    headg_ref[0, 0:1, :] += jnp.sum(draw, axis=0, keepdims=True)
    headg_ref[0, 1:2, :] += jnp.sum(dlog * dtc, axis=0, keepdims=True) * rate
    headg_ref[0, 2:3, :] += per_head(jnp.broadcast_to(skip_sum, (8, width)))[0:1, :]

    vin = vin_ref[0].astype(F32)
    total = jnp.zeros((BLOCK, width), F32)
    for j in range(4):
        shifted = buf[pl.ds(3 - j, BLOCK), :]
        total = total + taps_ref[j : j + 1, :] * shifted
        tapsg_ref[0, j : j + 1, :] += jnp.sum(shifted * vin, axis=0, keepdims=True)
    tapsg_ref[0, 4:5, :] += jnp.sum(buf[0:BLOCK, :], axis=0, keepdims=True)
    dvin_ref[0] = total.astype(BF16)
    buf[pl.ds(BLOCK, 8), :] = buf[pl.ds(0, 8), :]


def state_kernel(dmaps_ref, statein_ref, statec_ref, taps_ref, dstate_ref, tapsg_ref, buf):
    length, width = statein_ref.shape
    c = statec_ref[...]
    sg = sigmoid(c)
    dc = (dmaps_ref[0] + dmaps_ref[1]) * (sg * (1.0 + c * (1.0 - sg)))
    buf[0:length, :] = dc
    buf[pl.ds(length, 8), :] = jnp.zeros((8, width), F32)
    state_in = statein_ref[...]
    total = jnp.zeros((length, width), F32)
    tapsg_ref[...] = jnp.zeros(tapsg_ref.shape, F32)
    for j in range(4):
        shifted = buf[pl.ds(3 - j, length), :]
        total = total + taps_ref[j : j + 1, :] * shifted
        tapsg_ref[j : j + 1, :] = jnp.sum(shifted * state_in, axis=0, keepdims=True)
    tapsg_ref[4:5, :] = jnp.sum(dc, axis=0, keepdims=True)
    dstate_ref[...] = total.astype(BF16)


def input_kernel(
    x_ref, cot_ref, gain_ref, dgate_ref, dvin_ref, dstate_ref, dstep_ref, wg_ref, wv_ref, ws_ref, wt0_ref, wt1_ref,
    grad_ref, gaing_ref,
):
    step = pl.program_id(0)

    @pl.when(step == 0)
    def _():
        gaing_ref[...] = jnp.zeros(gaing_ref.shape, F32)

    total = dot_nt(dstate_ref[...], ws_ref[0])
    for half, wt_ref in enumerate((wt0_ref, wt1_ref)):
        total = total + dot_nt(dgate_ref[half], wg_ref[half])
        total = total + dot_nt(dvin_ref[half], wv_ref[half])
        total = total + dot_nt(dstep_ref[half], wt_ref[0])
    x = x_ref[0].astype(F32)
    inv = lax.rsqrt(jnp.mean(x * x, axis=-1, keepdims=True) + EPS)
    gaing_ref[0:1, :] += jnp.sum(total * x * inv, axis=0, keepdims=True)
    scaled = total * gain_ref[...]
    inner = jnp.mean(scaled * x, axis=-1, keepdims=True)
    grad_ref[0] = cot_ref[0].astype(F32) + inv * scaled - x * (inv * inv * inv * inner)


def call(body, grid, in_specs, out_specs, out_shape, scratch=(), flops=0):
    return pl.pallas_call(
        body,
        grid=grid,
        in_specs=in_specs,
        out_specs=out_specs,
        out_shape=out_shape,
        scratch_shapes=list(scratch),
        compiler_params=pltpu.CompilerParams(
            vmem_limit_bytes=VMEM_BYTES, dimension_semantics=("arbitrary",) * len(grid)
        ),
        cost_estimate=pl.CostEstimate(flops=flops, bytes_accessed=10_000_000, transcendentals=0),
    )


def shape(dims, dtype=F32):
    return jax.ShapeDtypeStruct(dims, dtype)


def fixed(dims, *index):
    return pl.BlockSpec(dims, lambda *_: index)


def local(
    inputs,
    prenorm,
    gate_weight,
    value_weight,
    state_weight,
    step_weight,
    value_conv,
    value_shift,
    state_conv,
    state_shift,
    step_shift,
    decay_log,
    skip_scale,
    gated_gain,
    output_matrix,
    cotangent,
):
    both = ("tensor", "dp")
    place = lax.axis_index("tensor")
    length, width = inputs.shape[1:]
    rows, half_width = gate_weight.shape
    heads = step_weight.shape[1]
    n = state_weight.shape[1] // 2
    blocks = length // BLOCK
    head_width = half_width // heads

    def lanes_of(v):
        return jnp.pad(v, ((0, 0), (0, PAD - v.shape[1])))

    pack = jnp.concatenate([value_weight, state_weight, lanes_of(step_weight)], axis=1)
    first = lax.all_gather(pack, both, axis=0, tiled=True).reshape(HALVES, width, pack.shape[1])
    pack = jnp.concatenate([gate_weight, output_matrix.T], axis=1)
    second = lax.all_gather(pack, both, axis=0, tiled=True).reshape(HALVES, width, pack.shape[1])
    small = jnp.concatenate(
        [
            value_conv.reshape(-1), value_shift, jnp.repeat(skip_scale, head_width), gated_gain,
            lanes_of(step_shift[None]).reshape(-1), lanes_of(-jnp.exp(decay_log)[None]).reshape(-1),
        ]
    )
    small = lax.all_gather(small, "tensor", axis=0)
    w = half_width
    value_taps = jnp.moveaxis(small[:, : 4 * w].reshape(HALVES, 4, w), 0, 1).reshape(4, HALVES * w)
    value_bias = small[:, 4 * w : 5 * w].reshape(1, HALVES * w)
    skip = small[:, 5 * w : 6 * w].reshape(1, HALVES * w)
    gain = small[:, 6 * w : 7 * w]
    step_bias = small[:, 7 * w : 7 * w + PAD]
    rate = small[:, 7 * w + PAD :]

    ws_spec = fixed((1, width, 2 * n), 0, 0, w // (2 * n))
    wt_specs = [fixed((1, width, PAD), half, 0, (w + 2 * n) // PAD) for half in range(HALVES)]
    row_block = lambda dims, dtype=None: pl.BlockSpec(dims, lambda b: (b, 0))
    tokens = pl.BlockSpec((1, BLOCK, width), lambda b: (0, b, 0))
    halves = lambda last: pl.BlockSpec((HALVES, BLOCK, last), lambda b: (0, b, 0))

    normed, state_in, state_c, maps, maps_t, cumc, dtc, sgc, cumr = call(
        maps_kernel,
        (blocks,),
        [tokens, fixed((1, width), 0, 0), ws_spec, *wt_specs, fixed((4, 2 * n), 0, 0), fixed((1, 2 * n), 0, 0),
         fixed((HALVES, PAD), 0, 0), fixed((HALVES, PAD), 0, 0)],
        [row_block((BLOCK, width)), row_block((BLOCK, 2 * n)), row_block((BLOCK, 2 * n)), row_block((BLOCK, 2 * n)),
         pl.BlockSpec((2 * n, BLOCK), lambda b: (0, b)), halves(PAD), halves(PAD), halves(PAD),
         pl.BlockSpec((HALVES, 16, BLOCK), lambda b: (0, 0, b))],
        [shape((length, width), BF16), shape((length, 2 * n)), shape((length, 2 * n)), shape((length, 2 * n), BF16),
         shape((2 * n, length), BF16), shape((HALVES, length, PAD)), shape((HALVES, length, PAD)),
         shape((HALVES, length, PAD)), shape((HALVES, 16, length))],
        [pltpu.VMEM((BLOCK + 8, 2 * n), F32)],
        flops=2 * length * width * 512,
    )(inputs, prenorm[None], first, first, first, state_conv, state_shift[None], step_bias, rate)

    def fwd(dims):
        return pl.BlockSpec(dims, lambda h, b: (h, b, 0))

    def channel(dims):
        return pl.BlockSpec(dims, lambda h, b: (0, h))

    value_in, value_c, mixed, states = call(
        forward_kernel,
        (HALVES, blocks),
        [pl.BlockSpec((BLOCK, width), lambda h, b: (b, 0)), pl.BlockSpec((1, width, w), lambda h, b: (h, 0, 0)),
         channel((4, w)), channel((1, w)), channel((1, w)),
         pl.BlockSpec((BLOCK, 2 * n), lambda h, b: (b, 0)), pl.BlockSpec((2 * n, BLOCK), lambda h, b: (0, b)),
         fwd((1, BLOCK, PAD)), fwd((1, BLOCK, PAD)), pl.BlockSpec((1, 16, BLOCK), lambda h, b: (h, 0, b))],
        [fwd((1, BLOCK, w)), fwd((1, BLOCK, w)), fwd((1, BLOCK, w)),
         pl.BlockSpec((1, 1, n, w), lambda h, b: (h, b, 0, 0))],
        [shape((HALVES, length, w), BF16), shape((HALVES, length, w)), shape((HALVES, length, w)),
         shape((HALVES, blocks, n, w))],
        [pltpu.VMEM((BLOCK + 8, w), F32), pltpu.VMEM((n, w), F32)],
        flops=20_000_000_000,
    )(normed, first, value_taps, value_bias, skip, maps, maps_t, cumc, dtc, cumr)

    wg_spec = fixed((HALVES, width, w), 0, 0, 0)
    result, dy, dgate, out_partial, gate_partial, gain_partial = call(
        gated_kernel,
        (blocks,),
        [tokens, tokens, row_block((BLOCK, width)), halves(w), wg_spec, fixed((HALVES, width, w), 0, 0, 1),
         fixed((HALVES, w), 0, 0)],
        [tokens, halves(w), halves(w), fixed((HALVES, width, w), 0, 0, 0), fixed((HALVES, width, w), 0, 0, 0),
         fixed((HALVES, w), 0, 0)],
        [shape(inputs.shape, BF16), shape((HALVES, length, w), BF16), shape((HALVES, length, w), BF16),
         shape((HALVES, width, w)), shape((HALVES, width, w)), shape((HALVES, w))],
        flops=20_000_000_000,
    )(inputs, cotangent, normed, mixed, second, second, gain)

    back = lambda dims: pl.BlockSpec(dims, lambda h, b: (h, blocks - 1 - b, 0))
    dvalue, dmaps, dstep, taps_partial, head_partial = call(
        backward_kernel,
        (HALVES, blocks),
        [back((1, BLOCK, w)), back((1, BLOCK, w)), back((1, BLOCK, w)),
         pl.BlockSpec((1, 1, n, w), lambda h, b: (h, blocks - 1 - b, 0, 0)),
         pl.BlockSpec((BLOCK, 2 * n), lambda h, b: (blocks - 1 - b, 0)),
         pl.BlockSpec((2 * n, BLOCK), lambda h, b: (0, blocks - 1 - b)),
         back((1, BLOCK, PAD)), back((1, BLOCK, PAD)), back((1, BLOCK, PAD)),
         pl.BlockSpec((1, 16, BLOCK), lambda h, b: (h, 0, blocks - 1 - b)),
         channel((4, w)), channel((1, w)), pl.BlockSpec((1, 1, PAD), lambda h, b: (h, 0, 0))],
        [back((1, BLOCK, w)), back((1, BLOCK, 2 * n)), back((1, BLOCK, PAD)),
         pl.BlockSpec((1, 8, w), lambda h, b: (h, 0, 0)), pl.BlockSpec((1, 8, PAD), lambda h, b: (h, 0, 0))],
        [shape((HALVES, length, w), BF16), shape((HALVES, length, 2 * n)), shape((HALVES, length, PAD), BF16),
         shape((HALVES, 8, w)), shape((HALVES, 8, PAD))],
        [pltpu.VMEM((BLOCK + 8, w), F32), pltpu.VMEM((n, w), F32), pltpu.VMEM((BLOCK, BLOCK), F32),
         pltpu.VMEM((BLOCK, w), F32), pltpu.VMEM((BLOCK, w), F32)],
        flops=40_000_000_000,
    )(value_c, value_in, dy, states, maps, maps_t, cumc, dtc, sgc, cumr, value_taps, skip, rate[:, None, :])

    dstate, state_taps = call(
        state_kernel,
        (1,),
        [fixed((HALVES, length, 2 * n), 0, 0, 0), fixed((length, 2 * n), 0, 0), fixed((length, 2 * n), 0, 0),
         fixed((4, 2 * n), 0, 0)],
        [fixed((length, 2 * n), 0, 0), fixed((8, 2 * n), 0, 0)],
        [shape((length, 2 * n), BF16), shape((8, 2 * n))],
        [pltpu.VMEM((length + 8, 2 * n), F32)],
        flops=1_000_000_000,
    )(dmaps, state_in, state_c, state_conv)

    input_grad, prenorm_partial = call(
        input_kernel,
        (blocks,),
        [tokens, tokens, fixed((1, width), 0, 0), halves(w), halves(w), row_block((BLOCK, 2 * n)), halves(PAD),
         wg_spec, wg_spec, ws_spec, *wt_specs],
        [tokens, fixed((8, width), 0, 0)],
        [shape(inputs.shape), shape((8, width))],
        flops=6_000_000_000,
    )(inputs, cotangent, prenorm[None], dgate, dvalue, dstate, dstep, second, first, first, first, first)

    value_partial = jnp.einsum("tk,htf->hkf", normed, dvalue, preferred_element_type=F32)
    state_partial = jnp.einsum("tk,tf->kf", normed, dstate, preferred_element_type=F32)
    step_partial = jnp.einsum("tk,htf->hkf", normed, dstep, preferred_element_type=F32)
    late = jnp.concatenate(
        [value_partial, jnp.broadcast_to(state_partial[None], (HALVES,) + state_partial.shape), step_partial], axis=2
    )
    early = jnp.concatenate([gate_partial, out_partial], axis=2)
    late = lax.psum_scatter(late.reshape(HALVES * width, -1), both, scatter_dimension=0, tiled=True)
    early = lax.psum_scatter(early.reshape(HALVES * width, -1), both, scatter_dimension=0, tiled=True)
    smalls = lax.psum(
        (taps_partial, head_partial, gain_partial, state_taps, prenorm_partial), both
    )
    taps_sum, head_sum, gain_sum, state_taps, prenorm_sum = smalls
    pick = lambda v: lax.dynamic_index_in_dim(v, place, 0, keepdims=False)
    taps_sum, head_sum, gain_sum = pick(taps_sum), pick(head_sum), pick(gain_sum)
    return (
        result,
        input_grad,
        prenorm_sum[0],
        early[:, :w],
        late[:, :w],
        late[:, w : w + 2 * n],
        late[:, w + 2 * n : w + 2 * n + heads],
        taps_sum[0:4],
        taps_sum[4],
        state_taps[0:4],
        state_taps[4],
        head_sum[0, :heads],
        head_sum[1, :heads],
        head_sum[2, :heads],
        gain_sum,
        early[:, w:].T,
    )


def solution(mesh):
    in_specs = (
        P(("dp", "tensor"), None, None),
        P(),
        P("dp", "tensor"),
        P("dp", "tensor"),
        P("dp", None),
        P("dp", "tensor"),
        P(None, "tensor"),
        P("tensor"),
        P(),
        P(),
        P("tensor"),
        P("tensor"),
        P("tensor"),
        P("tensor"),
        P("tensor", "dp"),
        P(("dp", "tensor"), None, None),
    )
    out_specs = (
        P(("dp", "tensor"), None, None),
        P(("dp", "tensor"), None, None),
        P(),
        P("dp", "tensor"),
        P("dp", "tensor"),
        P("dp", None),
        P("dp", "tensor"),
        P(None, "tensor"),
        P("tensor"),
        P(),
        P(),
        P("tensor"),
        P("tensor"),
        P("tensor"),
        P("tensor"),
        P("tensor", "dp"),
    )
    return jax.shard_map(local, mesh=mesh, in_specs=in_specs, out_specs=out_specs, check_vma=False)
```

```python
import functools

import jax
import jax.numpy as jnp
from jax import lax
from jax.experimental import pallas as pl
from jax.experimental.pallas import tpu as pltpu
from jax.sharding import PartitionSpec as P

BLOCK = 256
HALVES = 2
PAD = 128
SEGMENTS = 2
EPS = 1e-05
NEG = -1e30
F32 = jnp.float32
BF16 = jnp.bfloat16
VMEM_BYTES = 56 * 1024 * 1024


def dot(a, b):
    return jnp.dot(a, b, preferred_element_type=F32)


def dot_nt(a, b):
    return lax.dot_general(a, b, (((1,), (1,)), ((), ())), preferred_element_type=F32)


def dot_tn(a, b):
    return lax.dot_general(a, b, (((0,), (0,)), ((), ())), preferred_element_type=F32)


def split3(v):
    high = v.astype(BF16)
    rest = v - high.astype(F32)
    mid = rest.astype(BF16)
    low = (rest - mid.astype(F32)).astype(BF16)
    return high, mid, low


def dot_exact(mask, v):
    high, mid, low = split3(v)
    return dot(mask, high) + dot(mask, mid) + dot(mask, low)


def sigmoid(v):
    return 1.0 / (1.0 + jnp.exp(-v))


def spread(cols, pair, lane_low):
    rows = cols.shape[0]
    left = jnp.broadcast_to(cols[:, 2 * pair : 2 * pair + 1], (rows, 128))
    right = jnp.broadcast_to(cols[:, 2 * pair + 1 : 2 * pair + 2], (rows, 128))
    return jnp.where(lane_low, left, right)


def conv_taps(buf, taps_ref, shift_ref, first, rows):
    total = shift_ref[...] + taps_ref[0:1, :] * buf[pl.ds(first, rows), :]
    for j in range(1, 4):
        total = total + taps_ref[j : j + 1, :] * buf[pl.ds(first + j, rows), :]
    return total


def load_rows(pieces, target, sems, first=0, lanes=None):
    copies = []
    for i, piece in enumerate(pieces):
        rows = piece.shape[0]
        source = piece if lanes is None else piece.at[:, lanes]
        copies.append(pltpu.make_async_copy(source, target.at[pl.ds(i * rows, rows), :], sems.at[first + i]))
    for copy in copies:
        copy.start()
    return copies


def maps_kernel(
    x_ref, gain_ref, pm_ref, pmt_ref, own0, own1, own2, own3, oth0, oth1, oth2, oth3,
    taps_ref, shift_ref, tshift_ref, rate_ref,
    normed_ref, normedt_ref, statein_ref, statec_ref, maps_ref, mapst_ref, cumc_ref, dtc_ref, sgc_ref, cumr_ref,
    buf, wown, woth, sems,
):
    step = pl.program_id(0)
    n2 = buf.shape[1]

    @pl.when(step == 0)
    def _():
        copies = load_rows((own0, own1, own2, own3), wown, sems)
        copies += load_rows((oth0, oth1, oth2, oth3), woth, sems, 4)
        buf[pl.ds(0, 8), :] = jnp.zeros((8, n2), F32)
        for copy in copies:
            copy.wait()

    x = x_ref[0].astype(F32)
    inv = lax.rsqrt(jnp.mean(x * x, axis=-1, keepdims=True) + EPS)
    normed = (x * inv * gain_ref[...]).astype(BF16)
    normedt_ref[...] = dot_nt(pmt_ref[...], normed).astype(BF16)
    normed = dot(normed, pm_ref[...]).astype(BF16)
    normed_ref[...] = normed
    proj = dot(normed, wown[...])
    state_in = proj[:, 0:n2]
    statein_ref[...] = state_in
    buf[pl.ds(8, BLOCK), :] = state_in
    c = conv_taps(buf, taps_ref, shift_ref, 5, BLOCK)
    buf[pl.ds(0, 8), :] = buf[pl.ds(BLOCK, 8), :]
    statec_ref[...] = c
    maps = c * sigmoid(c)
    maps_ref[...] = maps.astype(BF16)
    mapst_ref[...] = maps.T.astype(BF16)
    row = lax.broadcasted_iota(jnp.int32, (BLOCK, BLOCK), 0)
    col = lax.broadcasted_iota(jnp.int32, (BLOCK, BLOCK), 1)
    lower = jnp.where(row >= col, 1.0, 0.0).astype(BF16)
    for half, raw in enumerate((proj[:, n2:], dot(normed, woth[...]))):
        raw = raw + tshift_ref[half : half + 1, :]
        soft = jnp.exp(-jnp.abs(raw))
        dt = jnp.maximum(raw, 0.0) + jnp.log1p(soft)
        dtc_ref[half] = dt
        sgc_ref[half] = jnp.where(raw >= 0, 1.0, soft) / (1.0 + soft)
        cum = dot_exact(lower, dt * rate_ref[half : half + 1, :])
        cumc_ref[half] = cum
        cumr_ref[half] = cum.T[0:16, :]


def forward_kernel(
    normed_ref, piece0, piece1, piece2, piece3, taps_ref, shift_ref, skip_ref, maps_ref, mapst_ref,
    cumc_ref, dtc_ref, cumr_ref,
    vin_ref, c_ref, y_ref, state_ref,
    buf, state, wv, sems,
):
    step = pl.program_id(0)
    width = buf.shape[1]
    n = state.shape[0]

    @pl.when(step == 0)
    def _():
        copies = load_rows((piece0, piece1, piece2, piece3), wv, sems)
        buf[pl.ds(0, 8), :] = jnp.zeros((8, width), F32)
        state[...] = jnp.zeros(state.shape, F32)
        for copy in copies:
            copy.wait()

    value_in = dot(normed_ref[...], wv[...])
    vin_ref[...] = value_in.astype(BF16)
    buf[pl.ds(8, BLOCK), :] = value_in
    c = conv_taps(buf, taps_ref, shift_ref, 5, BLOCK)
    buf[pl.ds(0, 8), :] = buf[pl.ds(BLOCK, 8), :]
    c_ref[...] = c
    state_ref[0] = state[...]
    write = maps_ref[:, 0:n]
    read = maps_ref[:, n : 2 * n]
    write_t = mapst_ref[0:n, :]
    grams = dot_nt(read, write)
    carried = dot(read, state[...].astype(BF16))
    cumc = cumc_ref[0]
    dtc = dtc_ref[0]
    ecum = jnp.exp(cumc)
    rem = jnp.exp(cumc[BLOCK - 1 : BLOCK, :] - cumc) * dtc
    lane_low = lax.broadcasted_iota(jnp.int32, (BLOCK, 128), 1) < 64
    hb = BLOCK // 2
    tri = lax.broadcasted_iota(jnp.int32, (hb, hb), 0) >= lax.broadcasted_iota(jnp.int32, (hb, hb), 1)
    zeros = jnp.zeros((hb, hb), BF16)
    g00 = grams[0:hb, 0:hb]
    g10 = grams[hb:, 0:hb]
    g11 = grams[hb:, hb:]
    for pair in range(width // 128):
        lanes = slice(pair * 128, pair * 128 + 128)
        cp = c[:, lanes]
        v = cp * sigmoid(cp)
        vdt = (v * spread(dtc, pair, lane_low)).astype(BF16)
        outs = []
        for j in range(2):
            h = 2 * pair + j
            cq = jnp.broadcast_to(cumc[:, h : h + 1], (BLOCK, hb))
            ck = cumr_ref[0, h : h + 1, :]
            d00 = jnp.exp(jnp.where(tri, cq[0:hb] - ck[:, 0:hb], NEG))
            d10 = jnp.exp(cq[hb:] - ck[:, 0:hb])
            d11 = jnp.exp(jnp.where(tri, cq[hb:] - ck[:, hb:], NEG))
            top = jnp.concatenate([(g00 * d00).astype(BF16), zeros], axis=1)
            bot = jnp.concatenate([(g10 * d10).astype(BF16), (g11 * d11).astype(BF16)], axis=1)
            outs.append(dot(jnp.concatenate([top, bot], axis=0), vdt))
        ec = spread(ecum, pair, lane_low)
        y = jnp.where(lane_low, outs[0], outs[1]) + ec * carried[:, lanes] + skip_ref[:, lanes] * v
        y_ref[:, lanes] = y
        vrem = (v * spread(rem, pair, lane_low)).astype(BF16)
        state[:, lanes] = state[:, lanes] * ec[BLOCK - 1 : BLOCK, :] + dot(write_t, vrem)


def gated_kernel(
    x_ref, cot_ref, normed_ref, normedt_ref, y0_ref, y1_ref, gain_ref, pm_ref, pmt_ref,
    own0, own1, own2, own3, oth0, oth1, oth2, oth3,
    result_ref, dy0_ref, dy1_ref, dgate_ref, send_ref, keep_ref, gaing_ref,
    wg, wo, wnat, acc, sems,
):
    step = pl.program_id(0)
    width = wg.shape[2]
    core = acc.shape[1]

    @pl.when(step == 0)
    def _():
        copies = []
        for half, pieces in enumerate(((own0, own1, own2, own3), (oth0, oth1, oth2, oth3))):
            copies += load_rows(pieces, wg.at[half], sems, half * 8, pl.ds(0, width))
            copies += load_rows(pieces, wo.at[half], sems, half * 8 + 4, pl.ds(width, width))
        acc[...] = jnp.zeros(acc.shape, F32)
        keep_ref[...] = jnp.zeros(keep_ref.shape, F32)
        gaing_ref[...] = jnp.zeros(gaing_ref.shape, F32)
        for copy in copies:
            copy.wait()
        for half in range(HALVES):
            wnat[half] = dot(pm_ref[...], wo[half]).astype(BF16)

    normed = normed_ref[...]
    normed_t = normedt_ref[...]
    cot = dot(cot_ref[0], pm_ref[...]).astype(BF16)
    cot_t = dot_nt(pmt_ref[...], cot_ref[0]).astype(BF16)
    y_refs = (y0_ref, y1_ref)
    gates, mixes = [], []
    squares = 0.0
    for half in range(HALVES):
        gate = dot(normed, wg[half])
        mixed = y_refs[half][...] * (gate * sigmoid(gate))
        squares = squares + jnp.sum(mixed * mixed, axis=-1, keepdims=True)
        gates.append(gate)
        mixes.append(mixed)
    rms = lax.rsqrt(squares / (HALVES * width) + EPS)
    total = x_ref[0].astype(F32)
    inner = 0.0
    scaled = []
    for half in range(HALVES):
        gain = gain_ref[half : half + 1, :]
        gated = (mixes[half] * rms * gain).astype(BF16)
        total = total + dot_nt(gated, wnat[half])
        keep_ref[half, :, width:] += dot(cot_t[0:core], gated)
        acc[half, :, width:] += dot(cot_t[core:], gated)
        grad = dot(cot, wo[half])
        gaing_ref[half : half + 1, :] += jnp.sum(grad * mixes[half] * rms, axis=0, keepdims=True)
        grad = grad * gain
        inner = inner + jnp.sum(grad * mixes[half], axis=-1, keepdims=True)
        scaled.append(grad)
    result_ref[0] = total.astype(BF16)
    factor = rms * rms * rms * (inner / (HALVES * width))
    for half, dy_ref in enumerate((dy0_ref, dy1_ref)):
        grad_mixed = rms * scaled[half] - mixes[half] * factor
        gate = gates[half]
        sg = sigmoid(gate)
        dy_ref[...] = (grad_mixed * (gate * sg)).astype(BF16)
        dgate = (grad_mixed * y_refs[half][...] * (sg * (1.0 + gate * (1.0 - sg)))).astype(BF16)
        dgate_ref[half] = dgate
        keep_ref[half, :, 0:width] += dot(normed_t[0:core], dgate)
        acc[half, :, 0:width] += dot(normed_t[core:], dgate)

    @pl.when(step == pl.num_programs(0) - 1)
    def _():
        send_ref[...] = acc[...].astype(BF16)


def backward_kernel(
    first_head, c_ref, vin_ref, dy_ref, state_ref, maps_ref, mapst_ref, cumc_ref, dtc_ref, sgc_ref, cumr_ref,
    taps_ref, skip_ref, rate_ref,
    dvin_ref, dmaps_ref, dstep_ref, tapsg_ref, headg_ref,
    buf, dstate, dgt, uacc, vacc,
):
    step = pl.program_id(0)
    width = buf.shape[1]
    n = dstate.shape[0]
    hb = BLOCK // 2

    @pl.when(step == 0)
    def _():
        buf[pl.ds(BLOCK, 8), :] = jnp.zeros((8, width), F32)
        dstate[...] = jnp.zeros(dstate.shape, F32)
        tapsg_ref[...] = jnp.zeros(tapsg_ref.shape, F32)
        headg_ref[...] = jnp.zeros(headg_ref.shape, F32)

    write = maps_ref[:, 0:n]
    read = maps_ref[:, n : 2 * n]
    read_t = mapst_ref[n : 2 * n, :]
    gt = dot_nt(write, read)
    state = state_ref[0]
    ds = dstate[...]
    ds_b = ds.astype(BF16)
    carried = dot(read, state.astype(BF16))
    wds = dot(write, ds_b)
    cumc = cumc_ref[0]
    dtc = dtc_ref[0]
    ecum = jnp.exp(cumc)
    last = jnp.exp(cumc[BLOCK - 1 : BLOCK, :] - cumc)
    rem = last * dtc
    lane = lax.broadcasted_iota(jnp.int32, (BLOCK, 128), 1)
    lane_low = lane < 64
    sub = lax.broadcasted_iota(jnp.int32, (16, BLOCK), 0)
    tri = lax.broadcasted_iota(jnp.int32, (hb, hb), 1) >= lax.broadcasted_iota(jnp.int32, (hb, hb), 0)
    zeros = jnp.zeros((hb, hb), BF16)
    g00 = gt[0:hb, 0:hb]
    g01 = gt[0:hb, hb:]
    g11 = gt[hb:, hb:]
    dgt[...] = jnp.zeros(dgt.shape, F32)
    to_k = jnp.zeros((BLOCK, 128), F32)
    to_q = jnp.zeros((16, BLOCK), F32)
    for pair in range(width // 128):
        lanes = slice(pair * 128, pair * 128 + 128)
        cp = c_ref[:, lanes]
        v = cp * sigmoid(cp)
        vacc[:, lanes] = v
        dt_s = spread(dtc, first_head // 2 + pair, lane_low)
        vdt = (v * dt_s).astype(BF16)
        dyp = dy_ref[:, lanes]
        us = []
        for j in range(2):
            h = first_head + 2 * pair + j
            ck = jnp.broadcast_to(cumc[:, h : h + 1], (BLOCK, hb))
            cq = cumr_ref[0, h : h + 1, :]
            d00 = jnp.exp(jnp.where(tri, cq[:, 0:hb] - ck[0:hb], NEG))
            d01 = jnp.exp(cq[:, hb:] - ck[0:hb])
            d11 = jnp.exp(jnp.where(tri, cq[:, hb:] - ck[hb:], NEG))
            mine = jnp.where(lane_low if j == 0 else jnp.logical_not(lane_low), dyp, jnp.zeros_like(dyp))
            qt = dot_nt(vdt, mine)
            e00 = d00 * qt[0:hb, 0:hb]
            e01 = d01 * qt[0:hb, hb:]
            e11 = d11 * qt[hb:, hb:]
            dgt[0:hb, 0:hb] += e00
            dgt[0:hb, hb:] += e01
            dgt[hb:, hb:] += e11
            a = jnp.concatenate(
                [
                    jnp.concatenate([(g00 * d00).astype(BF16), (g01 * d01).astype(BF16)], axis=1),
                    jnp.concatenate([zeros, (g11 * d11).astype(BF16)], axis=1),
                ],
                axis=0,
            )
            z = jnp.concatenate(
                [
                    jnp.concatenate([(g00 * e00).astype(BF16), (g01 * e01).astype(BF16)], axis=1),
                    jnp.concatenate([zeros, (g11 * e11).astype(BF16)], axis=1),
                ],
                axis=0,
            )
            us.append(dot(a, dyp))
            to_k = to_k + dot(z, jnp.where(lane == h, 1.0, 0.0).astype(BF16))
            to_q = to_q + dot(jnp.where(sub == h, 1.0, 0.0).astype(BF16), z)
        uacc[:, lanes] = jnp.where(lane_low, us[0], us[1])
        ec = spread(ecum, first_head // 2 + pair, lane_low)
        rem_s = spread(rem, first_head // 2 + pair, lane_low)
        dye = (dyp.astype(F32) * ec).astype(BF16)
        u = uacc[:, lanes]
        dv = dt_s * u + skip_ref[:, lanes] * dyp.astype(F32) + rem_s * wds[:, lanes]
        sg = sigmoid(cp)
        buf[0:BLOCK, lanes] = dv * (sg * (1.0 + cp * (1.0 - sg)))
        dstate[:, lanes] = ds[:, lanes] * ec[BLOCK - 1 : BLOCK, :] + dot(read_t, dye)
        vrem = (v * rem_s).astype(BF16)
        dmw = dot_nt(vrem, ds_b[:, lanes])
        dmr = dot_nt(dye, state[:, lanes].astype(BF16))
        if pair == 0:
            dmaps_w, dmaps_r = dmw, dmr
        else:
            dmaps_w, dmaps_r = dmaps_w + dmw, dmaps_r + dmr
    dg_b = dgt[...].astype(BF16)
    dmaps_ref[:, 0:n] = dmaps_w + dot(dg_b, read)
    dmaps_ref[:, n : 2 * n] = dmaps_r + dot_tn(dg_b, write)

    row = lax.broadcasted_iota(jnp.int32, (width, 128), 0)
    col = lax.broadcasted_iota(jnp.int32, (width, 128), 1)
    pick = jnp.where(row // 64 + first_head == col, 1.0, 0.0).astype(BF16)

    def per_head(values):
        high = values.astype(BF16)
        low = (values - high.astype(F32)).astype(BF16)
        return dot(high, pick) + dot(low, pick)

    v = vacc[...]
    dy = dy_ref[...].astype(F32)
    v_u = per_head(v * uacc[...])
    v_wds = per_head(v * wds)
    dy_c = per_head(dy * carried)
    skip_sum = jnp.sum(dy * v, axis=0, keepdims=True)
    ss = per_head(jnp.broadcast_to(jnp.sum(ds * state, axis=0, keepdims=True), (8, width)))
    sent = rem * v_wds
    d_last = ecum[BLOCK - 1 : BLOCK, :] * ss[0:1, :] + jnp.sum(sent, axis=0, keepdims=True)
    dcum = jnp.concatenate([to_q, jnp.zeros((112, BLOCK), F32)], axis=0).T - to_k + ecum * dy_c - sent
    token = lax.broadcasted_iota(jnp.int32, (BLOCK, 128), 0)
    dcum = dcum + jnp.where(token == BLOCK - 1, d_last, 0.0)
    row = lax.broadcasted_iota(jnp.int32, (BLOCK, BLOCK), 0)
    col = lax.broadcasted_iota(jnp.int32, (BLOCK, BLOCK), 1)
    upper = jnp.where(row <= col, 1.0, 0.0).astype(BF16)
    dlog = dot_exact(upper, dcum)
    rate = rate_ref[0]
    ddt = v_u + last * v_wds + dlog * rate
    mine = jnp.logical_and(lane >= first_head, lane < first_head + width // 64)
    draw = jnp.where(mine, ddt * sgc_ref[0], 0.0)
    dstep_ref[...] = draw.astype(BF16)
    headg_ref[0:1, :] += jnp.sum(draw, axis=0, keepdims=True)
    headg_ref[1:2, :] += jnp.sum(dlog * dtc, axis=0, keepdims=True) * rate
    headg_ref[2:3, :] += per_head(jnp.broadcast_to(skip_sum, (8, width)))[0:1, :]

    vin = vin_ref[...].astype(F32)
    total = jnp.zeros((BLOCK, width), F32)
    for j in range(4):
        shifted = buf[pl.ds(3 - j, BLOCK), :]
        total = total + taps_ref[j : j + 1, :] * shifted
        tapsg_ref[j : j + 1, :] += jnp.sum(shifted * vin, axis=0, keepdims=True)
    tapsg_ref[4:5, :] += jnp.sum(buf[0:BLOCK, :], axis=0, keepdims=True)
    dvin_ref[...] = total.astype(BF16)
    buf[pl.ds(BLOCK, 8), :] = buf[pl.ds(0, 8), :]


def state_kernel(*refs):
    dmaps_refs = refs[:-6]
    statein_ref, statec_ref, taps_ref, dstate_ref, tapsg_ref, buf = refs[-6:]
    length, width = statein_ref.shape
    c = statec_ref[...]
    sg = sigmoid(c)
    dmaps = dmaps_refs[0][...]
    for ref in dmaps_refs[1:]:
        dmaps = dmaps + ref[...]
    dc = dmaps * (sg * (1.0 + c * (1.0 - sg)))
    buf[0:length, :] = dc
    buf[pl.ds(length, 8), :] = jnp.zeros((8, width), F32)
    state_in = statein_ref[...]
    total = jnp.zeros((length, width), F32)
    tapsg_ref[...] = jnp.zeros(tapsg_ref.shape, F32)
    for j in range(4):
        shifted = buf[pl.ds(3 - j, length), :]
        total = total + taps_ref[j : j + 1, :] * shifted
        tapsg_ref[j : j + 1, :] = jnp.sum(shifted * state_in, axis=0, keepdims=True)
    tapsg_ref[4:5, :] = jnp.sum(dc, axis=0, keepdims=True)
    dstate_ref[...] = total.astype(BF16)


def partial_kernel(*refs):
    normedt_ref = refs[0]
    keep_ref, send_ref = refs[-2:]
    core = keep_ref.shape[0]
    col = 0
    for group in refs[1:-2]:
        cols = group.shape[-1]
        value = group[...]
        both = dot(normedt_ref[...], value)
        keep_ref[:, col : col + cols] = both[0:core]
        send_ref[:, col : col + cols] = both[core:].astype(BF16)
        col += cols


def input_kernel(*refs):
    x_ref, cot_ref, gain_ref, pm_ref, dgate_ref, dstate_ref = refs[:6]
    dvin_refs = refs[6 : 6 + HALVES * SEGMENTS]
    dstep_refs = refs[6 + HALVES * SEGMENTS : 6 + HALVES * (SEGMENTS + 1)]
    pieces = refs[6 + HALVES * (SEGMENTS + 1) : 6 + HALVES * (SEGMENTS + 1) + 24]
    grad_ref, gaing_ref, wg, wv, wown, woth, sems = refs[-7:]
    step = pl.program_id(0)
    width = wg.shape[2]
    n2 = dstate_ref.shape[1]

    @pl.when(step == 0)
    def _():
        copies = []
        for half in range(HALVES):
            copies += load_rows(pieces[half * 4 : half * 4 + 4], wg.at[half], sems, half * 4, pl.ds(0, width))
            copies += load_rows(pieces[8 + half * 4 : 12 + half * 4], wv.at[half], sems, 8 + half * 4)
        copies += load_rows(pieces[16:20], wown, sems, 16)
        copies += load_rows(pieces[20:24], woth, sems, 20)
        gaing_ref[...] = jnp.zeros(gaing_ref.shape, F32)
        for copy in copies:
            copy.wait()

    own_step, other_step = (ref[...] for ref in dstep_refs)
    total = dot_nt(dstate_ref[...], wown[:, 0:n2]) + dot_nt(own_step, wown[:, n2:]) + dot_nt(other_step, woth[...])
    for half in range(HALVES):
        total = total + dot_nt(dgate_ref[half], wg[half])
        for segment in range(SEGMENTS):
            dvin = dvin_refs[half * SEGMENTS + segment][...]
            cols = dvin.shape[1]
            total = total + dot_nt(dvin, wv[half, :, segment * cols : segment * cols + cols])
    high, mid, low = split3(total)
    total = dot_nt(high, pm_ref[...]) + dot_nt(mid, pm_ref[...]) + dot_nt(low, pm_ref[...])
    x = x_ref[0].astype(F32)
    inv = lax.rsqrt(jnp.mean(x * x, axis=-1, keepdims=True) + EPS)
    gaing_ref[0:1, :] += jnp.sum(total * x * inv, axis=0, keepdims=True)
    scaled = total * gain_ref[...]
    inner = jnp.mean(scaled * x, axis=-1, keepdims=True)
    grad_ref[0] = cot_ref[0].astype(F32) + inv * scaled - x * (inv * inv * inv * inner)


def call(body, grid, in_specs, out_specs, out_shape, scratch=(), flops=0):
    return pl.pallas_call(
        body,
        grid=grid,
        in_specs=in_specs,
        out_specs=out_specs,
        out_shape=out_shape,
        scratch_shapes=list(scratch),
        compiler_params=pltpu.CompilerParams(
            vmem_limit_bytes=VMEM_BYTES, dimension_semantics=("arbitrary",) * len(grid)
        ),
        cost_estimate=pl.CostEstimate(flops=flops, bytes_accessed=10_000_000, transcendentals=0),
    )


def shape(dims, dtype=F32):
    return jax.ShapeDtypeStruct(dims, dtype)


def fixed(dims, *index):
    return pl.BlockSpec(dims, lambda *_: index)


ANYWHERE = pl.BlockSpec(memory_space=pl.ANY)
AXES = ("dp", "tensor")
TENSOR, CORE, CHIP = 1, 2, 4
FAR = 3


def swap(v, mask):
    count = lax.axis_size("dp") * lax.axis_size("tensor")
    return lax.ppermute(v, AXES, [(i, i ^ mask) for i in range(count)])


def far_masks():
    count = lax.axis_size("dp") * lax.axis_size("tensor")
    return [m << FAR for m in range(1, count >> FAR)]


def near_rows(pack):
    return jnp.concatenate([pack] + [swap(pack, m) for m in far_masks()], axis=0)


def scatter_far(v, rows):
    masks = far_masks()
    got = [swap(v[(i + 1) * rows : (i + 2) * rows].astype(BF16), m) for i, m in enumerate(masks)]
    total = v[0:rows]
    for part in got:
        total = total + part.astype(F32)
    return total


def local(
    inputs,
    prenorm,
    gate_weight,
    value_weight,
    state_weight,
    step_weight,
    value_conv,
    value_shift,
    state_conv,
    state_shift,
    step_shift,
    decay_log,
    skip_scale,
    gated_gain,
    output_matrix,
    cotangent,
):
    length, width = inputs.shape[1:]
    rows, w = gate_weight.shape
    heads = step_weight.shape[1]
    n = state_weight.shape[1] // 2
    n2 = 2 * n
    blocks = length // BLOCK
    head_width = w // heads
    quarter = width // 4

    def lanes_of(v):
        return jnp.pad(v, ((0, 0), (0, PAD - v.shape[1])))

    spot = jnp.arange(width)
    owner = lax.axis_index("dp") ^ (
        spot // (2 * quarter) + 2 * (spot // quarter % 2) + 4 * (spot % quarter // rows)
    )
    natural = owner * rows + spot % rows
    pm = (spot[:, None] == natural[None, :]).astype(BF16)
    pmt = (natural[:, None] == spot[None, :]).astype(BF16)

    def gather_own(pack):
        near = near_rows(pack)
        chip = swap(near, CHIP)
        return [near, chip, swap(near, CORE), swap(chip, CORE)]

    def gather_other(near, chip):
        near, chip = swap(near, TENSOR), swap(chip, TENSOR)
        return [near, chip, swap(near, CORE), swap(chip, CORE)]

    small = jnp.concatenate(
        [
            value_conv.reshape(-1), value_shift, jnp.repeat(skip_scale, head_width), gated_gain,
            lanes_of(step_shift[None]).reshape(-1), lanes_of(-jnp.exp(decay_log)[None]).reshape(-1),
        ]
    )
    small = jnp.stack([small, swap(small, TENSOR)])
    value_taps = small[:, : 4 * w].reshape(HALVES, 4, w)
    value_bias = small[:, None, 4 * w : 5 * w]
    skip = small[:, None, 5 * w : 6 * w]
    gain = small[:, 6 * w : 7 * w]
    step_bias = small[:, 7 * w : 7 * w + PAD]
    rate = small[:, 7 * w + PAD :]

    step_pack = lanes_of(step_weight)
    state_own = gather_own(jnp.concatenate([state_weight, step_pack], axis=1))
    step_other = gather_other(state_own[0][:, n2:], state_own[1][:, n2:])
    value_own = gather_own(value_weight)
    value_other = gather_other(*value_own[:2])
    gate_own = gather_own(jnp.concatenate([gate_weight, output_matrix.T], axis=1))
    gate_other = gather_other(*gate_own[:2])

    row_block = lambda dims: pl.BlockSpec(dims, lambda b: (b, 0))
    col_block = lambda dims: pl.BlockSpec(dims, lambda b: (0, b))
    tokens = pl.BlockSpec((1, BLOCK, width), lambda b: (0, b, 0))
    halves = lambda last: pl.BlockSpec((HALVES, BLOCK, last), lambda b: (0, b, 0))
    square = fixed((width, width), 0, 0)
    sems = lambda count: pltpu.SemaphoreType.DMA((count,))

    normed, normed_t, state_in, state_c, maps, maps_t, cumc, dtc, sgc, cumr = call(
        maps_kernel,
        (blocks,),
        [tokens, fixed((1, width), 0, 0), square, square] + [ANYWHERE] * 8
        + [fixed((4, n2), 0, 0), fixed((1, n2), 0, 0), fixed((HALVES, PAD), 0, 0), fixed((HALVES, PAD), 0, 0)],
        [row_block((BLOCK, width)), col_block((width, BLOCK)), row_block((BLOCK, n2)), row_block((BLOCK, n2)),
         row_block((BLOCK, n2)), col_block((n2, BLOCK)), halves(PAD), halves(PAD), halves(PAD),
         pl.BlockSpec((HALVES, 16, BLOCK), lambda b: (0, 0, b))],
        [shape((length, width), BF16), shape((width, length), BF16), shape((length, n2)), shape((length, n2)),
         shape((length, n2), BF16), shape((n2, length), BF16), shape((HALVES, length, PAD)),
         shape((HALVES, length, PAD)), shape((HALVES, length, PAD)), shape((HALVES, 16, length))],
        [pltpu.VMEM((BLOCK + 8, n2), F32), pltpu.VMEM((width, n2 + PAD), BF16), pltpu.VMEM((width, PAD), BF16), sems(8)],
        flops=8_000_000_000,
    )(inputs, prenorm[None], pm, pmt, *state_own, *step_other, state_conv, state_shift[None], step_bias, rate)

    value_ins, value_cs, ys, states = [], [], [], []
    for half, pieces in enumerate((value_own, value_other)):
        per_half = lambda dims, half=half: pl.BlockSpec(dims, lambda b: (half, b, 0))
        value_in, value_c, y, state = call(
            forward_kernel,
            (blocks,),
            [row_block((BLOCK, width))] + [ANYWHERE] * 4
            + [fixed((4, w), 0, 0), fixed((1, w), 0, 0), fixed((1, w), 0, 0), row_block((BLOCK, n2)),
               col_block((n2, BLOCK)), per_half((1, BLOCK, PAD)), per_half((1, BLOCK, PAD)),
               pl.BlockSpec((1, 16, BLOCK), lambda b, half=half: (half, 0, b))],
            [row_block((BLOCK, w)), row_block((BLOCK, w)), row_block((BLOCK, w)),
             pl.BlockSpec((1, n, w), lambda b: (b, 0, 0))],
            [shape((length, w), BF16), shape((length, w)), shape((length, w)), shape((blocks, n, w))],
            [pltpu.VMEM((BLOCK + 8, w), F32), pltpu.VMEM((n, w), F32), pltpu.VMEM((width, w), BF16), sems(4)],
            flops=12_000_000_000,
        )(normed, *pieces, value_taps[half], value_bias[half], skip[half], maps, maps_t, cumc, dtc, cumr)
        value_ins.append(value_in)
        value_cs.append(value_c)
        ys.append(y)
        states.append(state)

    both_w = (HALVES, width, w)
    half_rows = (HALVES, width // 2, 2 * w)
    result, dy0, dy1, dgate, early_send, early_keep, gain_partial = call(
        gated_kernel,
        (blocks,),
        [tokens, tokens, row_block((BLOCK, width)), col_block((width, BLOCK)), row_block((BLOCK, w)),
         row_block((BLOCK, w)), fixed((HALVES, w), 0, 0), square, square] + [ANYWHERE] * 8,
        [tokens, row_block((BLOCK, w)), row_block((BLOCK, w)), halves(w), fixed(half_rows, 0, 0, 0),
         fixed(half_rows, 0, 0, 0), fixed((HALVES, w), 0, 0)],
        [shape(inputs.shape, BF16), shape((length, w), BF16), shape((length, w), BF16),
         shape((HALVES, length, w), BF16), shape(half_rows, BF16), shape(half_rows), shape((HALVES, w))],
        [pltpu.VMEM(both_w, BF16), pltpu.VMEM(both_w, BF16), pltpu.VMEM(both_w, BF16), pltpu.VMEM(half_rows, F32),
         sems(16)],
        flops=25_000_000_000,
    )(inputs, cotangent, normed, normed_t, *ys, gain, pm, pmt, *gate_own, *gate_other)

    dys = (dy0, dy1)
    seg_w = w // SEGMENTS
    seg_heads = heads // SEGMENTS

    def backward(half, segment):
        back = lambda dims, col=0: pl.BlockSpec(dims, lambda b: (blocks - 1 - b, col))
        per_half = pl.BlockSpec((1, BLOCK, PAD), lambda b: (half, blocks - 1 - b, 0))
        return call(
            functools.partial(backward_kernel, segment * seg_heads),
            (blocks,),
            [back((BLOCK, seg_w), segment)] * 3
            + [pl.BlockSpec((1, n, seg_w), lambda b: (blocks - 1 - b, 0, segment)), back((BLOCK, n2)),
               pl.BlockSpec((n2, BLOCK), lambda b: (0, blocks - 1 - b)), per_half, per_half, per_half,
               pl.BlockSpec((1, 16, BLOCK), lambda b: (half, 0, blocks - 1 - b)), fixed((4, seg_w), 0, segment),
               fixed((1, seg_w), 0, segment), fixed((1, PAD), 0, 0)],
            [back((BLOCK, seg_w)), back((BLOCK, n2)), back((BLOCK, PAD)), fixed((8, seg_w), 0, 0), fixed((8, PAD), 0, 0)],
            [shape((length, seg_w), BF16), shape((length, n2)), shape((length, PAD), BF16), shape((8, seg_w)),
             shape((8, PAD))],
            [pltpu.VMEM((BLOCK + 8, seg_w), F32), pltpu.VMEM((n, seg_w), F32), pltpu.VMEM((BLOCK, BLOCK), F32),
             pltpu.VMEM((BLOCK, seg_w), F32), pltpu.VMEM((BLOCK, seg_w), F32)],
            flops=12_000_000_000,
        )(value_cs[half], value_ins[half], dys[half], states[half], maps, maps_t, cumc, dtc, sgc, cumr,
          value_taps[half], skip[half], rate[half : half + 1])

    def partial(groups):
        cols = sum(group.shape[1] for group in groups)
        full = lambda dims: fixed(dims, 0, 0)
        return call(
            partial_kernel,
            (1,),
            [full((width, length))] + [full(group.shape) for group in groups],
            [full((width // 2, cols)), full((width // 2, cols))],
            [shape((width // 2, cols)), shape((width // 2, cols), BF16)],
            flops=2 * length * width * cols,
        )(normed_t, *groups)

    early = early_keep + swap(early_send, CORE).astype(F32)
    other = [backward(1, segment) for segment in range(SEGMENTS)]
    early = early[0] + swap(early[1].astype(BF16), TENSOR).astype(F32)
    dstep_other = sum((part[2] for part in other[1:]), other[0][2])
    keep, send = partial([part[0] for part in other] + [dstep_other])
    other_sum = keep + swap(send, CORE).astype(F32)
    own = [backward(0, segment) for segment in range(SEGMENTS)]
    early = early[:quarter] + swap(early[quarter:].astype(BF16), CHIP).astype(F32)
    other_got = swap(other_sum.astype(BF16), TENSOR)
    dstep_own = sum((part[2] for part in own[1:]), own[0][2])
    keep, send = partial([part[0] for part in own] + [dstep_own])
    late = keep + swap(send, CORE).astype(F32) + other_got.astype(F32)
    late = late[:quarter] + swap(late[quarter:].astype(BF16), CHIP).astype(F32)
    early = scatter_far(early, rows)
    late = scatter_far(late, rows)

    segs = own + other
    dstate, state_taps = call(
        state_kernel,
        (1,),
        [fixed((length, n2), 0, 0)] * (len(segs) + 2) + [fixed((4, n2), 0, 0)],
        [fixed((length, n2), 0, 0), fixed((8, n2), 0, 0)],
        [shape((length, n2), BF16), shape((8, n2))],
        [pltpu.VMEM((length + 8, n2), F32)],
        flops=1_000_000_000,
    )(*[part[1] for part in segs], state_in, state_c, state_conv)
    keep, send = partial([dstate])
    state = keep + swap(send, CORE).astype(F32)
    near, chip = state[:quarter], state[quarter:].astype(BF16)
    state = (
        near + swap(near.astype(BF16), TENSOR).astype(F32) + swap(chip, CHIP).astype(F32)
        + swap(chip, CHIP | TENSOR).astype(F32)
    )
    state = scatter_far(state, rows)

    input_grad, prenorm_partial = call(
        input_kernel,
        (blocks,),
        [tokens, tokens, fixed((1, width), 0, 0), square, halves(w), row_block((BLOCK, n2))]
        + [row_block((BLOCK, seg_w))] * len(segs) + [row_block((BLOCK, PAD))] * HALVES + [ANYWHERE] * 24,
        [tokens, fixed((8, width), 0, 0)],
        [shape(inputs.shape), shape((8, width))],
        [pltpu.VMEM(both_w, BF16), pltpu.VMEM(both_w, BF16), pltpu.VMEM((width, n2 + PAD), BF16),
         pltpu.VMEM((width, PAD), BF16), sems(24)],
        flops=12_000_000_000,
    )(inputs, cotangent, prenorm[None], pm, dgate, dstate, *[part[0] for part in segs], dstep_own, dstep_other,
      *gate_own, *gate_other, *value_own, *value_other, *state_own, *step_other)

    def smalls_of(parts, half):
        taps = jnp.concatenate([part[3][:5] for part in parts], axis=1).reshape(-1)
        head = sum((part[4][:3] for part in parts[1:]), parts[0][4][:3]).reshape(-1)
        return jnp.concatenate([taps, head, gain_partial[half]])

    mine, theirs = smalls_of(own, 0), smalls_of(other, 1)
    shared = jnp.concatenate([state_taps[:5].reshape(-1), prenorm_partial[0]])
    count = mine.shape[0]
    sums = jnp.concatenate([mine, shared, theirs])
    sums = sums + swap(sums, CORE)
    sums = sums[: count + shared.shape[0]] + swap(
        jnp.concatenate([sums[count + shared.shape[0] :], sums[count : count + shared.shape[0]]]), TENSOR
    )
    bit = CHIP
    while bit < lax.axis_size("dp") * lax.axis_size("tensor"):
        sums = sums + swap(sums, bit)
        bit *= 2
    taps = sums[: 5 * w].reshape(5, w)
    head = sums[5 * w : 5 * w + 3 * PAD].reshape(3, PAD)
    state_taps = sums[count : count + 5 * n2].reshape(5, n2)
    return (
        result,
        input_grad,
        sums[count + 5 * n2 :],
        early[:, :w],
        late[:, :w],
        state,
        late[:, w : w + heads],
        taps[0:4],
        taps[4],
        state_taps[0:4],
        state_taps[4],
        head[0, :heads],
        head[1, :heads],
        head[2, :heads],
        sums[5 * w + 3 * PAD : count],
        early[:, w:].T,
    )


def solution(mesh):
    in_specs = (
        P(("dp", "tensor"), None, None),
        P(),
        P("dp", "tensor"),
        P("dp", "tensor"),
        P("dp", None),
        P("dp", "tensor"),
        P(None, "tensor"),
        P("tensor"),
        P(),
        P(),
        P("tensor"),
        P("tensor"),
        P("tensor"),
        P("tensor"),
        P("tensor", "dp"),
        P(("dp", "tensor"), None, None),
    )
    out_specs = (
        P(("dp", "tensor"), None, None),
        P(("dp", "tensor"), None, None),
        P(),
        P("dp", "tensor"),
        P("dp", "tensor"),
        P("dp", None),
        P("dp", "tensor"),
        P(None, "tensor"),
        P("tensor"),
        P(),
        P(),
        P("tensor"),
        P("tensor"),
        P("tensor"),
        P("tensor"),
        P("tensor", "dp"),
    )
    return jax.shard_map(local, mesh=mesh, in_specs=in_specs, out_specs=out_specs, check_vma=False)
```

```python
import functools

import jax
import jax.numpy as jnp
from jax import lax
from jax.experimental import pallas as pl
from jax.experimental.pallas import tpu as pltpu
from jax.sharding import PartitionSpec as P

BLOCK = 256
HALVES = 2
PAD = 128
SEGMENTS = 2
EPS = 1e-05
NEG = -1e30
F32 = jnp.float32
BF16 = jnp.bfloat16
MIB = 1024 * 1024


def dot(a, b):
    return jnp.dot(a, b, preferred_element_type=F32)


def dot_nt(a, b):
    return lax.dot_general(a, b, (((1,), (1,)), ((), ())), preferred_element_type=F32)


def dot_tn(a, b):
    return lax.dot_general(a, b, (((0,), (0,)), ((), ())), preferred_element_type=F32)


def split3(v):
    high = v.astype(BF16)
    rest = v - high.astype(F32)
    mid = rest.astype(BF16)
    low = (rest - mid.astype(F32)).astype(BF16)
    return high, mid, low


def dot_twice(mask, v):
    high = v.astype(BF16)
    return dot(mask, high) + dot(mask, (v - high.astype(F32)).astype(BF16))


def dot_exact(mask, v):
    high, mid, low = split3(v)
    return dot(mask, high) + dot(mask, mid) + dot(mask, low)


def sigmoid(v):
    return 0.5 * jnp.tanh(0.5 * v) + 0.5


def spread(cols, pair, lane_low):
    rows = cols.shape[0]
    left = jnp.broadcast_to(cols[:, 2 * pair : 2 * pair + 1], (rows, 128))
    right = jnp.broadcast_to(cols[:, 2 * pair + 1 : 2 * pair + 2], (rows, 128))
    return jnp.where(lane_low, left, right)


def conv_taps(buf, taps_ref, shift, first, rows):
    total = shift + taps_ref[0:1, :] * buf[pl.ds(first, rows), :]
    for j in range(1, 4):
        total = total + taps_ref[j : j + 1, :] * buf[pl.ds(first + j, rows), :]
    return total


def pack_kernel(
    taps_ref, shift_ref, skip_ref, gain_ref, bias_ref, decay_ref, prenorm_ref, sshift_ref,
    gate_ref, value_ref, stept_ref, outt_ref,
    small_ref, shared_ref, vpack_ref, gpack_ref,
):
    rows, width = gate_ref.shape
    heads = stept_ref.shape[0]
    n2 = sshift_ref.shape[0]
    gpack_ref[:, 0:width] = gate_ref[...]
    gpack_ref[:, width:] = outt_ref[...]
    vpack_ref[:, 0:width] = value_ref[...]
    vpack_ref[:, width:] = jnp.zeros((rows, PAD), BF16)
    vpack_ref[:, width : width + heads] = stept_ref[...].astype(F32).T.astype(BF16)
    small_ref[...] = jnp.zeros(small_ref.shape, F32)
    shared_ref[...] = jnp.zeros(shared_ref.shape, F32)
    small_ref[0:4, :] = taps_ref[...]
    small_ref[4, :] = shift_ref[...]
    head = lax.broadcasted_iota(jnp.int32, (1, width), 1) // (width // heads)
    skip_row = skip_ref[...].reshape(1, heads)
    skip = jnp.zeros((1, width), F32)
    for h in range(heads):
        skip = jnp.where(head == h, skip_row[:, h : h + 1], skip)
    small_ref[5:6, :] = skip
    small_ref[6, :] = gain_ref[...]
    small_ref[7:8, 0:heads] = bias_ref[...].reshape(1, heads)
    small_ref[7:8, PAD : PAD + heads] = -jnp.exp(decay_ref[...].reshape(1, heads))
    shared_ref[0, :] = prenorm_ref[...]
    shared_ref[1:2, 0:n2] = sshift_ref[...].reshape(1, n2)


def load_rows(pieces, target, sems, first=0, lanes=None):
    copies = []
    for i, piece in enumerate(pieces):
        rows = piece.shape[0]
        source = piece if lanes is None else piece.at[:, lanes]
        copies.append(pltpu.make_async_copy(source, target.at[pl.ds(i * rows, rows), :], sems.at[first + i]))
    for copy in copies:
        copy.start()
    return copies


def load_halves(pieces, target, sems, first, lanes):
    near0, x0, y0, yx0, near1, x1, y1, yx1 = pieces
    copies = load_rows((near0, x0, near1, x1), target.at[0], sems, first, lanes)
    return copies + load_rows((y0, yx0, y1, yx1), target.at[1], sems, first + 4, lanes)


def weighted_tiles(grad, weight):
    product = grad * weight.astype(F32)
    return sum((product[:, col : col + 128] for col in range(128, product.shape[1], 128)), product[:, 0:128])


def along_lanes(tiles):
    ones = jnp.ones((8, tiles.shape[1]), BF16)
    high = tiles.astype(BF16)
    return dot_nt(ones, high) + dot_nt(ones, (tiles - high.astype(F32)).astype(BF16))


def maps_kernel(
    x_ref, pm_ref, pmt_ref, piece0, piece1, piece2, piece3, taps_ref, shared_ref,
    normed_ref, normedt_ref, statein_ref, statec_ref, maps_ref, mapst_ref,
    buf, ws, sems,
):
    step = pl.program_id(0)
    n2 = buf.shape[1]

    @pl.when(step == 0)
    def _():
        lanes = pl.ds(piece0.shape[1] - n2, n2)
        copies = load_rows((piece0, piece1, piece2, piece3), ws, sems, 0, lanes)
        buf[pl.ds(0, 8), :] = jnp.zeros((8, n2), F32)
        for copy in copies:
            copy.wait()

    x = x_ref[0].astype(F32)
    inv = lax.rsqrt(jnp.mean(x * x, axis=-1, keepdims=True) + EPS)
    normed = (x * inv * shared_ref[0:1, :]).astype(BF16)
    normedt_ref[...] = dot_nt(pmt_ref[...], normed).astype(BF16)
    normed = dot(normed, pm_ref[...]).astype(BF16)
    normed_ref[...] = normed
    state_in = dot(normed, ws[...])
    statein_ref[...] = state_in
    buf[pl.ds(8, BLOCK), :] = state_in
    c = conv_taps(buf, taps_ref, shared_ref[1:2, 0:n2], 5, BLOCK)
    buf[pl.ds(0, 8), :] = buf[pl.ds(BLOCK, 8), :]
    statec_ref[...] = c
    maps = c * sigmoid(c)
    maps_ref[...] = maps.astype(BF16)
    mapst_ref[...] = maps.T.astype(BF16)


def forward_kernel(*refs):
    pieces = refs[:-14]
    normed_ref, small_ref, maps_ref, mapst_ref = refs[-14:-10]
    vin_ref, c_ref, y_ref, state_ref, steps_ref, cumr_ref, buf, state, wv, sems = refs[-10:]
    step = pl.program_id(0)
    width = buf.shape[1]
    n = state.shape[0]

    @pl.when(step == 0)
    def _():
        copies = load_rows(pieces, wv, sems, 0, pl.ds(0, width + PAD))
        buf[pl.ds(0, 8), :] = jnp.zeros((8, width), F32)
        state[...] = jnp.zeros(state.shape, F32)
        for copy in copies:
            copy.wait()

    raw = dot(normed_ref[...], wv[:, width:]) + small_ref[7:8, 0:PAD]
    soft = jnp.exp(-jnp.abs(raw))
    dtc = jnp.maximum(raw, 0.0) + jnp.log1p(soft)
    slope = jnp.where(raw >= 0, 1.0, soft) / (1.0 + soft)
    row = lax.broadcasted_iota(jnp.int32, (BLOCK, BLOCK), 0)
    col = lax.broadcasted_iota(jnp.int32, (BLOCK, BLOCK), 1)
    lower = jnp.where(row >= col, 1.0, 0.0).astype(BF16)
    cumc = dot_exact(lower, dtc * small_ref[7:8, PAD : 2 * PAD])
    lane = lax.broadcasted_iota(jnp.int32, (BLOCK, PAD), 1)
    steps_ref[...] = jnp.where(
        lane < 32, cumc, jnp.where(lane < 64, pltpu.roll(dtc, 32, 1), pltpu.roll(slope, 64, 1))
    )
    cumr = cumc.T[0:16, :]
    cumr_ref[...] = cumr
    value_in = dot(normed_ref[...], wv[:, 0:width])
    vin_ref[...] = value_in.astype(BF16)
    buf[pl.ds(8, BLOCK), :] = value_in
    c = conv_taps(buf, small_ref, small_ref[4:5, :], 5, BLOCK)
    buf[pl.ds(0, 8), :] = buf[pl.ds(BLOCK, 8), :]
    c_ref[...] = c.astype(BF16)
    state_ref[0] = state[...]
    write = maps_ref[:, 0:n]
    read = maps_ref[:, n : 2 * n]
    write_t = mapst_ref[0:n, :]
    grams = dot_nt(read, write)
    carried = dot(read, state[...].astype(BF16))
    ecum = jnp.exp(cumc)
    rem = jnp.exp(cumc[BLOCK - 1 : BLOCK, :] - cumc) * dtc
    lane_low = lax.broadcasted_iota(jnp.int32, (BLOCK, 128), 1) < 64
    hb = BLOCK // 2
    tri = lax.broadcasted_iota(jnp.int32, (hb, hb), 0) >= lax.broadcasted_iota(jnp.int32, (hb, hb), 1)
    zeros = jnp.zeros((hb, hb), BF16)
    g00 = grams[0:hb, 0:hb]
    g10 = grams[hb:, 0:hb]
    g11 = grams[hb:, hb:]
    for pair in range(width // 128):
        lanes = slice(pair * 128, pair * 128 + 128)
        cp = c[:, lanes]
        v = cp * sigmoid(cp)
        vdt = (v * spread(dtc, pair, lane_low)).astype(BF16)
        outs = []
        for j in range(2):
            h = 2 * pair + j
            cq = jnp.broadcast_to(cumc[:, h : h + 1], (BLOCK, hb))
            ck = cumr[h : h + 1, :]
            d00 = jnp.exp(jnp.where(tri, cq[0:hb] - ck[:, 0:hb], NEG))
            d10 = jnp.exp(cq[hb:] - ck[:, 0:hb])
            d11 = jnp.exp(jnp.where(tri, cq[hb:] - ck[:, hb:], NEG))
            top = jnp.concatenate([(g00 * d00).astype(BF16), zeros], axis=1)
            bot = jnp.concatenate([(g10 * d10).astype(BF16), (g11 * d11).astype(BF16)], axis=1)
            outs.append(dot(jnp.concatenate([top, bot], axis=0), vdt))
        ec = spread(ecum, pair, lane_low)
        y = jnp.where(lane_low, outs[0], outs[1]) + ec * carried[:, lanes] + small_ref[5:6, lanes] * v
        y_ref[:, lanes] = y.astype(BF16)
        vrem = (v * spread(rem, pair, lane_low)).astype(BF16)
        state[:, lanes] = state[:, lanes] * ec[BLOCK - 1 : BLOCK, :] + dot(write_t, vrem)


def gated_kernel(
    x_ref, cot_ref, normed_ref, normedt_ref, y0_ref, y1_ref, small0_ref, small1_ref, pm_ref, pmt_ref,
    near0, x0, y0, yx0, near1, x1, y1, yx1,
    result_ref, dy0_ref, dy1_ref, dgate_ref, send_ref, keep_ref, gaing_ref, pre_ref,
    wg, wo, wnat, acc, sems,
):
    step = pl.program_id(0)
    width = wg.shape[2]
    core = acc.shape[1]

    @pl.when(step == 0)
    def _():
        copies = []
        pieces = (near0, x0, y0, yx0, near1, x1, y1, yx1)
        copies += load_halves(pieces, wg, sems, 0, pl.ds(0, width)) + load_halves(pieces, wo, sems, 8, pl.ds(width, width))
        acc[...] = jnp.zeros(acc.shape, F32)
        keep_ref[...] = jnp.zeros(keep_ref.shape, F32)
        gaing_ref[...] = jnp.zeros(gaing_ref.shape, F32)
        for copy in copies:
            copy.wait()
        for half in range(HALVES):
            wnat[half] = dot_tn(wo[half], pmt_ref[...]).astype(BF16)

    normed = normed_ref[...]
    normed_t = normedt_ref[...]
    cot = dot(cot_ref[0], pm_ref[...]).astype(BF16)
    cot_t = dot_nt(pmt_ref[...], cot_ref[0]).astype(BF16)
    y_refs = (y0_ref, y1_ref)
    small_refs = (small0_ref, small1_ref)
    gates, mixes = [], []
    squares = 0.0
    for half in range(HALVES):
        gate = dot(normed, wg[half])
        mixed = y_refs[half][...].astype(F32) * (gate * sigmoid(gate))
        squares = squares + jnp.sum(mixed * mixed, axis=-1, keepdims=True)
        gates.append(gate)
        mixes.append(mixed)
    rms = lax.rsqrt(squares / (HALVES * width) + EPS)
    total = x_ref[0].astype(F32)
    inner = 0.0
    scaled = []
    for half in range(HALVES):
        gain = small_refs[half][6:7, :]
        gated = (mixes[half] * rms * gain).astype(BF16)
        total = total + dot(gated, wnat[half])
        keep_ref[half, :, width:] += dot(cot_t[0:core], gated)
        acc[half, :, width:] += dot(cot_t[core:], gated)
        grad = dot(cot, wo[half])
        gaing_ref[half : half + 1, :] += jnp.sum(grad * mixes[half] * rms, axis=0, keepdims=True)
        grad = grad * gain
        inner = inner + jnp.sum(grad * mixes[half], axis=-1, keepdims=True)
        scaled.append(grad)
    result_ref[0] = total.astype(BF16)
    factor = rms * rms * rms * (inner / (HALVES * width))
    for half, dy_ref in enumerate((dy0_ref, dy1_ref)):
        grad_mixed = rms * scaled[half] - mixes[half] * factor
        gate = gates[half]
        sg = sigmoid(gate)
        dy_ref[...] = (grad_mixed * (gate * sg)).astype(BF16)
        dgate = (grad_mixed * y_refs[half][...].astype(F32) * (sg * (1.0 + gate * (1.0 - sg)))).astype(BF16)
        dgate_ref[half] = dgate
        keep_ref[half, :, 0:width] += dot(normed_t[0:core], dgate)
        acc[half, :, 0:width] += dot(normed_t[core:], dgate)

    @pl.when(step == pl.num_programs(0) - 1)
    def _():
        send_ref[...] = acc[...].astype(BF16)
        pre_ref[:, 0:core] = along_lanes(
            sum(weighted_tiles(keep_ref[half, :, 0:width], wg[half, 0:core, :]) for half in range(HALVES))
        )
        pre_ref[:, core:] = along_lanes(
            sum(weighted_tiles(acc[half, :, 0:width], wg[half, core:, :]) for half in range(HALVES))
        )


def backward_kernel(first_head, has_maps, has_step, *refs):
    c_ref, vin_ref, dy_ref, state_ref, maps_ref, mapst_ref, steps_ref, cumr_ref, taps_ref, rate_ref = refs[:10]
    dvin_ref, dmaps_ref, dstep_ref, tapsg_ref, headg_ref, buf, dstate, dgt, uacc, vacc, vrems, dyes, pick, upper = refs[-14:]
    step = pl.program_id(0)
    width = buf.shape[1]
    n = dstate.shape[0]
    hb = BLOCK // 2

    @pl.when(step == 0)
    def _():
        buf[pl.ds(BLOCK, 8), :] = jnp.zeros((8, width), F32)
        dstate[...] = jnp.zeros(dstate.shape, F32)
        row = lax.broadcasted_iota(jnp.int32, pick.shape, 0)
        col = lax.broadcasted_iota(jnp.int32, pick.shape, 1)
        pick[...] = jnp.where(row % width // 64 + first_head == col, 1.0, 0.0).astype(BF16)
        row = lax.broadcasted_iota(jnp.int32, upper.shape, 0)
        col = lax.broadcasted_iota(jnp.int32, upper.shape, 1)
        upper[...] = jnp.where(row <= col, 1.0, 0.0).astype(BF16)
        tapsg_ref[...] = jnp.zeros(tapsg_ref.shape, F32)
        headg_ref[...] = jnp.zeros(headg_ref.shape, F32)

    write = maps_ref[:, 0:n]
    read = maps_ref[:, n : 2 * n]
    read_t = mapst_ref[n : 2 * n, :]
    gt = dot_nt(write, read)
    state = state_ref[0]
    ds = dstate[...]
    ds_b = ds.astype(BF16)
    carried = dot(read, state.astype(BF16))
    wds = dot(write, ds_b)
    lane = lax.broadcasted_iota(jnp.int32, (BLOCK, 128), 1)
    steps = steps_ref[...]
    cumc = jnp.where(lane < 32, steps, 0.0)
    dtc = jnp.where(lane < 32, pltpu.roll(steps, PAD - 32, 1), 0.0)
    ecum = jnp.exp(cumc)
    last = jnp.exp(cumc[BLOCK - 1 : BLOCK, :] - cumc)
    rem = last * dtc
    lane_low = lane < 64
    sub = lax.broadcasted_iota(jnp.int32, (16, BLOCK), 0)
    tri = lax.broadcasted_iota(jnp.int32, (hb, hb), 1) >= lax.broadcasted_iota(jnp.int32, (hb, hb), 0)
    zeros = jnp.zeros((hb, hb), BF16)
    g00 = gt[0:hb, 0:hb]
    g01 = gt[0:hb, hb:]
    g11 = gt[hb:, hb:]
    dgt[...] = jnp.zeros(dgt.shape, F32)
    to_k = jnp.zeros((BLOCK, 128), F32)
    to_q = jnp.zeros((16, BLOCK), F32)
    for pair in range(width // 128):
        lanes = slice(pair * 128, pair * 128 + 128)
        cp = c_ref[:, lanes].astype(F32)
        v = cp * sigmoid(cp)
        vacc[:, lanes] = v
        dt_s = spread(dtc, first_head // 2 + pair, lane_low)
        vdt = (v * dt_s).astype(BF16)
        dyp = dy_ref[:, lanes]
        us = []
        for j in range(2):
            h = first_head + 2 * pair + j
            ck = jnp.broadcast_to(cumc[:, h : h + 1], (BLOCK, hb))
            cq = cumr_ref[h : h + 1, :]
            d00 = jnp.exp(jnp.where(tri, cq[:, 0:hb] - ck[0:hb], NEG))
            d01 = jnp.exp(cq[:, hb:] - ck[0:hb])
            d11 = jnp.exp(jnp.where(tri, cq[:, hb:] - ck[hb:], NEG))
            mine = jnp.where(lane_low if j == 0 else jnp.logical_not(lane_low), dyp, jnp.zeros_like(dyp))
            qt = dot_nt(vdt, mine)
            e00 = d00 * qt[0:hb, 0:hb]
            e01 = d01 * qt[0:hb, hb:]
            e11 = d11 * qt[hb:, hb:]
            dgt[0:hb, 0:hb] += e00
            dgt[0:hb, hb:] += e01
            dgt[hb:, hb:] += e11
            a = jnp.concatenate(
                [
                    jnp.concatenate([(g00 * d00).astype(BF16), (g01 * d01).astype(BF16)], axis=1),
                    jnp.concatenate([zeros, (g11 * d11).astype(BF16)], axis=1),
                ],
                axis=0,
            )
            z = jnp.concatenate(
                [
                    jnp.concatenate([(g00 * e00).astype(BF16), (g01 * e01).astype(BF16)], axis=1),
                    jnp.concatenate([zeros, (g11 * e11).astype(BF16)], axis=1),
                ],
                axis=0,
            )
            us.append(dot(a, dyp))
            to_k = to_k + dot(z, jnp.where(lane == h, 1.0, 0.0).astype(BF16))
            to_q = to_q + dot(jnp.where(sub == h, 1.0, 0.0).astype(BF16), z)
        uacc[:, lanes] = jnp.where(lane_low, us[0], us[1])
        ec = spread(ecum, first_head // 2 + pair, lane_low)
        rem_s = spread(rem, first_head // 2 + pair, lane_low)
        dye = (dyp.astype(F32) * ec).astype(BF16)
        u = uacc[:, lanes]
        dv = dt_s * u + taps_ref[5:6, lanes] * dyp.astype(F32) + rem_s * wds[:, lanes]
        sg = sigmoid(cp)
        buf[0:BLOCK, lanes] = dv * (sg * (1.0 + cp * (1.0 - sg)))
        dyes[:, lanes] = dye
        vrems[:, lanes] = (v * rem_s).astype(BF16)
        dstate[:, lanes] = ds[:, lanes] * ec[BLOCK - 1 : BLOCK, :]
    dstate[...] += dot(read_t, dyes[...])
    dmaps_w = dot_nt(vrems[...], ds_b)
    dmaps_r = dot_nt(dyes[...], state.astype(BF16))
    dg_b = dgt[...].astype(BF16)
    dmaps_w = dmaps_w + dot(dg_b, read)
    dmaps_r = dmaps_r + dot_tn(dg_b, write)
    if has_maps:
        dmaps_w = dmaps_w + refs[10][:, 0:n]
        dmaps_r = dmaps_r + refs[10][:, n : 2 * n]
    dmaps_ref[:, 0:n] = dmaps_w
    dmaps_ref[:, n : 2 * n] = dmaps_r

    def per_head(values):
        high = values.astype(BF16)
        low = (values - high.astype(F32)).astype(BF16)
        return dot(jnp.concatenate([high, low], axis=1), pick[...])

    v = vacc[...]
    dy = dy_ref[...].astype(F32)
    v_u = per_head(v * uacc[...])
    v_wds = per_head(v * wds)
    dy_c = per_head(dy * carried)
    skip_sum = jnp.sum(dy * v, axis=0, keepdims=True)
    ss = per_head(jnp.broadcast_to(jnp.sum(ds * state, axis=0, keepdims=True), (8, width)))
    sent = rem * v_wds
    d_last = ecum[BLOCK - 1 : BLOCK, :] * ss[0:1, :] + jnp.sum(sent, axis=0, keepdims=True)
    dcum = jnp.concatenate([to_q, jnp.zeros((112, BLOCK), F32)], axis=0).T - to_k + ecum * dy_c - sent
    token = lax.broadcasted_iota(jnp.int32, (BLOCK, 128), 0)
    dcum = dcum + jnp.where(token == BLOCK - 1, d_last, 0.0)
    dlog = dot_twice(upper[...], dcum)
    rate = rate_ref[7:8, :]
    ddt = v_u + last * v_wds + dlog * rate
    mine = jnp.logical_and(lane >= first_head, lane < first_head + width // 64)
    draw = jnp.where(mine, ddt * pltpu.roll(steps, 64, 1), 0.0)
    dstep = draw.astype(BF16)
    dstep_ref[...] = dstep + refs[10 + has_maps][...] if has_step else dstep
    headg_ref[0:1, :] += jnp.sum(draw, axis=0, keepdims=True)
    headg_ref[1:2, :] += jnp.sum(dlog * dtc, axis=0, keepdims=True) * rate
    headg_ref[2:3, :] += per_head(jnp.broadcast_to(skip_sum, (8, width)))[0:1, :]

    vin = vin_ref[...].astype(F32)
    total = jnp.zeros((BLOCK, width), F32)
    for j in range(4):
        shifted = buf[pl.ds(3 - j, BLOCK), :]
        total = total + taps_ref[j : j + 1, :] * shifted
        tapsg_ref[j : j + 1, :] += jnp.sum(shifted * vin, axis=0, keepdims=True)
    tapsg_ref[4:5, :] += jnp.sum(buf[0:BLOCK, :], axis=0, keepdims=True)
    dvin_ref[...] = total.astype(BF16)
    buf[pl.ds(BLOCK, 8), :] = buf[pl.ds(0, 8), :]


def split_products(normedt_ref, groups, weight, send_ref, keep_ref, pre):
    core = keep_ref.shape[0]

    def product(target, first):
        col, total = 0, 0.0
        for group in groups:
            cols = slice(col, col + group.shape[-1])
            value = dot(normedt_ref[...], group[...])
            target[:, cols] = value.astype(target.dtype)
            total = total + weighted_tiles(value, weight[first : first + core, cols])
            col = cols.stop
        pre[:, first : first + core] = along_lanes(total)

    @pl.when(pl.program_id(0) == 0)
    def _():
        product(send_ref, core)

    @pl.when(pl.program_id(0) == 1)
    def _():
        product(keep_ref, 0)


def partial_kernel(normedt_ref, *refs):
    groups, pieces = refs[:-9], refs[-9:-5]
    keep_ref, send_ref, pre_ref, weight, sems = refs[-5:]

    @pl.when(pl.program_id(0) == 0)
    def _():
        for copy in load_rows(pieces, weight, sems):
            copy.wait()

    split_products(normedt_ref, groups, weight, send_ref, keep_ref, pre_ref)


def late_kernel(normedt_ref, dmaps_ref, statein_ref, statec_ref, taps_ref, pm_ref, shared_ref, gain_ref, pre0_ref, pre1_ref, *refs):
    count = HALVES * SEGMENTS
    tap_refs, head_refs = refs[:count], refs[count : 2 * count]
    groups, pieces = refs[2 * count : -16], refs[-16:-8]
    keep_ref, send_ref, dstate_ref, sums_ref, buf, weight, pre, sems = refs[-8:]
    length, n2 = statein_ref.shape
    width = weight.shape[0]
    seg_w = tap_refs[0].shape[1]
    step = pl.program_id(0)

    @pl.when(step == 0)
    def _():
        columns = weight.shape[1] - n2
        copies = load_rows(pieces[:4], weight.at[:, pl.ds(0, columns)], sems)
        copies += load_rows(pieces[4:], weight.at[:, pl.ds(columns, n2)], sems, 4)
        sums_ref[...] = jnp.zeros(sums_ref.shape, F32)
        for half, first in enumerate((16, 0)):
            mine = range(half * SEGMENTS, (half + 1) * SEGMENTS)
            for i, segment in enumerate(mine):
                sums_ref[first : first + 5, i * seg_w : (i + 1) * seg_w] = tap_refs[segment][0:5, :]
            sums_ref[first + 5 : first + 6, :] = gain_ref[half : half + 1, :]
            head = sum((head_refs[segment][...] for segment in mine[1:]), head_refs[mine[0]][...])
            for i in range(3):
                sums_ref[first + 6 : first + 7, i * PAD : (i + 1) * PAD] = head[i : i + 1, :]
        c = statec_ref[...]
        sg = sigmoid(c)
        dc = dmaps_ref[...] * (sg * (1.0 + c * (1.0 - sg)))
        buf[0:length, :] = dc
        buf[pl.ds(length, 8), :] = jnp.zeros((8, n2), F32)
        state_in = statein_ref[...]
        total = jnp.zeros((length, n2), F32)
        for j in range(4):
            shifted = buf[pl.ds(3 - j, length), :]
            total = total + taps_ref[j : j + 1, :] * shifted
            sums_ref[8 + j : 9 + j, 0:n2] = jnp.sum(shifted * state_in, axis=0, keepdims=True)
        sums_ref[12:13, 0:n2] = jnp.sum(dc, axis=0, keepdims=True)
        dstate_ref[...] = total.astype(BF16)
        for copy in copies:
            copy.wait()

    split_products(normedt_ref, groups + (dstate_ref,), weight, send_ref, keep_ref, pre)

    @pl.when(step == 1)
    def _():
        high, mid, low = split3(pre[...] + pre0_ref[...] + pre1_ref[...])
        total = dot_nt(high, pm_ref[...]) + dot_nt(mid, pm_ref[...]) + dot_nt(low, pm_ref[...])
        sums_ref[13:14, :] = total[0:1, :] / shared_ref[0:1, :]


def turn_value_kernel(*refs):
    pmt_ref, pieces = refs[0], refs[1:-7]
    tv_ref, to_ref, ts_ref, wv, wo, ws, sems = refs[-7:]
    copies = load_rows(pieces[:4], wv, sems) + load_rows(pieces[4:8], wo, sems, 4) + load_rows(pieces[8:], ws, sems, 8)
    for copy in copies:
        copy.wait()
    tv_ref[...] = dot_tn(wv[...], pmt_ref[...]).astype(BF16)
    to_ref[...] = dot_tn(wo[...], pmt_ref[...]).astype(BF16)
    ts_ref[...] = dot_tn(ws[...], pmt_ref[...]).astype(BF16)


def turn_gate_kernel(*refs):
    pmt_ref, pieces = refs[0], refs[1:-3]
    tg_ref, wg, sems = refs[-3:]
    for copy in load_halves(pieces, wg, sems, 0, pl.ds(0, wg.shape[2])):
        copy.wait()
    for half in range(HALVES):
        tg_ref[half] = dot_tn(wg[half], pmt_ref[...]).astype(BF16)


def input_kernel(*refs):
    x_ref, cot_ref, shared_ref, dgate_ref, dstate_ref, tg_ref, tv_ref, to_ref, ts_ref = refs[:9]
    count = HALVES * SEGMENTS
    dvin_refs, dstep_refs = refs[9 : 9 + count], refs[9 + count : 9 + count + HALVES]
    grad_ref = refs[-1]
    width = x_ref.shape[2]
    total = dot(dstate_ref[...], ts_ref[...])
    for half, weights in enumerate((tv_ref, to_ref)):
        total = total + dot(dgate_ref[half], tg_ref[half]) + dot(dstep_refs[half][...], weights[width:, :])
        for segment in range(SEGMENTS):
            dvin = dvin_refs[half * SEGMENTS + segment][...]
            cols = dvin.shape[1]
            total = total + dot(dvin, weights[segment * cols : segment * cols + cols, :])
    x = x_ref[0].astype(F32)
    inv = lax.rsqrt(jnp.mean(x * x, axis=-1, keepdims=True) + EPS)
    scaled = total * shared_ref[0:1, :]
    inner = jnp.mean(scaled * x, axis=-1, keepdims=True)
    grad_ref[0] = cot_ref[0].astype(F32) + inv * scaled - x * (inv * inv * inv * inner)


def early_end_kernel(keep_ref, *refs):
    gate_ref, out_ref = refs[-2:]
    rows, width = gate_ref.shape
    total = keep_ref[0:rows, :]
    for ref in refs[:-2]:
        total = total + ref[...].astype(F32)
    gate_ref[...] = total[:, 0:width]
    out_ref[...] = total[:, width:]


def late_end_kernel(keep_ref, *refs):
    value_ref, step_ref, state_ref = refs[-3:]
    rows, width = value_ref.shape
    total = keep_ref[0:rows, :]
    for ref in refs[:-3]:
        total = total + ref[...].astype(F32)
    value_ref[...] = total[:, 0:width]
    step_ref[...] = total[:, width : width + PAD].T[0 : step_ref.shape[0], :]
    state_ref[...] = total[:, width + PAD :]


def sums_end_kernel(
    sums_ref, got_ref,
    prenorm_ref, taps_ref, shift_ref, staps_ref, sshift_ref, bias_ref, decay_ref, skip_ref, gain_ref,
):
    total = sums_ref[...] + got_ref[...]
    n2 = sshift_ref.shape[0]
    heads = bias_ref.shape[0]
    taps_ref[...] = total[0:4, :]
    shift_ref[...] = total[4, :]
    gain_ref[...] = total[5, :]
    bias_ref[...] = total[6, 0:PAD][0:heads]
    decay_ref[...] = total[6, PAD : 2 * PAD][0:heads]
    skip_ref[...] = total[6, 2 * PAD : 3 * PAD][0:heads]
    staps_ref[...] = total[8:12, 0:n2]
    sshift_ref[...] = total[12, 0:n2]
    prenorm_ref[...] = total[13, :]


def call(body, grid, in_specs, out_specs, out_shape, scratch=(), flops=0, vmem=24, aliases={}):
    return pl.pallas_call(
        body,
        grid=grid,
        in_specs=in_specs,
        out_specs=out_specs,
        out_shape=out_shape,
        scratch_shapes=list(scratch),
        input_output_aliases=aliases,
        compiler_params=pltpu.CompilerParams(
            vmem_limit_bytes=vmem * MIB, dimension_semantics=("arbitrary",) * len(grid)
        ),
        cost_estimate=pl.CostEstimate(flops=flops, bytes_accessed=10_000_000, transcendentals=0),
    )


def shape(dims, dtype=F32):
    return jax.ShapeDtypeStruct(dims, dtype)


def hbm(v):
    return pltpu.with_memory_space_constraint(v, pltpu.HBM)


def fixed(dims, *index):
    return pl.BlockSpec(dims, lambda *_: index)


ANYWHERE = pl.BlockSpec(memory_space=pl.ANY)
AXES = ("dp", "tensor")
TENSOR, CORE, CHIP = 1, 2, 4
FAR = 3


def swap(v, mask):
    count = lax.axis_size("dp") * lax.axis_size("tensor")
    return lax.ppermute(v, AXES, [(i, i ^ mask) for i in range(count)])


def far_masks():
    count = lax.axis_size("dp") * lax.axis_size("tensor")
    return [m << FAR for m in range(1, count >> FAR)]


def start_near(pack):
    return [pack] + [swap(pack, m) for m in far_masks()]


def start_far(v, rows):
    return [swap(v[(i + 1) * rows : (i + 2) * rows].astype(BF16), m) for i, m in enumerate(far_masks())]


def wide(*parts):
    return sum((part.astype(F32) for part in parts[1:]), parts[0].astype(F32))


def meet(*values):
    return lax.optimization_barrier(values)


def after(v, *others):
    return lax.optimization_barrier((v,) + others)[0]


def local(
    inputs,
    prenorm,
    gate_weight,
    value_weight,
    state_weight,
    step_weight,
    value_conv,
    value_shift,
    state_conv,
    state_shift,
    step_shift,
    decay_log,
    skip_scale,
    gated_gain,
    output_matrix,
    cotangent,
):
    length, width = inputs.shape[1:]
    rows, w = gate_weight.shape
    heads = step_weight.shape[1]
    n = state_weight.shape[1] // 2
    n2 = 2 * n
    blocks = length // BLOCK
    quarter = width // 4
    wp = w + PAD
    whole = lambda v: fixed(v.shape, *([0] * v.ndim))
    row_block = lambda dims: pl.BlockSpec(dims, lambda b: (b, 0))
    col_block = lambda dims: pl.BlockSpec(dims, lambda b: (0, b))
    tokens = pl.BlockSpec((1, BLOCK, width), lambda b: (0, b, 0))
    halves = lambda last: pl.BlockSpec((HALVES, BLOCK, last), lambda b: (0, b, 0))
    square = fixed((width, width), 0, 0)
    small_spec = fixed((8, w), 0, 0)
    sems = lambda count: pltpu.SemaphoreType.DMA((count,))

    to_pack = (
        value_conv, value_shift, skip_scale, gated_gain, step_shift, decay_log, prenorm, state_shift,
        gate_weight, value_weight, step_weight.T, output_matrix.T,
    )
    small, shared, vpack, gpack = call(
        pack_kernel,
        (1,),
        [whole(v) for v in to_pack],
        [small_spec, fixed((8, width), 0, 0), fixed((rows, wp), 0, 0), fixed((rows, 2 * w), 0, 0)],
        [shape((8, w)), shape((8, width)), shape((rows, wp), BF16), shape((rows, 2 * w), BF16)],
        flops=1_000_000,
    )(*(hbm(v) for v in to_pack))

    spot = jnp.arange(width)
    owner = lax.axis_index("dp") ^ (
        spot // (2 * quarter) + 2 * (spot // quarter % 2) + 4 * (spot % quarter // rows)
    )
    natural = owner * rows + spot % rows
    pm = (spot[:, None] == natural[None, :]).astype(BF16)
    pmt = (natural[:, None] == spot[None, :]).astype(BF16)

    near = jnp.concatenate(start_near(state_weight), axis=0)
    chip = swap(near, CHIP)
    state_own = (near, chip, swap(near, CORE), swap(chip, CORE))
    value_near = jnp.concatenate(start_near(vpack), axis=0)
    value_chip, value_y = swap(value_near, CHIP), swap(value_near, TENSOR)
    gate_near = start_near(after(gpack, chip))
    smalls = (small, swap(small, TENSOR))

    normed, normed_t, state_in, state_c, maps, maps_t = call(
        maps_kernel,
        (blocks,),
        [tokens, square, square] + [ANYWHERE] * 4 + [fixed((4, n2), 0, 0), fixed((8, width), 0, 0)],
        [row_block((BLOCK, width)), col_block((width, BLOCK)), row_block((BLOCK, n2)), row_block((BLOCK, n2)),
         row_block((BLOCK, n2)), col_block((n2, BLOCK))],
        [shape((length, width), BF16), shape((width, length), BF16), shape((length, n2)), shape((length, n2)),
         shape((length, n2), BF16), shape((n2, length), BF16)],
        [pltpu.VMEM((BLOCK + 8, n2), F32), pltpu.VMEM((width, n2), BF16), sems(4)],
        flops=6_000_000_000,
    )(inputs, pm, pmt, *state_own, state_conv, after(shared, smalls[1]))

    def forward(pieces, half, normed):
        return call(
            forward_kernel,
            (blocks,),
            [ANYWHERE] * len(pieces)
            + [row_block((BLOCK, width)), small_spec, row_block((BLOCK, n2)), col_block((n2, BLOCK))],
            [row_block((BLOCK, w))] * 3 + [pl.BlockSpec((1, n, w), lambda b: (b, 0, 0))]
            + [row_block((BLOCK, PAD)), col_block((16, BLOCK))],
            [pltpu.HBM((length, w), BF16), pltpu.HBM((length, w), BF16), shape((length, w), BF16),
             pltpu.HBM((blocks, n, w), F32), pltpu.HBM((length, PAD), F32), pltpu.HBM((16, length), F32)],
            [pltpu.VMEM((BLOCK + 8, w), F32), pltpu.VMEM((n, w), F32), pltpu.VMEM((width, wp), BF16), sems(4)],
            flops=12_000_000_000,
        )(*pieces, normed, smalls[half], maps, maps_t)

    normed, value_chip, value_y, *gate_near = meet(normed, value_chip, value_y, *gate_near)
    value_own = (value_near, value_chip, swap(value_near, CORE), swap(value_chip, CORE))
    value_yx = swap(value_chip, TENSOR)
    gate_near = jnp.concatenate(gate_near, axis=0)
    gate_y, gate_x = swap(gate_near, TENSOR), swap(gate_near, CHIP)
    scan_own = forward(value_own, 0, after(normed, gate_near))
    normed, value_y, value_yx, gate_x, _ = meet(normed, value_y, value_yx, gate_x, scan_own[2])
    gate_yx = swap(gate_x, TENSOR)
    value_other = (value_y, value_yx, swap(value_y, CORE), swap(value_yx, CORE))
    scan_other = forward(value_other, 1, normed)
    scans = (scan_own, scan_other)

    both_w = (HALVES, width, w)
    given = (after(pmt, scan_other[2]), *value_own, *value_other, *state_own)
    turned = call(
        turn_value_kernel,
        (1,),
        [square] + [ANYWHERE] * 12,
        [fixed((wp, width), 0, 0), fixed((wp, width), 0, 0), fixed((n2, width), 0, 0)],
        [shape((wp, width), BF16), shape((wp, width), BF16), shape((n2, width), BF16)],
        [pltpu.VMEM((width, wp), BF16), pltpu.VMEM((width, wp), BF16), pltpu.VMEM((width, n2), BF16), sems(12)],
        flops=4_000_000_000,
    )(*given)
    half_rows = (HALVES, width // 2, 2 * w)
    gate_y, gate_yx, _ = meet(gate_y, gate_yx, turned[0])
    gate_pieces = (gate_near, gate_x, gate_y, gate_yx)
    gate_pieces += tuple(swap(v, CORE) for v in gate_pieces)
    result, dy0, dy1, dgate, early_send, early_keep, gain_partial, gate_pre = call(
        gated_kernel,
        (blocks,),
        [tokens, tokens, row_block((BLOCK, width)), col_block((width, BLOCK)), row_block((BLOCK, w)),
         row_block((BLOCK, w)), small_spec, small_spec, square, square] + [ANYWHERE] * 8,
        [tokens, row_block((BLOCK, w)), row_block((BLOCK, w)), halves(w), fixed(half_rows, 0, 0, 0),
         fixed(half_rows, 0, 0, 0), fixed((HALVES, w), 0, 0), fixed((8, width), 0, 0)],
        [shape(inputs.shape, BF16), shape((length, w), BF16), shape((length, w), BF16),
         shape((HALVES, length, w), BF16), shape(half_rows, BF16), shape(half_rows), shape((HALVES, w)),
         shape((8, width))],
        [pltpu.VMEM(both_w, BF16), pltpu.VMEM(both_w, BF16), pltpu.VMEM(both_w, BF16), pltpu.VMEM(half_rows, F32),
         sems(16)],
        flops=25_000_000_000,
        vmem=48,
    )(inputs, cotangent, normed, normed_t, scans[0][2], scans[1][2], *smalls, pm, pmt, *gate_pieces)

    seg_w = w // SEGMENTS
    seg_heads = heads // SEGMENTS

    def backward(half, segment, dy, dmaps=None, dstep=None):
        back = lambda dims, col=0: pl.BlockSpec(dims, lambda b: (blocks - 1 - b, col))
        value_in, value_c, _, states, steps, cumr = scans[half]
        extra = ([dmaps] if dmaps is not None else []) + ([dstep] if dstep is not None else [])
        return call(
            functools.partial(backward_kernel, segment * seg_heads, dmaps is not None, dstep is not None),
            (blocks,),
            [back((BLOCK, seg_w), segment)] * 3
            + [pl.BlockSpec((1, n, seg_w), lambda b: (blocks - 1 - b, 0, segment)), back((BLOCK, n2)),
               pl.BlockSpec((n2, BLOCK), lambda b: (0, blocks - 1 - b))] + [back((BLOCK, PAD))]
            + [pl.BlockSpec((16, BLOCK), lambda b: (0, blocks - 1 - b)), fixed((8, seg_w), 0, segment),
               fixed((8, PAD), 0, 1)] + [back((BLOCK, v.shape[1])) for v in extra],
            [back((BLOCK, seg_w)), back((BLOCK, n2)), back((BLOCK, PAD)), fixed((8, seg_w), 0, 0), fixed((8, PAD), 0, 0)],
            [shape((length, seg_w), BF16), shape((length, n2)), shape((length, PAD), BF16), shape((8, seg_w)),
             shape((8, PAD))],
            [pltpu.VMEM((BLOCK + 8, seg_w), F32), pltpu.VMEM((n, seg_w), F32), pltpu.VMEM((BLOCK, BLOCK), F32),
             pltpu.VMEM((BLOCK, seg_w), F32), pltpu.VMEM((BLOCK, seg_w), F32), pltpu.VMEM((BLOCK, seg_w), BF16),
             pltpu.VMEM((BLOCK, seg_w), BF16), pltpu.VMEM((2 * seg_w, PAD), BF16), pltpu.VMEM((BLOCK, BLOCK), BF16)],
            flops=12_000_000_000,
        )(hbm(value_c), hbm(value_in), dy, hbm(states), maps, maps_t, hbm(steps), hbm(cumr), smalls[half], smalls[half],
          *extra)

    core = width // 2
    lead = pl.BlockSpec((core, length), lambda b: (1 - b, 0))
    split_specs = lambda cols: [fixed((core, cols), 0, 0)] * 2
    split_shapes = lambda cols: [shape((core, cols)), shape((core, cols), BF16)]

    early_got = swap(early_send, CORE)
    other0 = backward(1, 0, dy1)
    early_keep, early_got, _ = meet(early_keep, early_got, other0[2])
    gate = wide(early_keep[:, :, :w], early_got[:, :, :w])
    out = wide(early_keep[:, :, w:], early_got[:, :, w:])
    gate_out, gate = gate[1].astype(BF16), gate[0]
    out_out, out = out[:, quarter:].astype(BF16), out[:, :quarter]
    gate_got, out_got = swap(gate_out, TENSOR), swap(out_out, CHIP)
    other1 = backward(1, 1, after(dy1, gate_out, gate, out_out, out), other0[1], other0[2])
    gate, out, gate_got, out_got, _ = meet(gate, out, gate_got, out_got, other1[2])
    gate, out = wide(gate, gate_got), wide(out, out_got)
    gate_out, gate = gate[quarter:].astype(BF16), gate[:quarter]
    out_out, out = out[1].astype(BF16), out[0]
    gate_got, out_got = swap(gate_out, CHIP), swap(out_out, TENSOR)
    groups = (other0[0], other1[0], after(other1[2], gate_out, gate, out_out, out))
    other_keep, other_send, other_pre = call(
        partial_kernel,
        (2,),
        [lead] + [whole(v) for v in groups] + [ANYWHERE] * 4,
        split_specs(wp) + [fixed((8, width), 0, 0)],
        split_shapes(wp) + [shape((8, width))],
        [pltpu.VMEM((width, wp), BF16), sems(4)],
        flops=3_000_000_000,
    )(normed_t, *groups, *value_other)
    other_got = swap(other_send, CORE)
    own0 = backward(0, 0, after(dy0, other_send), other1[1])
    gate, out, gate_got, out_got, other_keep, other_got, _ = meet(
        gate, out, gate_got, out_got, other_keep, other_got, own0[2]
    )
    other_out = wide(other_keep, other_got).astype(BF16)
    other_got = swap(other_out, TENSOR)
    early = jnp.concatenate([wide(gate, gate_got), wide(out, out_got)], axis=1)
    early_far = start_far(early, rows)
    own1 = backward(0, 1, after(dy0, other_out, early), own0[1], own0[2])

    def end(body, given, dims):
        return call(
            body, (1,), [whole(v) for v in given], [fixed(d, *([0] * len(d))) for d in dims], [shape(d) for d in dims],
            flops=1_000_000,
        )(*given)

    dmaps, other_got, early, *early_far = meet(own1[1], other_got, early, *early_far)
    gate_grad, out_grad = end(early_end_kernel, (early, *early_far), ((rows, w), (rows, w)))
    groups = (own0[0], own1[0], own1[2])
    parts = (own0, own1, other0, other1)
    given = (
        (dmaps, state_in, state_c, state_conv, pm, shared, gain_partial, gate_pre, other_pre)
        + tuple(part[3] for part in parts) + tuple(part[4] for part in parts) + groups
    )
    late_keep, late_send, dstate, sums = call(
        late_kernel,
        (2,),
        [lead] + [whole(v) for v in given] + [ANYWHERE] * 8,
        split_specs(wp + n2) + [fixed((length, n2), 0, 0), fixed((24, width), 0, 0)],
        split_shapes(wp + n2) + [shape((length, n2), BF16), shape((24, width))],
        [pltpu.VMEM((length + 8, n2), F32), pltpu.VMEM((width, wp + n2), BF16), pltpu.VMEM((8, width), F32), sems(8)],
        flops=4_000_000_000,
    )(normed_t, *given, *value_own, *state_own)
    late_got, sums_got = swap(late_send, CORE), swap(sums, CORE)
    turned_gate = call(
        turn_gate_kernel,
        (1,),
        [square] + [ANYWHERE] * 8,
        [fixed(both_w, 0, 0, 0)],
        [shape(both_w, BF16)],
        [pltpu.VMEM(both_w, BF16), sems(16)],
        flops=2_000_000_000,
    )(after(pmt, late_send), *gate_pieces)[0]
    late_keep, late_got, other_got, sums, sums_got, turned_gate = meet(
        late_keep, late_got, other_got, sums, sums_got, turned_gate
    )
    state = wide(late_keep[:, wp:], late_got[:, wp:])
    late = wide(late_keep[:, :wp], late_got[:, :wp], other_got)
    state_out, late_out = state.astype(BF16), late[quarter:].astype(BF16)
    state, late = state[:quarter], late[:quarter]
    sums = sums + sums_got
    late_got = (
        swap(jnp.concatenate([late_out, state_out[quarter:]], axis=1), CHIP),
        swap(state_out[:quarter], TENSOR),
        swap(state_out[quarter:], CHIP | TENSOR),
    )
    sums_got = swap(sums[:16], TENSOR)

    def input_part(dgate, first, grad=None):
        token = pl.BlockSpec((1, BLOCK, width), lambda b: (0, b + first, 0))
        tall = lambda cols: pl.BlockSpec((BLOCK, cols), lambda b: (b + first, 0))
        given = (
            (inputs, cotangent, shared, dgate, dstate, turned_gate, *turned)
            + tuple(part[0] for part in parts) + (own1[2], other1[2])
        )
        return call(
            input_kernel,
            (blocks // 2,),
            [token, token, fixed((8, width), 0, 0), pl.BlockSpec((HALVES, BLOCK, w), lambda b: (0, b + first, 0)), tall(n2),
             fixed(both_w, 0, 0, 0)] + [whole(v) for v in turned] + [tall(seg_w)] * len(parts) + [tall(PAD)] * HALVES
            + ([] if grad is None else [ANYWHERE]),
            [token],
            [shape(inputs.shape)],
            flops=6_000_000_000,
            aliases={} if grad is None else {len(given): 0},
        )(*given, *(() if grad is None else (grad,)))[0]

    input_grad = input_part(after(dgate, late_out, late, state_out, state, sums), 0)
    late, state, sums, sums_got, input_grad, *late_got = meet(late, state, sums, sums_got, input_grad, *late_got)
    late = jnp.concatenate(
        [wide(late, late_got[0][:, :wp]), wide(state, late_got[0][:, wp:], late_got[1], late_got[2])], axis=1
    )
    late_far = start_far(late, rows)
    sums = jnp.concatenate([sums[16:] + sums_got[:8], sums[8:16] + sums_got[8:]], axis=0)
    bits = [1 << FAR]
    while 2 * bits[-1] < lax.axis_size("dp") * lax.axis_size("tensor"):
        bits.append(2 * bits[-1])
    bits.append(CHIP)
    sums_got = swap(sums, bits[0])
    input_grad = input_part(after(dgate, late, sums), blocks // 2, input_grad)
    sums, sums_got, input_grad = meet(sums, sums_got, input_grad)
    for bit in bits[1:]:
        sums = sums + sums_got
        sums_got = swap(sums, bit)

    value_grad, step_grad, state_grad = end(
        late_end_kernel, (late, *late_far), ((rows, w), (heads, rows), (rows, n2))
    )
    prenorm_grad, taps, shift, state_taps, state_bias, bias, decay, skip, gain = end(
        sums_end_kernel,
        (sums, sums_got),
        ((width,), (4, w), (w,), (4, n2), (n2,), (heads,), (heads,), (heads,), (w,)),
    )
    return (
        result, input_grad, prenorm_grad, gate_grad, value_grad, state_grad, step_grad.T, taps, shift, state_taps,
        state_bias, bias, decay, skip, gain, out_grad.T,
    )


def solution(mesh):
    in_specs = (
        P(("dp", "tensor"), None, None),
        P(),
        P("dp", "tensor"),
        P("dp", "tensor"),
        P("dp", None),
        P("dp", "tensor"),
        P(None, "tensor"),
        P("tensor"),
        P(),
        P(),
        P("tensor"),
        P("tensor"),
        P("tensor"),
        P("tensor"),
        P("tensor", "dp"),
        P(("dp", "tensor"), None, None),
    )
    out_specs = (
        P(("dp", "tensor"), None, None),
        P(("dp", "tensor"), None, None),
        P(),
        P("dp", "tensor"),
        P("dp", "tensor"),
        P("dp", None),
        P("dp", "tensor"),
        P(None, "tensor"),
        P("tensor"),
        P(),
        P(),
        P("tensor"),
        P("tensor"),
        P("tensor"),
        P("tensor"),
        P("tensor", "dp"),
    )
    return jax.shard_map(local, mesh=mesh, in_specs=in_specs, out_specs=out_specs, check_vma=False)
```

```python
import functools

import jax
import jax.numpy as jnp
from jax import lax
from jax.experimental import pallas as pl
from jax.experimental.pallas import tpu as pltpu
from jax.sharding import PartitionSpec as P

BLOCK = 256
HALVES = 2
PAD = 128
SEGMENTS = 2
EPS = 1e-05
NEG = -1e30
F32 = jnp.float32
BF16 = jnp.bfloat16
MIB = 1024 * 1024


def dot(a, b):
    return jnp.dot(a, b, preferred_element_type=F32)


def dot_nt(a, b):
    return lax.dot_general(a, b, (((1,), (1,)), ((), ())), preferred_element_type=F32)


def dot_tn(a, b):
    return lax.dot_general(a, b, (((0,), (0,)), ((), ())), preferred_element_type=F32)


def split3(v):
    high = v.astype(BF16)
    rest = v - high.astype(F32)
    mid = rest.astype(BF16)
    low = (rest - mid.astype(F32)).astype(BF16)
    return high, mid, low


def dot_twice(mask, v):
    high = v.astype(BF16)
    return dot(mask, high) + dot(mask, (v - high.astype(F32)).astype(BF16))


def dot_exact(mask, v):
    high, mid, low = split3(v)
    return dot(mask, high) + dot(mask, mid) + dot(mask, low)


def sigmoid(v):
    return 0.5 * jnp.tanh(0.5 * v) + 0.5


def spread_pair(cols, pair, lane_low):
    rows = cols.shape[0]
    left = jnp.broadcast_to(cols[:, 2 * pair : 2 * pair + 1], (rows, 128))
    right = jnp.broadcast_to(cols[:, 2 * pair + 1 : 2 * pair + 2], (rows, 128))
    return jnp.where(lane_low, left, right)


def fill_spread(mask, first_head):
    row = lax.broadcasted_iota(jnp.int32, mask.shape, 0)
    col = lax.broadcasted_iota(jnp.int32, mask.shape, 1)
    mask[...] = jnp.where(row % PAD == first_head + col // 64, 1.0, 0.0).astype(BF16)


def spread(cols, mask):
    high = cols.astype(BF16)
    low = (cols - high.astype(F32)).astype(BF16)
    return dot(jnp.concatenate([high, low], axis=1), mask[...])


def conv_taps(buf, taps_ref, shift, first, rows):
    total = shift + taps_ref[0:1, :] * buf[pl.ds(first, rows), :]
    for j in range(1, 4):
        total = total + taps_ref[j : j + 1, :] * buf[pl.ds(first + j, rows), :]
    return total


def pack_kernel(
    taps_ref, shift_ref, skip_ref, gain_ref, bias_ref, decay_ref, prenorm_ref, sshift_ref,
    gate_ref, value_ref, stept_ref, outt_ref,
    small_ref, shared_ref, vpack_ref, gpack_ref,
):
    rows, width = gate_ref.shape
    heads = stept_ref.shape[0]
    n2 = sshift_ref.shape[0]
    gpack_ref[:, 0:width] = gate_ref[...]
    gpack_ref[:, width:] = outt_ref[...]
    vpack_ref[:, 0:width] = value_ref[...]
    vpack_ref[:, width:] = jnp.zeros((rows, PAD), BF16)
    vpack_ref[:, width : width + heads] = stept_ref[...].astype(F32).T.astype(BF16)
    small_ref[...] = jnp.zeros(small_ref.shape, F32)
    shared_ref[...] = jnp.zeros(shared_ref.shape, F32)
    small_ref[0:4, :] = taps_ref[...]
    small_ref[4, :] = shift_ref[...]
    head = lax.broadcasted_iota(jnp.int32, (1, width), 1) // (width // heads)
    skip_row = skip_ref[...].reshape(1, heads)
    skip = jnp.zeros((1, width), F32)
    for h in range(heads):
        skip = jnp.where(head == h, skip_row[:, h : h + 1], skip)
    small_ref[5:6, :] = skip
    small_ref[6, :] = gain_ref[...]
    small_ref[7:8, 0:heads] = bias_ref[...].reshape(1, heads)
    small_ref[7:8, PAD : PAD + heads] = -jnp.exp(decay_ref[...].reshape(1, heads))
    shared_ref[0, :] = prenorm_ref[...]
    shared_ref[1:2, 0:n2] = sshift_ref[...].reshape(1, n2)


def load_rows(pieces, target, sems, first=0, lanes=None, start=True):
    copies = []
    for i, piece in enumerate(pieces):
        rows = piece.shape[0]
        source = piece if lanes is None else piece.at[:, lanes]
        copies.append(pltpu.make_async_copy(source, target.at[pl.ds(i * rows, rows), :], sems.at[first + i]))
    for copy in copies if start else ():
        copy.start()
    return copies


def load_halves(pieces, target, sems, first, lanes, start=True):
    near0, x0, far0, near1, x1, far1 = pieces
    copies = load_rows((near0, x0, near1, x1), target.at[0], sems, first, lanes, start)
    return copies + load_rows((far0, far1), target.at[1], sems, first + 4, lanes, start)


def weighted_tiles(grad, weight):
    product = grad * weight.astype(F32)
    return sum((product[:, col : col + 128] for col in range(128, product.shape[1], 128)), product[:, 0:128])


def along_lanes(tiles):
    ones = jnp.ones((8, tiles.shape[1]), BF16)
    high = tiles.astype(BF16)
    return dot_nt(ones, high) + dot_nt(ones, (tiles - high.astype(F32)).astype(BF16))


def maps_kernel(
    x_ref, pm_ref, piece0, piece1, piece2, piece3, taps_ref, shared_ref,
    normed_ref, normedt_ref, statein_ref, statec_ref, maps_ref, mapst_ref,
    buf, ws, sems,
):
    step = pl.program_id(0)
    n2 = buf.shape[1]

    @pl.when(step == 0)
    def _():
        lanes = pl.ds(piece0.shape[1] - n2, n2)
        copies = load_rows((piece0, piece1, piece2, piece3), ws, sems, 0, lanes)
        buf[pl.ds(0, 8), :] = jnp.zeros((8, n2), F32)
        for copy in copies:
            copy.wait()

    x = x_ref[0].astype(F32)
    inv = lax.rsqrt(jnp.mean(x * x, axis=-1, keepdims=True) + EPS)
    normed = (x * inv * shared_ref[0:1, :]).astype(BF16)
    normed = dot(normed, pm_ref[...])
    normedt_ref[...] = normed.T.astype(BF16)
    normed = normed.astype(BF16)
    normed_ref[...] = normed
    state_in = dot(normed, ws[...])
    statein_ref[...] = state_in
    buf[pl.ds(8, BLOCK), :] = state_in
    c = conv_taps(buf, taps_ref, shared_ref[1:2, 0:n2], 5, BLOCK)
    buf[pl.ds(0, 8), :] = buf[pl.ds(BLOCK, 8), :]
    statec_ref[...] = c
    maps = c * sigmoid(c)
    maps_ref[...] = maps.astype(BF16)
    mapst_ref[...] = maps.T.astype(BF16)


def forward_kernel(*refs):
    pieces = refs[:-15]
    normed_ref, small_ref, maps_ref, mapst_ref = refs[-15:-11]
    vin_ref, c_ref, y_ref, state_ref, steps_ref, cumr_ref, buf, state, wv, mask, sems = refs[-11:]
    step = pl.program_id(0)
    width = buf.shape[1]
    n = state.shape[0]

    @pl.when(step == 0)
    def _():
        copies = load_rows(pieces, wv, sems, 0, pl.ds(0, width + PAD))
        buf[pl.ds(0, 8), :] = jnp.zeros((8, width), F32)
        state[...] = jnp.zeros(state.shape, F32)
        fill_spread(mask, 0)
        for copy in copies:
            copy.wait()

    raw = dot(normed_ref[...], wv[:, width:]) + small_ref[7:8, 0:PAD]
    soft = jnp.exp(-jnp.abs(raw))
    dtc = jnp.maximum(raw, 0.0) + jnp.log1p(soft)
    slope = jnp.where(raw >= 0, 1.0, soft) / (1.0 + soft)
    row = lax.broadcasted_iota(jnp.int32, (BLOCK, BLOCK), 0)
    col = lax.broadcasted_iota(jnp.int32, (BLOCK, BLOCK), 1)
    lower = jnp.where(row >= col, 1.0, 0.0).astype(BF16)
    cumc = dot_exact(lower, dtc * small_ref[7:8, PAD : 2 * PAD])
    lane = lax.broadcasted_iota(jnp.int32, (BLOCK, PAD), 1)
    steps_ref[...] = jnp.where(
        lane < 32, cumc, jnp.where(lane < 64, pltpu.roll(dtc, 32, 1), pltpu.roll(slope, 64, 1))
    )
    cumr = cumc.T[0:16, :]
    cumr_ref[...] = cumr
    value_in = dot(normed_ref[...], wv[:, 0:width])
    vin_ref[...] = value_in.astype(BF16)
    buf[pl.ds(8, BLOCK), :] = value_in
    c = conv_taps(buf, small_ref, small_ref[4:5, :], 5, BLOCK)
    buf[pl.ds(0, 8), :] = buf[pl.ds(BLOCK, 8), :]
    c_ref[...] = c.astype(BF16)
    state_ref[0] = state[...]
    write = maps_ref[:, 0:n]
    read = maps_ref[:, n : 2 * n]
    write_t = mapst_ref[0:n, :]
    grams = dot_nt(read, write)
    carried = dot(read, state[...].astype(BF16))
    ec_all = spread(jnp.exp(cumc), mask)
    rem_all = spread(jnp.exp(cumc[BLOCK - 1 : BLOCK, :] - cumc) * dtc, mask)
    dt_all = spread(dtc, mask)
    lane_low = lax.broadcasted_iota(jnp.int32, (BLOCK, 128), 1) < 64
    hb = BLOCK // 2
    tri = lax.broadcasted_iota(jnp.int32, (hb, hb), 0) >= lax.broadcasted_iota(jnp.int32, (hb, hb), 1)
    zeros = jnp.zeros((hb, hb), BF16)
    g00 = grams[0:hb, 0:hb]
    g10 = grams[hb:, 0:hb]
    g11 = grams[hb:, hb:]
    for pair in range(width // 128):
        lanes = slice(pair * 128, pair * 128 + 128)
        cp = c[:, lanes]
        v = cp * sigmoid(cp)
        vdt = (v * dt_all[:, lanes]).astype(BF16)
        outs = []
        for j in range(2):
            h = 2 * pair + j
            cq = jnp.broadcast_to(cumc[:, h : h + 1], (BLOCK, hb))
            ck = cumr[h : h + 1, :]
            d00 = jnp.exp(jnp.where(tri, cq[0:hb] - ck[:, 0:hb], NEG))
            d10 = jnp.exp(cq[hb:] - ck[:, 0:hb])
            d11 = jnp.exp(jnp.where(tri, cq[hb:] - ck[:, hb:], NEG))
            top = jnp.concatenate([(g00 * d00).astype(BF16), zeros], axis=1)
            bot = jnp.concatenate([(g10 * d10).astype(BF16), (g11 * d11).astype(BF16)], axis=1)
            outs.append(dot(jnp.concatenate([top, bot], axis=0), vdt))
        ec = ec_all[:, lanes]
        y = jnp.where(lane_low, outs[0], outs[1]) + ec * carried[:, lanes] + small_ref[5:6, lanes] * v
        y_ref[:, lanes] = y.astype(BF16)
        vrem = (v * rem_all[:, lanes]).astype(BF16)
        state[:, lanes] = state[:, lanes] * ec[BLOCK - 1 : BLOCK, :] + dot(write_t, vrem)


def gated_kernel(
    x_ref, cot_ref, normed_ref, normedt_ref, y0_ref, y1_ref, small0_ref, small1_ref, pmt_ref,
    near0, x0, far0, near1, x1, far1,
    result_ref, dy0_ref, dy1_ref, dgate_ref, send_ref, keep_ref, gaing_ref, pre_ref,
    wg, wo, wnat, acc, sems,
):
    step = pl.program_id(0)
    width = wg.shape[2]
    core = acc.shape[1]
    pieces = (near0, x0, far0, near1, x1, far1)

    @pl.when(step == 0)
    def _():
        copies = load_halves(pieces, wg, sems, 0, pl.ds(0, width))
        load_halves(pieces, wo, sems, 8, pl.ds(width, width))
        acc[...] = jnp.zeros(acc.shape, F32)
        keep_ref[...] = jnp.zeros(keep_ref.shape, F32)
        gaing_ref[...] = jnp.zeros(gaing_ref.shape, F32)
        for copy in copies:
            copy.wait()

    normed = normed_ref[...]
    normed_t = normedt_ref[...]
    cot = cot_ref[0]
    y_refs = (y0_ref, y1_ref)
    small_refs = (small0_ref, small1_ref)
    gates, mixes = [], []
    squares = 0.0
    for half in range(HALVES):
        gate = dot(normed, wg[half])
        mixed = y_refs[half][...].astype(F32) * (gate * sigmoid(gate))
        squares = squares + jnp.sum(mixed * mixed, axis=-1, keepdims=True)
        gates.append(gate)
        mixes.append(mixed)
    cot_t = dot_nt(pmt_ref[...], cot).astype(BF16)

    @pl.when(step == 0)
    def _():
        for copy in load_halves(pieces, wo, sems, 8, pl.ds(width, width), False):
            copy.wait()
        for half in range(HALVES):
            wnat[half] = dot_tn(wo[half], pmt_ref[...]).astype(BF16)

    rms = lax.rsqrt(squares / (HALVES * width) + EPS)
    total = x_ref[0].astype(F32)
    inner = 0.0
    scaled = []
    for half in range(HALVES):
        gain = small_refs[half][6:7, :]
        gated = (mixes[half] * rms * gain).astype(BF16)
        total = total + dot(gated, wnat[half])
        keep_ref[half, :, width:] += dot(cot_t[0:core], gated)
        acc[half, :, width:] += dot(cot_t[core:], gated)
        grad = dot_nt(cot, wnat[half])
        gaing_ref[half : half + 1, :] += jnp.sum(grad * mixes[half] * rms, axis=0, keepdims=True)
        grad = grad * gain
        inner = inner + jnp.sum(grad * mixes[half], axis=-1, keepdims=True)
        scaled.append(grad)
    result_ref[0] = total.astype(BF16)
    factor = rms * rms * rms * (inner / (HALVES * width))
    for half, dy_ref in enumerate((dy0_ref, dy1_ref)):
        grad_mixed = rms * scaled[half] - mixes[half] * factor
        gate = gates[half]
        sg = sigmoid(gate)
        dy_ref[...] = (grad_mixed * (gate * sg)).astype(BF16)
        dgate = (grad_mixed * y_refs[half][...].astype(F32) * (sg * (1.0 + gate * (1.0 - sg)))).astype(BF16)
        dgate_ref[half] = dgate
        keep_ref[half, :, 0:width] += dot(normed_t[0:core], dgate)
        acc[half, :, 0:width] += dot(normed_t[core:], dgate)

    @pl.when(step == pl.num_programs(0) - 1)
    def _():
        send_ref[...] = acc[...].astype(BF16)
        pre_ref[:, 0:core] = along_lanes(
            sum(weighted_tiles(keep_ref[half, :, 0:width], wg[half, 0:core, :]) for half in range(HALVES))
        )
        pre_ref[:, core:] = along_lanes(
            sum(weighted_tiles(acc[half, :, 0:width], wg[half, core:, :]) for half in range(HALVES))
        )


def backward_kernel(first_head, has_maps, has_step, *refs):
    c_ref, vin_ref, dy_ref, state_ref, maps_ref, mapst_ref, steps_ref, cumr_ref, taps_ref, rate_ref = refs[:10]
    dvin_ref, dmaps_ref, dstep_ref, tapsg_ref, headg_ref, buf, dstate, dgt, vacc, vrems, dyes, pick, upper, mask = refs[-14:]
    step = pl.program_id(0)
    width = buf.shape[1]
    n = dstate.shape[0]
    hb = BLOCK // 2

    @pl.when(step == 0)
    def _():
        buf[pl.ds(BLOCK, 8), :] = jnp.zeros((8, width), F32)
        dstate[...] = jnp.zeros(dstate.shape, F32)
        row = lax.broadcasted_iota(jnp.int32, pick.shape, 0)
        col = lax.broadcasted_iota(jnp.int32, pick.shape, 1)
        fill_spread(mask, first_head)
        pick[...] = jnp.where(row % width // 64 + first_head == col, 1.0, 0.0).astype(BF16)
        row = lax.broadcasted_iota(jnp.int32, upper.shape, 0)
        col = lax.broadcasted_iota(jnp.int32, upper.shape, 1)
        upper[...] = jnp.where(row <= col, 1.0, 0.0).astype(BF16)
        tapsg_ref[...] = jnp.zeros(tapsg_ref.shape, F32)
        headg_ref[...] = jnp.zeros(headg_ref.shape, F32)

    write = maps_ref[:, 0:n]
    read = maps_ref[:, n : 2 * n]
    read_t = mapst_ref[n : 2 * n, :]
    gt = dot_nt(write, read)
    state = state_ref[0]
    ds = dstate[...]
    ds_b = ds.astype(BF16)
    carried = dot(read, state.astype(BF16))
    wds = dot(write, ds_b)
    lane = lax.broadcasted_iota(jnp.int32, (BLOCK, 128), 1)
    steps = steps_ref[...]
    cumc = jnp.where(lane < 32, steps, 0.0)
    dtc = jnp.where(lane < 32, pltpu.roll(steps, PAD - 32, 1), 0.0)
    ecum = jnp.exp(cumc)
    last = jnp.exp(cumc[BLOCK - 1 : BLOCK, :] - cumc)
    rem = last * dtc
    ec_all = spread(ecum, mask)
    lane_low = lane < 64
    sub = lax.broadcasted_iota(jnp.int32, (16, BLOCK), 0)
    tri = lax.broadcasted_iota(jnp.int32, (hb, hb), 1) >= lax.broadcasted_iota(jnp.int32, (hb, hb), 0)
    zeros = jnp.zeros((hb, hb), BF16)
    g00 = gt[0:hb, 0:hb]
    g01 = gt[0:hb, hb:]
    g11 = gt[hb:, hb:]
    dgt[...] = jnp.zeros(dgt.shape, F32)
    to_k = jnp.zeros((BLOCK, 128), F32)
    to_q = jnp.zeros((16, BLOCK), F32)
    for pair in range(width // 128):
        lanes = slice(pair * 128, pair * 128 + 128)
        cp = c_ref[:, lanes].astype(F32)
        v = cp * sigmoid(cp)
        vacc[:, lanes] = v
        dt_s = spread_pair(dtc, first_head // 2 + pair, lane_low)
        vdt = (v * dt_s).astype(BF16)
        dyp = dy_ref[:, lanes]
        us = []
        for j in range(2):
            h = first_head + 2 * pair + j
            ck = jnp.broadcast_to(cumc[:, h : h + 1], (BLOCK, hb))
            cq = cumr_ref[h : h + 1, :]
            d00 = jnp.exp(jnp.where(tri, cq[:, 0:hb] - ck[0:hb], NEG))
            d01 = jnp.exp(cq[:, hb:] - ck[0:hb])
            d11 = jnp.exp(jnp.where(tri, cq[:, hb:] - ck[hb:], NEG))
            mine = jnp.where(lane_low if j == 0 else jnp.logical_not(lane_low), dyp, jnp.zeros_like(dyp))
            qt = dot_nt(vdt, mine)
            e00 = d00 * qt[0:hb, 0:hb]
            e01 = d01 * qt[0:hb, hb:]
            e11 = d11 * qt[hb:, hb:]
            dgt[0:hb, 0:hb] += e00
            dgt[0:hb, hb:] += e01
            dgt[hb:, hb:] += e11
            a = jnp.concatenate(
                [
                    jnp.concatenate([(g00 * d00).astype(BF16), (g01 * d01).astype(BF16)], axis=1),
                    jnp.concatenate([zeros, (g11 * d11).astype(BF16)], axis=1),
                ],
                axis=0,
            )
            z = jnp.concatenate(
                [
                    jnp.concatenate([(g00 * e00).astype(BF16), (g01 * e01).astype(BF16)], axis=1),
                    jnp.concatenate([zeros, (g11 * e11).astype(BF16)], axis=1),
                ],
                axis=0,
            )
            us.append(dot(a, dyp))
            to_k = jnp.where(lane == h, dot(z, jnp.ones((BLOCK, 128), BF16)), to_k)
            to_q = to_q + dot(jnp.where(sub == h, 1.0, 0.0).astype(BF16), z)
        u = jnp.where(lane_low, us[0], us[1])
        ec = ec_all[:, lanes]
        rem_s = spread_pair(rem, first_head // 2 + pair, lane_low)
        dye = (dyp.astype(F32) * ec).astype(BF16)
        dv = dt_s * u + taps_ref[5:6, lanes] * dyp.astype(F32) + rem_s * wds[:, lanes]
        sg = sigmoid(cp)
        buf[0:BLOCK, lanes] = dv * (sg * (1.0 + cp * (1.0 - sg)))
        dyes[:, lanes] = dye
        vrems[:, lanes] = (v * rem_s).astype(BF16)
        dstate[:, lanes] = ds[:, lanes] * ec[BLOCK - 1 : BLOCK, :]
    dstate[...] += dot(read_t, dyes[...])
    dmaps_w = dot_nt(vrems[...], ds_b)
    dmaps_r = dot_nt(dyes[...], state.astype(BF16))
    dg_b = dgt[...].astype(BF16)
    dmaps_w = dmaps_w + dot(dg_b, read)
    dmaps_r = dmaps_r + dot_tn(dg_b, write)
    if has_maps:
        dmaps_w = dmaps_w + refs[10][:, 0:n]
        dmaps_r = dmaps_r + refs[10][:, n : 2 * n]
    dmaps_ref[:, 0:n] = dmaps_w
    dmaps_ref[:, n : 2 * n] = dmaps_r

    def per_head_once(values):
        return dot(values.astype(BF16), pick[0 : values.shape[1], :])

    def per_head(values):
        high = values.astype(BF16)
        low = (values - high.astype(F32)).astype(BF16)
        return dot(jnp.concatenate([high, low], axis=1), pick[...])

    v = vacc[...]
    dy = dy_ref[...].astype(F32)
    v_wds = per_head_once(v * wds)
    dy_c = per_head_once(dy * carried)
    skip_sum = jnp.sum(dy * v, axis=0, keepdims=True)
    ss = per_head(jnp.broadcast_to(jnp.sum(ds * state, axis=0, keepdims=True), (8, width)))
    sent = rem * v_wds
    d_last = ecum[BLOCK - 1 : BLOCK, :] * ss[0:1, :] + jnp.sum(sent, axis=0, keepdims=True)
    dcum = jnp.concatenate([to_q, jnp.zeros((112, BLOCK), F32)], axis=0).T - to_k + ecum * dy_c - sent
    token = lax.broadcasted_iota(jnp.int32, (BLOCK, 128), 0)
    dcum = dcum + jnp.where(token == BLOCK - 1, d_last, 0.0)
    dlog = dot_twice(upper[...], dcum)
    rate = rate_ref[7:8, :]
    slope = pltpu.roll(steps, 64, 1)
    ratio = jnp.where(dtc > 0, slope / dtc, 1.0)
    draw = to_k * ratio + (last * v_wds + dlog * rate) * slope
    mine = jnp.logical_and(lane >= first_head, lane < first_head + width // 64)
    draw = jnp.where(mine, draw, 0.0)
    dstep = draw.astype(BF16)
    dstep_ref[...] = dstep + refs[10 + has_maps][...] if has_step else dstep
    headg_ref[0:1, :] += jnp.sum(draw, axis=0, keepdims=True)
    headg_ref[1:2, :] += jnp.sum(dlog * dtc, axis=0, keepdims=True) * rate
    headg_ref[2:3, :] += per_head(jnp.broadcast_to(skip_sum, (8, width)))[0:1, :]

    vin = vin_ref[...].astype(F32)
    total = jnp.zeros((BLOCK, width), F32)
    for j in range(4):
        shifted = buf[pl.ds(3 - j, BLOCK), :]
        total = total + taps_ref[j : j + 1, :] * shifted
        tapsg_ref[j : j + 1, :] += jnp.sum(shifted * vin, axis=0, keepdims=True)
    tapsg_ref[4:5, :] += jnp.sum(buf[0:BLOCK, :], axis=0, keepdims=True)
    dvin_ref[...] = total.astype(BF16)
    buf[pl.ds(BLOCK, 8), :] = buf[pl.ds(0, 8), :]


def split_products(normedt_ref, groups, weight, send_ref, keep_ref, pre):
    core = keep_ref.shape[0]

    def product(target, first):
        col, total = 0, 0.0
        for group in groups:
            cols = slice(col, col + group.shape[-1])
            value = dot(normedt_ref[...], group[...])
            target[:, cols] = value.astype(target.dtype)
            total = total + weighted_tiles(value, weight[first : first + core, cols])
            col = cols.stop
        pre[:, first : first + core] = along_lanes(total)

    @pl.when(pl.program_id(0) == 0)
    def _():
        product(send_ref, core)

    @pl.when(pl.program_id(0) == 1)
    def _():
        product(keep_ref, 0)


def partial_kernel(normedt_ref, *refs):
    groups, pieces = refs[:-9], refs[-9:-5]
    keep_ref, send_ref, pre_ref, weight, sems = refs[-5:]

    @pl.when(pl.program_id(0) == 0)
    def _():
        for copy in load_rows(pieces, weight, sems):
            copy.wait()

    split_products(normedt_ref, groups, weight, send_ref, keep_ref, pre_ref)


def late_kernel(normedt_ref, dmaps_ref, statein_ref, statec_ref, taps_ref, pm_ref, shared_ref, gain_ref, pre0_ref, pre1_ref, *refs):
    count = HALVES * SEGMENTS
    tap_refs, head_refs = refs[:count], refs[count : 2 * count]
    groups, pieces = refs[2 * count : -16], refs[-16:-8]
    keep_ref, send_ref, dstate_ref, sums_ref, buf, weight, pre, sems = refs[-8:]
    length, n2 = statein_ref.shape
    width = weight.shape[0]
    seg_w = tap_refs[0].shape[1]
    step = pl.program_id(0)

    @pl.when(step == 0)
    def _():
        columns = weight.shape[1] - n2
        copies = load_rows(pieces[:4], weight.at[:, pl.ds(0, columns)], sems)
        copies += load_rows(pieces[4:], weight.at[:, pl.ds(columns, n2)], sems, 4)
        sums_ref[...] = jnp.zeros(sums_ref.shape, F32)
        for half, first in enumerate((16, 0)):
            mine = range(half * SEGMENTS, (half + 1) * SEGMENTS)
            for i, segment in enumerate(mine):
                sums_ref[first : first + 5, i * seg_w : (i + 1) * seg_w] = tap_refs[segment][0:5, :]
            sums_ref[first + 5 : first + 6, :] = gain_ref[half : half + 1, :]
            head = sum((head_refs[segment][...] for segment in mine[1:]), head_refs[mine[0]][...])
            for i in range(3):
                sums_ref[first + 6 : first + 7, i * PAD : (i + 1) * PAD] = head[i : i + 1, :]
        c = statec_ref[...]
        sg = sigmoid(c)
        dc = dmaps_ref[...] * (sg * (1.0 + c * (1.0 - sg)))
        buf[0:length, :] = dc
        buf[pl.ds(length, 8), :] = jnp.zeros((8, n2), F32)
        state_in = statein_ref[...]
        total = jnp.zeros((length, n2), F32)
        for j in range(4):
            shifted = buf[pl.ds(3 - j, length), :]
            total = total + taps_ref[j : j + 1, :] * shifted
            sums_ref[8 + j : 9 + j, 0:n2] = jnp.sum(shifted * state_in, axis=0, keepdims=True)
        sums_ref[12:13, 0:n2] = jnp.sum(dc, axis=0, keepdims=True)
        dstate_ref[...] = total.astype(BF16)
        for copy in copies:
            copy.wait()

    split_products(normedt_ref, groups + (dstate_ref,), weight, send_ref, keep_ref, pre)

    @pl.when(step == 1)
    def _():
        high, mid, low = split3(pre[...] + pre0_ref[...] + pre1_ref[...])
        total = dot_nt(high, pm_ref[...]) + dot_nt(mid, pm_ref[...]) + dot_nt(low, pm_ref[...])
        sums_ref[13:14, :] = total[0:1, :] / shared_ref[0:1, :]


def turn_value_kernel(*refs):
    pmt_ref, pieces = refs[0], refs[1:-7]
    tv_ref, to_ref, ts_ref, wv, wo, ws, sems = refs[-7:]
    copies = load_rows(pieces[:4], wv, sems) + load_rows(pieces[4:8], wo, sems, 4) + load_rows(pieces[8:], ws, sems, 8)
    for copy in copies:
        copy.wait()
    tv_ref[...] = dot_tn(wv[...], pmt_ref[...]).astype(BF16)
    to_ref[...] = dot_tn(wo[...], pmt_ref[...]).astype(BF16)
    ts_ref[...] = dot_tn(ws[...], pmt_ref[...]).astype(BF16)


def turn_gate_kernel(*refs):
    pmt_ref, pieces = refs[0], refs[1:-3]
    tg_ref, wg, sems = refs[-3:]
    for copy in load_halves(pieces, wg, sems, 0, pl.ds(0, wg.shape[2])):
        copy.wait()
    for half in range(HALVES):
        tg_ref[half] = dot_tn(wg[half], pmt_ref[...]).astype(BF16)


def input_kernel(*refs):
    x_ref, cot_ref, shared_ref, dgate_ref, dstate_ref, tg_ref, tv_ref, to_ref, ts_ref = refs[:9]
    count = HALVES * SEGMENTS
    dvin_refs, dstep_refs = refs[9 : 9 + count], refs[9 + count : 9 + count + HALVES]
    grad_ref = refs[-1]
    width = x_ref.shape[2]
    total = dot(dstate_ref[...], ts_ref[...])
    for half, weights in enumerate((tv_ref, to_ref)):
        total = total + dot(dgate_ref[half], tg_ref[half]) + dot(dstep_refs[half][...], weights[width:, :])
        for segment in range(SEGMENTS):
            dvin = dvin_refs[half * SEGMENTS + segment][...]
            cols = dvin.shape[1]
            total = total + dot(dvin, weights[segment * cols : segment * cols + cols, :])
    x = x_ref[0].astype(F32)
    inv = lax.rsqrt(jnp.mean(x * x, axis=-1, keepdims=True) + EPS)
    scaled = total * shared_ref[0:1, :]
    inner = jnp.mean(scaled * x, axis=-1, keepdims=True)
    grad_ref[0] = cot_ref[0].astype(F32) + inv * scaled - x * (inv * inv * inv * inner)


def early_end_kernel(keep_ref, *refs):
    gate_ref, out_ref = refs[-2:]
    rows, width = gate_ref.shape
    total = keep_ref[0:rows, :]
    for ref in refs[:-2]:
        total = total + ref[...].astype(F32)
    gate_ref[...] = total[:, 0:width]
    out_ref[...] = total[:, width:]


def late_end_kernel(keep_ref, *refs):
    value_ref, step_ref, state_ref = refs[-3:]
    rows, width = value_ref.shape
    total = keep_ref[0:rows, :]
    for ref in refs[:-3]:
        total = total + ref[...].astype(F32)
    value_ref[...] = total[:, 0:width]
    step_ref[...] = total[:, width : width + PAD].T[0 : step_ref.shape[0], :]
    state_ref[...] = total[:, width + PAD :]


def sums_end_kernel(
    sums_ref, got_ref,
    prenorm_ref, taps_ref, shift_ref, staps_ref, sshift_ref, bias_ref, decay_ref, skip_ref, gain_ref,
):
    total = sums_ref[...] + got_ref[...]
    n2 = sshift_ref.shape[0]
    heads = bias_ref.shape[0]
    taps_ref[...] = total[0:4, :]
    shift_ref[...] = total[4, :]
    gain_ref[...] = total[5, :]
    bias_ref[...] = total[6, 0:PAD][0:heads]
    decay_ref[...] = total[6, PAD : 2 * PAD][0:heads]
    skip_ref[...] = total[6, 2 * PAD : 3 * PAD][0:heads]
    staps_ref[...] = total[8:12, 0:n2]
    sshift_ref[...] = total[12, 0:n2]
    prenorm_ref[...] = total[13, :]


def call(body, grid, in_specs, out_specs, out_shape, scratch=(), flops=0, vmem=24, aliases={}):
    return pl.pallas_call(
        body,
        grid=grid,
        in_specs=in_specs,
        out_specs=out_specs,
        out_shape=out_shape,
        scratch_shapes=list(scratch),
        input_output_aliases=aliases,
        compiler_params=pltpu.CompilerParams(
            vmem_limit_bytes=vmem * MIB, dimension_semantics=("arbitrary",) * len(grid)
        ),
        cost_estimate=pl.CostEstimate(flops=flops, bytes_accessed=10_000_000, transcendentals=0),
    )


def shape(dims, dtype=F32):
    return jax.ShapeDtypeStruct(dims, dtype)


def hbm(v):
    return pltpu.with_memory_space_constraint(v, pltpu.HBM)


def fixed(dims, *index):
    return pl.BlockSpec(dims, lambda *_: index)


ANYWHERE = pl.BlockSpec(memory_space=pl.ANY)
AXES = ("dp", "tensor")
TENSOR, CORE, CHIP = 1, 2, 4
FAR = 3


def swap(v, mask):
    count = lax.axis_size("dp") * lax.axis_size("tensor")
    return lax.ppermute(v, AXES, [(i, i ^ mask) for i in range(count)])


def far_masks():
    count = lax.axis_size("dp") * lax.axis_size("tensor")
    return [m << FAR for m in range(1, count >> FAR)]


def start_near(pack):
    return [pack] + [swap(pack, m) for m in far_masks()]


def start_far(v, rows):
    return [swap(v[(i + 1) * rows : (i + 2) * rows].astype(BF16), m) for i, m in enumerate(far_masks())]


def wide(*parts):
    return sum((part.astype(F32) for part in parts[1:]), parts[0].astype(F32))


def meet(*values):
    return lax.optimization_barrier(values)


def after(v, *others):
    return lax.optimization_barrier((v,) + others)[0]


def local(
    inputs,
    prenorm,
    gate_weight,
    value_weight,
    state_weight,
    step_weight,
    value_conv,
    value_shift,
    state_conv,
    state_shift,
    step_shift,
    decay_log,
    skip_scale,
    gated_gain,
    output_matrix,
    cotangent,
):
    length, width = inputs.shape[1:]
    rows, w = gate_weight.shape
    heads = step_weight.shape[1]
    n = state_weight.shape[1] // 2
    n2 = 2 * n
    blocks = length // BLOCK
    quarter = width // 4
    wp = w + PAD
    whole = lambda v: fixed(v.shape, *([0] * v.ndim))
    row_block = lambda dims: pl.BlockSpec(dims, lambda b: (b, 0))
    col_block = lambda dims: pl.BlockSpec(dims, lambda b: (0, b))
    tokens = pl.BlockSpec((1, BLOCK, width), lambda b: (0, b, 0))
    halves = lambda last: pl.BlockSpec((HALVES, BLOCK, last), lambda b: (0, b, 0))
    square = fixed((width, width), 0, 0)
    small_spec = fixed((8, w), 0, 0)
    sems = lambda count: pltpu.SemaphoreType.DMA((count,))

    to_pack = (
        value_conv, value_shift, skip_scale, gated_gain, step_shift, decay_log, prenorm, state_shift,
        gate_weight, value_weight, step_weight.T, output_matrix.T,
    )
    small, shared, vpack, gpack = call(
        pack_kernel,
        (1,),
        [whole(v) for v in to_pack],
        [small_spec, fixed((8, width), 0, 0), fixed((rows, wp), 0, 0), fixed((rows, 2 * w), 0, 0)],
        [shape((8, w)), shape((8, width)), shape((rows, wp), BF16), shape((rows, 2 * w), BF16)],
        flops=1_000_000,
    )(*(hbm(v) for v in to_pack))

    spot = jnp.arange(width)
    owner = lax.axis_index("dp") ^ (
        spot // (2 * quarter) + 2 * (spot // quarter % 2) + 4 * (spot % quarter // rows)
    )
    natural = owner * rows + spot % rows
    pm = (spot[:, None] == natural[None, :]).astype(BF16)
    pmt = (natural[:, None] == spot[None, :]).astype(BF16)

    near = jnp.concatenate(start_near(state_weight), axis=0)
    chip = swap(near, CHIP)
    chip, *value_near = meet(chip, *start_near(vpack))
    state_own = (near, chip, swap(near, CORE), swap(chip, CORE))
    value_near = jnp.concatenate(value_near, axis=0)
    value_chip, value_y = swap(value_near, CHIP), swap(value_near, TENSOR)
    gate_near = start_near(after(gpack, near))
    small_got = swap(small, TENSOR)

    normed, normed_t, state_in, state_c, maps, maps_t = call(
        maps_kernel,
        (blocks,),
        [tokens, square] + [ANYWHERE] * 4 + [fixed((4, n2), 0, 0), fixed((8, width), 0, 0)],
        [row_block((BLOCK, width)), col_block((width, BLOCK)), row_block((BLOCK, n2)), row_block((BLOCK, n2)),
         row_block((BLOCK, n2)), col_block((n2, BLOCK))],
        [shape((length, width), BF16), shape((width, length), BF16), shape((length, n2)), shape((length, n2)),
         shape((length, n2), BF16), shape((n2, length), BF16)],
        [pltpu.VMEM((BLOCK + 8, n2), F32), pltpu.VMEM((width, n2), BF16), sems(4)],
        flops=6_000_000_000,
    )(inputs, pm, *state_own, state_conv, shared)

    def forward(pieces, half, normed):
        return call(
            forward_kernel,
            (blocks,),
            [ANYWHERE] * len(pieces)
            + [row_block((BLOCK, width)), small_spec, row_block((BLOCK, n2)), col_block((n2, BLOCK))],
            [row_block((BLOCK, w))] * 3 + [pl.BlockSpec((1, n, w), lambda b: (b, 0, 0))]
            + [row_block((BLOCK, PAD)), col_block((16, BLOCK))],
            [pltpu.HBM((length, w), BF16), pltpu.HBM((length, w), BF16), shape((length, w), BF16),
             pltpu.HBM((blocks, n, w), F32), pltpu.HBM((length, PAD), F32), pltpu.HBM((16, length), F32)],
            [pltpu.VMEM((BLOCK + 8, w), F32), pltpu.VMEM((n, w), F32), pltpu.VMEM((width, wp), BF16),
             pltpu.VMEM((2 * PAD, w), BF16), sems(4)],
            flops=12_000_000_000,
        )(*pieces, normed, smalls[half], maps, maps_t)

    normed, value_chip, value_y, small_got, *gate_near = meet(normed, value_chip, value_y, small_got, *gate_near)
    smalls = (small, small_got)
    value_own = (value_near, value_chip, swap(value_near, CORE), swap(value_chip, CORE))
    value_yx = swap(value_chip, TENSOR)
    gate_near = jnp.concatenate(gate_near, axis=0)
    gate_y, gate_x = swap(gate_near[:, :w], TENSOR), swap(gate_near, CHIP)
    out_y = swap(gate_near[:, w:], TENSOR)
    scan_own = forward(value_own, 0, after(normed, gate_near))
    normed, value_y, value_yx, gate_x, gate_y, _ = meet(normed, value_y, value_yx, gate_x, gate_y, scan_own[2])
    gate_yx, out_yx = swap(gate_y, CHIP), swap(gate_x[:, w:], TENSOR)
    value_other = (value_y, value_yx, swap(value_y, CORE), swap(value_yx, CORE))
    scan_other = forward(value_other, 1, normed)
    scans = (scan_own, scan_other)

    both_w = (HALVES, width, w)
    out_y, gate_yx, out_yx, _ = meet(out_y, gate_yx, out_yx, scan_other[2])
    far = jnp.concatenate([jnp.concatenate([gate_y, out_y], axis=1), jnp.concatenate([gate_yx, out_yx], axis=1)], axis=0)
    gate_pieces = (gate_near, gate_x, far)
    gate_pieces += tuple(swap(v, CORE) for v in gate_pieces)
    given = (after(pmt, far), *value_own, *value_other, *state_own)
    turned = call(
        turn_value_kernel,
        (1,),
        [square] + [ANYWHERE] * 12,
        [fixed((wp, width), 0, 0), fixed((wp, width), 0, 0), fixed((n2, width), 0, 0)],
        [shape((wp, width), BF16), shape((wp, width), BF16), shape((n2, width), BF16)],
        [pltpu.VMEM((width, wp), BF16), pltpu.VMEM((width, wp), BF16), pltpu.VMEM((width, n2), BF16), sems(12)],
        flops=4_000_000_000,
    )(*given)
    half_rows = (HALVES, width // 2, 2 * w)
    turned = list(turned)
    turned[0], *gate_pieces = meet(turned[0], *gate_pieces)
    result, dy0, dy1, dgate, early_send, early_keep, gain_partial, gate_pre = call(
        gated_kernel,
        (blocks,),
        [tokens, tokens, row_block((BLOCK, width)), col_block((width, BLOCK)), row_block((BLOCK, w)),
         row_block((BLOCK, w)), small_spec, small_spec, square] + [ANYWHERE] * 6,
        [tokens, row_block((BLOCK, w)), row_block((BLOCK, w)), halves(w), fixed(half_rows, 0, 0, 0),
         fixed(half_rows, 0, 0, 0), fixed((HALVES, w), 0, 0), fixed((8, width), 0, 0)],
        [shape(inputs.shape, BF16), shape((length, w), BF16), shape((length, w), BF16),
         shape((HALVES, length, w), BF16), shape(half_rows, BF16), shape(half_rows), shape((HALVES, w)),
         shape((8, width))],
        [pltpu.VMEM(both_w, BF16), pltpu.VMEM(both_w, BF16), pltpu.VMEM(both_w, BF16), pltpu.VMEM(half_rows, F32),
         sems(16)],
        flops=25_000_000_000,
        vmem=48,
    )(inputs, cotangent, normed, normed_t, scans[0][2], scans[1][2], *smalls, pmt, *gate_pieces)

    seg_w = w // SEGMENTS
    seg_heads = heads // SEGMENTS

    def backward(half, segment, dy, dmaps=None, dstep=None):
        back = lambda dims, col=0: pl.BlockSpec(dims, lambda b: (blocks - 1 - b, col))
        value_in, value_c, _, states, steps, cumr = scans[half]
        extra = ([dmaps] if dmaps is not None else []) + ([dstep] if dstep is not None else [])
        return call(
            functools.partial(backward_kernel, segment * seg_heads, dmaps is not None, dstep is not None),
            (blocks,),
            [back((BLOCK, seg_w), segment)] * 3
            + [pl.BlockSpec((1, n, seg_w), lambda b: (blocks - 1 - b, 0, segment)), back((BLOCK, n2)),
               pl.BlockSpec((n2, BLOCK), lambda b: (0, blocks - 1 - b))] + [back((BLOCK, PAD))]
            + [pl.BlockSpec((16, BLOCK), lambda b: (0, blocks - 1 - b)), fixed((8, seg_w), 0, segment),
               fixed((8, PAD), 0, 1)] + [back((BLOCK, v.shape[1])) for v in extra],
            [back((BLOCK, seg_w)), back((BLOCK, n2)), back((BLOCK, PAD)), fixed((8, seg_w), 0, 0), fixed((8, PAD), 0, 0)],
            [shape((length, seg_w), BF16), shape((length, n2)), shape((length, PAD), BF16), shape((8, seg_w)),
             shape((8, PAD))],
            [pltpu.VMEM((BLOCK + 8, seg_w), F32), pltpu.VMEM((n, seg_w), F32), pltpu.VMEM((BLOCK, BLOCK), F32),
             pltpu.VMEM((BLOCK, seg_w), F32), pltpu.VMEM((BLOCK, seg_w), BF16),
             pltpu.VMEM((BLOCK, seg_w), BF16), pltpu.VMEM((2 * seg_w, PAD), BF16), pltpu.VMEM((BLOCK, BLOCK), BF16),
             pltpu.VMEM((2 * PAD, seg_w), BF16)],
            flops=12_000_000_000,
        )(hbm(value_c), hbm(value_in), dy, hbm(states), maps, maps_t, hbm(steps), hbm(cumr), smalls[half], smalls[half],
          *extra)

    core = width // 2
    lead = pl.BlockSpec((core, length), lambda b: (1 - b, 0))
    split_specs = lambda cols: [fixed((core, cols), 0, 0)] * 2
    split_shapes = lambda cols: [shape((core, cols)), shape((core, cols), BF16)]

    early_got = swap(early_send, CORE)
    other0 = backward(1, 0, dy1)
    early_keep, early_got, _ = meet(early_keep, early_got, other0[2])
    gate = wide(early_keep[:, :, :w], early_got[:, :, :w])
    out = wide(early_keep[:, :, w:], early_got[:, :, w:])
    gate_out, gate = gate[1].astype(BF16), gate[0]
    out_out, out = out[:, quarter:].astype(BF16), out[:, :quarter]
    gate_got, out_got = swap(gate_out, TENSOR), swap(out_out, CHIP)
    other1 = backward(1, 1, after(dy1, gate_out, gate, out_out, out), other0[1], other0[2])
    gate, out, gate_got, out_got, _ = meet(gate, out, gate_got, out_got, other1[2])
    gate, out = wide(gate, gate_got), wide(out, out_got)
    gate_out, gate = gate[quarter:].astype(BF16), gate[:quarter]
    out_out, out = out[1].astype(BF16), out[0]
    gate_got, out_got = swap(gate_out, CHIP), swap(out_out, TENSOR)
    groups = (other0[0], other1[0], after(other1[2], gate_out, gate, out_out, out))
    other_keep, other_send, other_pre = call(
        partial_kernel,
        (2,),
        [lead] + [whole(v) for v in groups] + [ANYWHERE] * 4,
        split_specs(wp) + [fixed((8, width), 0, 0)],
        split_shapes(wp) + [shape((8, width))],
        [pltpu.VMEM((width, wp), BF16), sems(4)],
        flops=3_000_000_000,
    )(normed_t, *groups, *value_other)
    other_got = swap(other_send, CORE)
    own0 = backward(0, 0, after(dy0, other_send), other1[1])
    gate, out, gate_got, out_got, other_keep, other_got, _ = meet(
        gate, out, gate_got, out_got, other_keep, other_got, own0[2]
    )
    other_out = wide(other_keep, other_got).astype(BF16)
    other_got = swap(other_out, TENSOR)
    early = jnp.concatenate([wide(gate, gate_got), wide(out, out_got)], axis=1)
    early_far = start_far(early, rows)
    own1 = backward(0, 1, after(dy0, other_out, early), own0[1], own0[2])

    def end(body, given, dims):
        return call(
            body, (1,), [whole(v) for v in given], [fixed(d, *([0] * len(d))) for d in dims], [shape(d) for d in dims],
            flops=1_000_000,
        )(*given)

    dmaps, other_got, early, *early_far = meet(own1[1], other_got, early, *early_far)
    gate_grad, out_grad = end(early_end_kernel, (early, *early_far), ((rows, w), (rows, w)))
    groups = (own0[0], own1[0], own1[2])
    parts = (own0, own1, other0, other1)
    given = (
        (dmaps, state_in, state_c, state_conv, pm, shared, gain_partial, gate_pre, other_pre)
        + tuple(part[3] for part in parts) + tuple(part[4] for part in parts) + groups
    )
    late_keep, late_send, dstate, sums = call(
        late_kernel,
        (2,),
        [lead] + [whole(v) for v in given] + [ANYWHERE] * 8,
        split_specs(wp + n2) + [fixed((length, n2), 0, 0), fixed((24, width), 0, 0)],
        split_shapes(wp + n2) + [shape((length, n2), BF16), shape((24, width))],
        [pltpu.VMEM((length + 8, n2), F32), pltpu.VMEM((width, wp + n2), BF16), pltpu.VMEM((8, width), F32), sems(8)],
        flops=4_000_000_000,
    )(normed_t, *given, *value_own, *state_own)
    late_got, sums_got = swap(late_send, CORE), swap(sums[:16], TENSOR)
    turned_gate = call(
        turn_gate_kernel,
        (1,),
        [square] + [ANYWHERE] * 6,
        [fixed(both_w, 0, 0, 0)],
        [shape(both_w, BF16)],
        [pltpu.VMEM(both_w, BF16), sems(16)],
        flops=2_000_000_000,
    )(after(pmt, late_send), *gate_pieces)[0]
    late_keep, late_got, other_got, sums, sums_got, turned_gate = meet(
        late_keep, late_got, other_got, sums, sums_got, turned_gate
    )
    late = wide(late_keep, late_got)
    late = jnp.concatenate([late[:, :wp] + other_got.astype(F32), late[:, wp:]], axis=1)
    late_out, late = late[quarter:].astype(BF16), late[:quarter]
    late_got = swap(late_out, CHIP)
    sums = jnp.concatenate([sums[16:] + sums_got[:8], sums[8:16] + sums_got[8:]], axis=0)
    sums_got = swap(sums, CORE)

    def input_part(dgate, first, grad=None):
        token = pl.BlockSpec((1, BLOCK, width), lambda b: (0, b + first, 0))
        tall = lambda cols: pl.BlockSpec((BLOCK, cols), lambda b: (b + first, 0))
        given = (
            (inputs, cotangent, shared, dgate, dstate, turned_gate, *turned)
            + tuple(part[0] for part in parts) + (own1[2], other1[2])
        )
        return call(
            input_kernel,
            (blocks // 2,),
            [token, token, fixed((8, width), 0, 0), pl.BlockSpec((HALVES, BLOCK, w), lambda b: (0, b + first, 0)), tall(n2),
             fixed(both_w, 0, 0, 0)] + [whole(v) for v in turned] + [tall(seg_w)] * len(parts) + [tall(PAD)] * HALVES
            + ([] if grad is None else [ANYWHERE]),
            [token],
            [shape(inputs.shape)],
            flops=6_000_000_000,
            aliases={} if grad is None else {len(given): 0},
        )(*given, *(() if grad is None else (grad,)))[0]

    input_grad = input_part(after(dgate, late_out, late, sums), 0)
    sums, sums_got, input_grad = meet(sums, sums_got, input_grad)
    sums = sums + sums_got
    bits = [1 << FAR]
    while 2 * bits[-1] < lax.axis_size("dp") * lax.axis_size("tensor"):
        bits.append(2 * bits[-1])
    bits.append(CHIP)
    sums_got = swap(sums, bits[0])
    late, sums, sums_got, late_got = meet(late, sums, sums_got, late_got)
    late = wide(late, late_got)
    late_far = start_far(late, rows)
    sums = sums + sums_got
    sums_got = swap(sums, bits[1])
    input_grad = input_part(after(dgate, late, sums), blocks // 2, input_grad)
    sums, sums_got, input_grad = meet(sums, sums_got, input_grad)
    for bit in bits[2:]:
        sums = sums + sums_got
        sums_got = swap(sums, bit)

    value_grad, step_grad, state_grad = end(
        late_end_kernel, (late, *late_far), ((rows, w), (heads, rows), (rows, n2))
    )
    state_grad = state_grad + swap(state_grad, TENSOR)
    prenorm_grad, taps, shift, state_taps, state_bias, bias, decay, skip, gain = end(
        sums_end_kernel,
        (sums, sums_got),
        ((width,), (4, w), (w,), (4, n2), (n2,), (heads,), (heads,), (heads,), (w,)),
    )
    return (
        result, input_grad, prenorm_grad, gate_grad, value_grad, state_grad, step_grad.T, taps, shift, state_taps,
        state_bias, bias, decay, skip, gain, out_grad.T,
    )


def solution(mesh):
    in_specs = (
        P(("dp", "tensor"), None, None),
        P(),
        P("dp", "tensor"),
        P("dp", "tensor"),
        P("dp", None),
        P("dp", "tensor"),
        P(None, "tensor"),
        P("tensor"),
        P(),
        P(),
        P("tensor"),
        P("tensor"),
        P("tensor"),
        P("tensor"),
        P("tensor", "dp"),
        P(("dp", "tensor"), None, None),
    )
    out_specs = (
        P(("dp", "tensor"), None, None),
        P(("dp", "tensor"), None, None),
        P(),
        P("dp", "tensor"),
        P("dp", "tensor"),
        P("dp", None),
        P("dp", "tensor"),
        P(None, "tensor"),
        P("tensor"),
        P(),
        P(),
        P("tensor"),
        P("tensor"),
        P("tensor"),
        P("tensor"),
        P("tensor", "dp"),
    )
    return jax.shard_map(local, mesh=mesh, in_specs=in_specs, out_specs=out_specs, check_vma=False)
```

```python
import functools

import jax
import jax.numpy as jnp
from jax import lax
from jax.experimental import pallas as pl
from jax.experimental.pallas import tpu as pltpu
from jax.sharding import PartitionSpec as P

BLOCK = 256
HALVES = 2
PAD = 128
SEGMENTS = 2
EPS = 1e-05
NEG = -1e30
F32 = jnp.float32
BF16 = jnp.bfloat16
MIB = 1024 * 1024


def dot(a, b):
    return jnp.dot(a, b, preferred_element_type=F32)


def dot_nt(a, b):
    return lax.dot_general(a, b, (((1,), (1,)), ((), ())), preferred_element_type=F32)


def dot_tn(a, b):
    return lax.dot_general(a, b, (((0,), (0,)), ((), ())), preferred_element_type=F32)


def split3(v):
    high = v.astype(BF16)
    rest = v - high.astype(F32)
    mid = rest.astype(BF16)
    low = (rest - mid.astype(F32)).astype(BF16)
    return high, mid, low


def dot_twice(mask, v):
    high = v.astype(BF16)
    return dot(mask, high) + dot(mask, (v - high.astype(F32)).astype(BF16))


def dot_exact(mask, v):
    high, mid, low = split3(v)
    return dot(mask, high) + dot(mask, mid) + dot(mask, low)


def sigmoid(v):
    return 0.5 * jnp.tanh(0.5 * v) + 0.5


def spread_pair(cols, pair, lane_low):
    rows = cols.shape[0]
    left = jnp.broadcast_to(cols[:, 2 * pair : 2 * pair + 1], (rows, 128))
    right = jnp.broadcast_to(cols[:, 2 * pair + 1 : 2 * pair + 2], (rows, 128))
    return jnp.where(lane_low, left, right)


def fill_spread(mask, first_head):
    row = lax.broadcasted_iota(jnp.int32, mask.shape, 0)
    col = lax.broadcasted_iota(jnp.int32, mask.shape, 1)
    mask[...] = jnp.where(row % PAD == first_head + col // 64, 1.0, 0.0).astype(BF16)


def spread(cols, mask):
    high = cols.astype(BF16)
    low = (cols - high.astype(F32)).astype(BF16)
    return dot(jnp.concatenate([high, low], axis=1), mask[...])


def conv_taps(buf, taps_ref, shift, first, rows):
    total = shift + taps_ref[0:1, :] * buf[pl.ds(first, rows), :]
    for j in range(1, 4):
        total = total + taps_ref[j : j + 1, :] * buf[pl.ds(first + j, rows), :]
    return total


def pack_kernel(
    taps_ref, shift_ref, skip_ref, gain_ref, bias_ref, decay_ref, prenorm_ref, sshift_ref,
    gate_ref, value_ref, stept_ref, outt_ref,
    small_ref, shared_ref, vpack_ref, gpack_ref,
):
    rows, width = gate_ref.shape
    heads = stept_ref.shape[0]
    n2 = sshift_ref.shape[0]
    gpack_ref[:, 0:width] = gate_ref[...]
    gpack_ref[:, width:] = outt_ref[...]
    vpack_ref[:, 0:width] = value_ref[...]
    vpack_ref[:, width:] = jnp.zeros((rows, PAD), BF16)
    vpack_ref[:, width : width + heads] = stept_ref[...].astype(F32).T.astype(BF16)
    small_ref[...] = jnp.zeros(small_ref.shape, F32)
    shared_ref[...] = jnp.zeros(shared_ref.shape, F32)
    small_ref[0:4, :] = taps_ref[...]
    small_ref[4, :] = shift_ref[...]
    head = lax.broadcasted_iota(jnp.int32, (1, width), 1) // (width // heads)
    skip_row = skip_ref[...].reshape(1, heads)
    skip = jnp.zeros((1, width), F32)
    for h in range(heads):
        skip = jnp.where(head == h, skip_row[:, h : h + 1], skip)
    small_ref[5:6, :] = skip
    small_ref[6, :] = gain_ref[...]
    small_ref[7:8, 0:heads] = bias_ref[...].reshape(1, heads)
    small_ref[7:8, PAD : PAD + heads] = -jnp.exp(decay_ref[...].reshape(1, heads))
    shared_ref[0, :] = prenorm_ref[...]
    shared_ref[1:2, 0:n2] = sshift_ref[...].reshape(1, n2)


def load_rows(pieces, target, sems, first=0, lanes=None, start=True):
    copies = []
    for i, piece in enumerate(pieces):
        rows = piece.shape[0]
        source = piece if lanes is None else piece.at[:, lanes]
        copies.append(pltpu.make_async_copy(source, target.at[pl.ds(i * rows, rows), :], sems.at[first + i]))
    for copy in copies if start else ():
        copy.start()
    return copies


def load_halves(pieces, target, sems, first, lanes, start=True):
    near0, x0, far0, near1, x1, far1 = pieces
    copies = load_rows((near0, x0, near1, x1), target.at[0], sems, first, lanes, start)
    return copies + load_rows((far0, far1), target.at[1], sems, first + 4, lanes, start)


def weighted_tiles(grad, weight):
    product = grad * weight.astype(F32)
    return sum((product[:, col : col + 128] for col in range(128, product.shape[1], 128)), product[:, 0:128])


def along_lanes(tiles):
    ones = jnp.ones((8, tiles.shape[1]), BF16)
    high = tiles.astype(BF16)
    return dot_nt(ones, high) + dot_nt(ones, (tiles - high.astype(F32)).astype(BF16))


def maps_kernel(
    x_ref, pm_ref, piece0, piece1, piece2, piece3, taps_ref, shared_ref,
    normed_ref, normedt_ref, statein_ref, statec_ref, maps_ref, mapst_ref,
    buf, ws, sems,
):
    step = pl.program_id(0)
    n2 = buf.shape[1]

    @pl.when(step == 0)
    def _():
        lanes = pl.ds(piece0.shape[1] - n2, n2)
        copies = load_rows((piece0, piece1, piece2, piece3), ws, sems, 0, lanes)
        buf[pl.ds(0, 8), :] = jnp.zeros((8, n2), F32)
        for copy in copies:
            copy.wait()

    x = x_ref[0].astype(F32)
    inv = lax.rsqrt(jnp.mean(x * x, axis=-1, keepdims=True) + EPS)
    normed = (x * inv * shared_ref[0:1, :]).astype(BF16)
    normed = dot(normed, pm_ref[...])
    normedt_ref[...] = normed.T.astype(BF16)
    normed = normed.astype(BF16)
    normed_ref[...] = normed
    state_in = dot(normed, ws[...])
    statein_ref[...] = state_in
    buf[pl.ds(8, BLOCK), :] = state_in
    c = conv_taps(buf, taps_ref, shared_ref[1:2, 0:n2], 5, BLOCK)
    buf[pl.ds(0, 8), :] = buf[pl.ds(BLOCK, 8), :]
    statec_ref[...] = c
    maps = c * sigmoid(c)
    maps_ref[...] = maps.astype(BF16)
    mapst_ref[...] = maps.T.astype(BF16)


def forward_kernel(*refs):
    pieces = refs[:-15]
    normed_ref, small_ref, maps_ref, mapst_ref = refs[-15:-11]
    vin_ref, c_ref, y_ref, state_ref, steps_ref, cumr_ref, buf, state, wv, mask, sems = refs[-11:]
    step = pl.program_id(0)
    width = buf.shape[1]
    n = state.shape[0]

    @pl.when(step == 0)
    def _():
        copies = load_rows(pieces, wv, sems, 0, pl.ds(0, width + PAD))
        buf[pl.ds(0, 8), :] = jnp.zeros((8, width), F32)
        state[...] = jnp.zeros(state.shape, F32)
        fill_spread(mask, 0)
        for copy in copies:
            copy.wait()

    raw = dot(normed_ref[...], wv[:, width:]) + small_ref[7:8, 0:PAD]
    soft = jnp.exp(-jnp.abs(raw))
    dtc = jnp.maximum(raw, 0.0) + jnp.log1p(soft)
    slope = jnp.where(raw >= 0, 1.0, soft) / (1.0 + soft)
    row = lax.broadcasted_iota(jnp.int32, (BLOCK, BLOCK), 0)
    col = lax.broadcasted_iota(jnp.int32, (BLOCK, BLOCK), 1)
    lower = jnp.where(row >= col, 1.0, 0.0).astype(BF16)
    cumc = dot_exact(lower, dtc * small_ref[7:8, PAD : 2 * PAD])
    lane = lax.broadcasted_iota(jnp.int32, (BLOCK, PAD), 1)
    steps_ref[...] = jnp.where(
        lane < 32, cumc, jnp.where(lane < 64, pltpu.roll(dtc, 32, 1), pltpu.roll(slope, 64, 1))
    )
    cumr = cumc.T[0:16, :]
    cumr_ref[...] = cumr
    value_in = dot(normed_ref[...], wv[:, 0:width])
    vin_ref[...] = value_in.astype(BF16)
    buf[pl.ds(8, BLOCK), :] = value_in
    c = conv_taps(buf, small_ref, small_ref[4:5, :], 5, BLOCK)
    buf[pl.ds(0, 8), :] = buf[pl.ds(BLOCK, 8), :]
    c_ref[...] = c
    state_ref[0] = state[...]
    write = maps_ref[:, 0:n]
    read = maps_ref[:, n : 2 * n]
    write_t = mapst_ref[0:n, :]
    grams = dot_nt(read, write)
    carried = dot(read, state[...].astype(BF16))
    ec_all = spread(jnp.exp(cumc), mask)
    rem_all = spread(jnp.exp(cumc[BLOCK - 1 : BLOCK, :] - cumc) * dtc, mask)
    dt_all = spread(dtc, mask)
    lane_low = lax.broadcasted_iota(jnp.int32, (BLOCK, 128), 1) < 64
    hb = BLOCK // 2
    tri = lax.broadcasted_iota(jnp.int32, (hb, hb), 0) >= lax.broadcasted_iota(jnp.int32, (hb, hb), 1)
    zeros = jnp.zeros((hb, hb), BF16)
    g00 = grams[0:hb, 0:hb]
    g10 = grams[hb:, 0:hb]
    g11 = grams[hb:, hb:]
    for pair in range(width // 128):
        lanes = slice(pair * 128, pair * 128 + 128)
        cp = c[:, lanes]
        v = cp * sigmoid(cp)
        vdt = (v * dt_all[:, lanes]).astype(BF16)
        outs = []
        for j in range(2):
            h = 2 * pair + j
            cq = jnp.broadcast_to(cumc[:, h : h + 1], (BLOCK, hb))
            ck = cumr[h : h + 1, :]
            d00 = jnp.exp(jnp.where(tri, cq[0:hb] - ck[:, 0:hb], NEG))
            d10 = jnp.exp(cq[hb:] - ck[:, 0:hb])
            d11 = jnp.exp(jnp.where(tri, cq[hb:] - ck[:, hb:], NEG))
            top = jnp.concatenate([(g00 * d00).astype(BF16), zeros], axis=1)
            bot = jnp.concatenate([(g10 * d10).astype(BF16), (g11 * d11).astype(BF16)], axis=1)
            outs.append(dot(jnp.concatenate([top, bot], axis=0), vdt))
        ec = ec_all[:, lanes]
        y = jnp.where(lane_low, outs[0], outs[1]) + ec * carried[:, lanes] + small_ref[5:6, lanes] * v
        y_ref[:, lanes] = y
        vrem = (v * rem_all[:, lanes]).astype(BF16)
        state[:, lanes] = state[:, lanes] * ec[BLOCK - 1 : BLOCK, :] + dot(write_t, vrem)


def gated_kernel(
    x_ref, cot_ref, normed_ref, normedt_ref, y0_ref, y1_ref, small0_ref, small1_ref, pmt_ref,
    near0, x0, far0, near1, x1, far1,
    result_ref, dy0_ref, dy1_ref, dgate_ref, send_ref, keep_ref, gaing_ref, pre_ref,
    wg, wo, wnat, acc, sems,
):
    step = pl.program_id(0)
    width = wg.shape[2]
    core = acc.shape[1]
    pieces = (near0, x0, far0, near1, x1, far1)

    @pl.when(step == 0)
    def _():
        copies = load_halves(pieces, wg, sems, 0, pl.ds(0, width))
        load_halves(pieces, wo, sems, 8, pl.ds(width, width))
        acc[...] = jnp.zeros(acc.shape, F32)
        keep_ref[...] = jnp.zeros(keep_ref.shape, F32)
        gaing_ref[...] = jnp.zeros(gaing_ref.shape, F32)
        for copy in copies:
            copy.wait()

    normed = normed_ref[...]
    normed_t = normedt_ref[...]
    cot = cot_ref[0]
    y_refs = (y0_ref, y1_ref)
    small_refs = (small0_ref, small1_ref)
    gates, mixes = [], []
    squares = 0.0
    for half in range(HALVES):
        gate = dot(normed, wg[half])
        mixed = y_refs[half][...].astype(F32) * (gate * sigmoid(gate))
        squares = squares + jnp.sum(mixed * mixed, axis=-1, keepdims=True)
        gates.append(gate)
        mixes.append(mixed)
    cot_t = dot_nt(pmt_ref[...], cot).astype(BF16)

    @pl.when(step == 0)
    def _():
        for copy in load_halves(pieces, wo, sems, 8, pl.ds(width, width), False):
            copy.wait()
        for half in range(HALVES):
            wnat[half] = dot_tn(wo[half], pmt_ref[...]).astype(BF16)

    rms = lax.rsqrt(squares / (HALVES * width) + EPS)
    total = x_ref[0].astype(F32)
    inner = 0.0
    scaled = []
    for half in range(HALVES):
        gain = small_refs[half][6:7, :]
        gated = (mixes[half] * rms * gain).astype(BF16)
        total = total + dot(gated, wnat[half])
        keep_ref[half, :, width:] += dot(cot_t[0:core], gated)
        acc[half, :, width:] += dot(cot_t[core:], gated)
        grad = dot_nt(cot, wnat[half])
        gaing_ref[half : half + 1, :] += jnp.sum(grad * mixes[half] * rms, axis=0, keepdims=True)
        grad = grad * gain
        inner = inner + jnp.sum(grad * mixes[half], axis=-1, keepdims=True)
        scaled.append(grad)
    result_ref[0] = total.astype(BF16)
    factor = rms * rms * rms * (inner / (HALVES * width))
    for half, dy_ref in enumerate((dy0_ref, dy1_ref)):
        grad_mixed = rms * scaled[half] - mixes[half] * factor
        gate = gates[half]
        sg = sigmoid(gate)
        dy_ref[...] = (grad_mixed * (gate * sg)).astype(BF16)
        dgate = (grad_mixed * y_refs[half][...].astype(F32) * (sg * (1.0 + gate * (1.0 - sg)))).astype(BF16)
        dgate_ref[half] = dgate
        keep_ref[half, :, 0:width] += dot(normed_t[0:core], dgate)
        acc[half, :, 0:width] += dot(normed_t[core:], dgate)

    @pl.when(step == pl.num_programs(0) - 1)
    def _():
        send_ref[...] = acc[...].astype(BF16)
        pre_ref[:, 0:core] = along_lanes(
            sum(weighted_tiles(keep_ref[half, :, 0:width], wg[half, 0:core, :]) for half in range(HALVES))
        )
        pre_ref[:, core:] = along_lanes(
            sum(weighted_tiles(acc[half, :, 0:width], wg[half, core:, :]) for half in range(HALVES))
        )


def backward_kernel(first_head, has_maps, has_step, *refs):
    c_ref, vin_ref, dy_ref, state_ref, maps_ref, mapst_ref, steps_ref, cumr_ref, taps_ref, rate_ref = refs[:10]
    dvin_ref, dmaps_ref, dstep_ref, tapsg_ref, headg_ref, buf, dstate, dgt, vacc, vrems, dyes, pick, upper, mask = refs[-14:]
    step = pl.program_id(0)
    width = buf.shape[1]
    n = dstate.shape[0]
    hb = BLOCK // 2

    @pl.when(step == 0)
    def _():
        buf[pl.ds(BLOCK, 8), :] = jnp.zeros((8, width), F32)
        dstate[...] = jnp.zeros(dstate.shape, F32)
        row = lax.broadcasted_iota(jnp.int32, pick.shape, 0)
        col = lax.broadcasted_iota(jnp.int32, pick.shape, 1)
        fill_spread(mask, first_head)
        pick[...] = jnp.where(row % width // 64 + first_head == col, 1.0, 0.0).astype(BF16)
        row = lax.broadcasted_iota(jnp.int32, upper.shape, 0)
        col = lax.broadcasted_iota(jnp.int32, upper.shape, 1)
        upper[...] = jnp.where(row <= col, 1.0, 0.0).astype(BF16)
        tapsg_ref[...] = jnp.zeros(tapsg_ref.shape, F32)
        headg_ref[...] = jnp.zeros(headg_ref.shape, F32)

    write = maps_ref[:, 0:n]
    read = maps_ref[:, n : 2 * n]
    read_t = mapst_ref[n : 2 * n, :]
    gt = dot_nt(write, read)
    state = state_ref[0]
    ds = dstate[...]
    ds_b = ds.astype(BF16)
    carried = dot(read, state.astype(BF16))
    wds = dot(write, ds_b)
    lane = lax.broadcasted_iota(jnp.int32, (BLOCK, 128), 1)
    steps = steps_ref[...]
    cumc = jnp.where(lane < 32, steps, 0.0)
    dtc = jnp.where(lane < 32, pltpu.roll(steps, PAD - 32, 1), 0.0)
    ecum = jnp.exp(cumc)
    last = jnp.exp(cumc[BLOCK - 1 : BLOCK, :] - cumc)
    rem = last * dtc
    ec_all = spread(ecum, mask)
    lane_low = lane < 64
    sub = lax.broadcasted_iota(jnp.int32, (16, BLOCK), 0)
    tri = lax.broadcasted_iota(jnp.int32, (hb, hb), 1) >= lax.broadcasted_iota(jnp.int32, (hb, hb), 0)
    zeros = jnp.zeros((hb, hb), BF16)
    g00 = gt[0:hb, 0:hb]
    g01 = gt[0:hb, hb:]
    g11 = gt[hb:, hb:]
    dgt[...] = jnp.zeros(dgt.shape, F32)
    to_k = jnp.zeros((BLOCK, 128), F32)
    to_q = jnp.zeros((16, BLOCK), F32)
    for pair in range(width // 128):
        lanes = slice(pair * 128, pair * 128 + 128)
        cp = c_ref[:, lanes].astype(F32)
        v = cp * sigmoid(cp)
        vacc[:, lanes] = v
        dt_s = spread_pair(dtc, first_head // 2 + pair, lane_low)
        vdt = (v * dt_s).astype(BF16)
        dyp = dy_ref[:, lanes]
        us = []
        for j in range(2):
            h = first_head + 2 * pair + j
            ck = jnp.broadcast_to(cumc[:, h : h + 1], (BLOCK, hb))
            cq = cumr_ref[h : h + 1, :]
            d00 = jnp.exp(jnp.where(tri, cq[:, 0:hb] - ck[0:hb], NEG))
            d01 = jnp.exp(cq[:, hb:] - ck[0:hb])
            d11 = jnp.exp(jnp.where(tri, cq[:, hb:] - ck[hb:], NEG))
            mine = jnp.where(lane_low if j == 0 else jnp.logical_not(lane_low), dyp, jnp.zeros_like(dyp))
            qt = dot_nt(vdt, mine)
            e00 = d00 * qt[0:hb, 0:hb]
            e01 = d01 * qt[0:hb, hb:]
            e11 = d11 * qt[hb:, hb:]
            dgt[0:hb, 0:hb] += e00
            dgt[0:hb, hb:] += e01
            dgt[hb:, hb:] += e11
            a = jnp.concatenate(
                [
                    jnp.concatenate([(g00 * d00).astype(BF16), (g01 * d01).astype(BF16)], axis=1),
                    jnp.concatenate([zeros, (g11 * d11).astype(BF16)], axis=1),
                ],
                axis=0,
            )
            z = jnp.concatenate(
                [
                    jnp.concatenate([(g00 * e00).astype(BF16), (g01 * e01).astype(BF16)], axis=1),
                    jnp.concatenate([zeros, (g11 * e11).astype(BF16)], axis=1),
                ],
                axis=0,
            )
            us.append(dot(a, dyp))
            to_k = jnp.where(lane == h, dot(z, jnp.ones((BLOCK, 128), BF16)), to_k)
            to_q = to_q + dot(jnp.where(sub == h, 1.0, 0.0).astype(BF16), z)
        u = jnp.where(lane_low, us[0], us[1])
        ec = ec_all[:, lanes]
        rem_s = spread_pair(rem, first_head // 2 + pair, lane_low)
        dye = (dyp.astype(F32) * ec).astype(BF16)
        dv = dt_s * u + taps_ref[5:6, lanes] * dyp.astype(F32) + rem_s * wds[:, lanes]
        sg = sigmoid(cp)
        buf[0:BLOCK, lanes] = dv * (sg * (1.0 + cp * (1.0 - sg)))
        dyes[:, lanes] = dye
        vrems[:, lanes] = (v * rem_s).astype(BF16)
        dstate[:, lanes] = ds[:, lanes] * ec[BLOCK - 1 : BLOCK, :]
    dstate[...] += dot(read_t, dyes[...])
    dmaps_w = dot_nt(vrems[...], ds_b)
    dmaps_r = dot_nt(dyes[...], state.astype(BF16))
    dg_b = dgt[...].astype(BF16)
    dg_low = (dgt[...] - dg_b.astype(F32)).astype(BF16)
    dmaps_w = dmaps_w + dot(dg_b, read) + dot(dg_low, read)
    dmaps_r = dmaps_r + dot_tn(dg_b, write) + dot_tn(dg_low, write)
    if has_maps:
        dmaps_w = dmaps_w + refs[10][:, 0:n]
        dmaps_r = dmaps_r + refs[10][:, n : 2 * n]
    dmaps_ref[:, 0:n] = dmaps_w
    dmaps_ref[:, n : 2 * n] = dmaps_r

    def per_head(values):
        high = values.astype(BF16)
        low = (values - high.astype(F32)).astype(BF16)
        return dot(jnp.concatenate([high, low], axis=1), pick[...])

    v = vacc[...]
    dy = dy_ref[...].astype(F32)
    v_wds = per_head(v * wds)
    dy_c = per_head(dy * carried)
    skip_sum = jnp.sum(dy * v, axis=0, keepdims=True)
    ss = per_head(jnp.broadcast_to(jnp.sum(ds * state, axis=0, keepdims=True), (8, width)))
    sent = rem * v_wds
    d_last = ecum[BLOCK - 1 : BLOCK, :] * ss[0:1, :] + jnp.sum(sent, axis=0, keepdims=True)
    dcum = jnp.concatenate([to_q, jnp.zeros((112, BLOCK), F32)], axis=0).T - to_k + ecum * dy_c - sent
    token = lax.broadcasted_iota(jnp.int32, (BLOCK, 128), 0)
    dcum = dcum + jnp.where(token == BLOCK - 1, d_last, 0.0)
    dlog = dot_twice(upper[...], dcum)
    rate = rate_ref[7:8, :]
    slope = pltpu.roll(steps, 64, 1)
    ratio = jnp.where(dtc > 0, slope / dtc, 1.0)
    draw = to_k * ratio + (last * v_wds + dlog * rate) * slope
    mine = jnp.logical_and(lane >= first_head, lane < first_head + width // 64)
    draw = jnp.where(mine, draw, 0.0)
    dstep = draw.astype(BF16)
    dstep_ref[...] = dstep + refs[10 + has_maps][...] if has_step else dstep
    headg_ref[0:1, :] += jnp.sum(draw, axis=0, keepdims=True)
    headg_ref[1:2, :] += jnp.sum(dlog * dtc, axis=0, keepdims=True) * rate
    headg_ref[2:3, :] += per_head(jnp.broadcast_to(skip_sum, (8, width)))[0:1, :]

    vin = vin_ref[...].astype(F32)
    total = jnp.zeros((BLOCK, width), F32)
    for j in range(4):
        shifted = buf[pl.ds(3 - j, BLOCK), :]
        total = total + taps_ref[j : j + 1, :] * shifted
        tapsg_ref[j : j + 1, :] += jnp.sum(shifted * vin, axis=0, keepdims=True)
    tapsg_ref[4:5, :] += jnp.sum(buf[0:BLOCK, :], axis=0, keepdims=True)
    dvin_ref[...] = total.astype(BF16)
    buf[pl.ds(BLOCK, 8), :] = buf[pl.ds(0, 8), :]


def split_products(normedt_ref, groups, weight, send_ref, keep_ref, pre):
    core = keep_ref.shape[0]

    def product(target, first):
        col, total = 0, 0.0
        for group in groups:
            cols = slice(col, col + group.shape[-1])
            value = dot(normedt_ref[...], group[...])
            target[:, cols] = value.astype(target.dtype)
            total = total + weighted_tiles(value, weight[first : first + core, cols])
            col = cols.stop
        pre[:, first : first + core] = along_lanes(total)

    @pl.when(pl.program_id(0) == 0)
    def _():
        product(send_ref, core)

    @pl.when(pl.program_id(0) == 1)
    def _():
        product(keep_ref, 0)


def partial_kernel(normedt_ref, *refs):
    groups, pieces = refs[:-9], refs[-9:-5]
    keep_ref, send_ref, pre_ref, weight, sems = refs[-5:]

    @pl.when(pl.program_id(0) == 0)
    def _():
        for copy in load_rows(pieces, weight, sems):
            copy.wait()

    split_products(normedt_ref, groups, weight, send_ref, keep_ref, pre_ref)


def late_kernel(normedt_ref, dmaps_ref, statein_ref, statec_ref, taps_ref, pm_ref, shared_ref, gain_ref, pre0_ref, pre1_ref, *refs):
    count = HALVES * SEGMENTS
    tap_refs, head_refs = refs[:count], refs[count : 2 * count]
    groups, pieces = refs[2 * count : -16], refs[-16:-8]
    keep_ref, send_ref, dstate_ref, sums_ref, buf, weight, pre, sems = refs[-8:]
    length, n2 = statein_ref.shape
    width = weight.shape[0]
    seg_w = tap_refs[0].shape[1]
    step = pl.program_id(0)

    @pl.when(step == 0)
    def _():
        columns = weight.shape[1] - n2
        copies = load_rows(pieces[:4], weight.at[:, pl.ds(0, columns)], sems)
        copies += load_rows(pieces[4:], weight.at[:, pl.ds(columns, n2)], sems, 4)
        sums_ref[...] = jnp.zeros(sums_ref.shape, F32)
        for half, first in enumerate((16, 0)):
            mine = range(half * SEGMENTS, (half + 1) * SEGMENTS)
            for i, segment in enumerate(mine):
                sums_ref[first : first + 5, i * seg_w : (i + 1) * seg_w] = tap_refs[segment][0:5, :]
            sums_ref[first + 5 : first + 6, :] = gain_ref[half : half + 1, :]
            head = sum((head_refs[segment][...] for segment in mine[1:]), head_refs[mine[0]][...])
            for i in range(3):
                sums_ref[first + 6 : first + 7, i * PAD : (i + 1) * PAD] = head[i : i + 1, :]
        c = statec_ref[...]
        sg = sigmoid(c)
        dc = dmaps_ref[...] * (sg * (1.0 + c * (1.0 - sg)))
        buf[0:length, :] = dc
        buf[pl.ds(length, 8), :] = jnp.zeros((8, n2), F32)
        state_in = statein_ref[...]
        total = jnp.zeros((length, n2), F32)
        for j in range(4):
            shifted = buf[pl.ds(3 - j, length), :]
            total = total + taps_ref[j : j + 1, :] * shifted
            sums_ref[8 + j : 9 + j, 0:n2] = jnp.sum(shifted * state_in, axis=0, keepdims=True)
        sums_ref[12:13, 0:n2] = jnp.sum(dc, axis=0, keepdims=True)
        dstate_ref[...] = total.astype(BF16)
        for copy in copies:
            copy.wait()

    split_products(normedt_ref, groups + (dstate_ref,), weight, send_ref, keep_ref, pre)

    @pl.when(step == 1)
    def _():
        high, mid, low = split3(pre[...] + pre0_ref[...] + pre1_ref[...])
        total = dot_nt(high, pm_ref[...]) + dot_nt(mid, pm_ref[...]) + dot_nt(low, pm_ref[...])
        sums_ref[13:14, :] = total[0:1, :] / shared_ref[0:1, :]


def turn_value_kernel(*refs):
    pmt_ref, pieces = refs[0], refs[1:-7]
    tv_ref, to_ref, ts_ref, wv, wo, ws, sems = refs[-7:]
    copies = load_rows(pieces[:4], wv, sems) + load_rows(pieces[4:8], wo, sems, 4) + load_rows(pieces[8:], ws, sems, 8)
    for copy in copies:
        copy.wait()
    tv_ref[...] = dot_tn(wv[...], pmt_ref[...]).astype(BF16)
    to_ref[...] = dot_tn(wo[...], pmt_ref[...]).astype(BF16)
    ts_ref[...] = dot_tn(ws[...], pmt_ref[...]).astype(BF16)


def turn_gate_kernel(*refs):
    pmt_ref, pieces = refs[0], refs[1:-3]
    tg_ref, wg, sems = refs[-3:]
    for copy in load_halves(pieces, wg, sems, 0, pl.ds(0, wg.shape[2])):
        copy.wait()
    for half in range(HALVES):
        tg_ref[half] = dot_tn(wg[half], pmt_ref[...]).astype(BF16)


def input_kernel(*refs):
    x_ref, cot_ref, shared_ref, dgate_ref, dstate_ref, tg_ref, tv_ref, to_ref, ts_ref = refs[:9]
    count = HALVES * SEGMENTS
    dvin_refs, dstep_refs = refs[9 : 9 + count], refs[9 + count : 9 + count + HALVES]
    grad_ref = refs[-1]
    width = x_ref.shape[2]
    total = dot(dstate_ref[...], ts_ref[...])
    for half, weights in enumerate((tv_ref, to_ref)):
        total = total + dot(dgate_ref[half], tg_ref[half]) + dot(dstep_refs[half][...], weights[width:, :])
        for segment in range(SEGMENTS):
            dvin = dvin_refs[half * SEGMENTS + segment][...]
            cols = dvin.shape[1]
            total = total + dot(dvin, weights[segment * cols : segment * cols + cols, :])
    x = x_ref[0].astype(F32)
    inv = lax.rsqrt(jnp.mean(x * x, axis=-1, keepdims=True) + EPS)
    scaled = total * shared_ref[0:1, :]
    inner = jnp.mean(scaled * x, axis=-1, keepdims=True)
    grad_ref[0] = cot_ref[0].astype(F32) + inv * scaled - x * (inv * inv * inv * inner)


def early_end_kernel(keep_ref, *refs):
    gate_ref, out_ref = refs[-2:]
    rows, width = gate_ref.shape
    total = keep_ref[0:rows, :]
    for ref in refs[:-2]:
        total = total + ref[...].astype(F32)
    gate_ref[...] = total[:, 0:width]
    out_ref[...] = total[:, width:]


def late_end_kernel(keep_ref, *refs):
    value_ref, step_ref, state_ref = refs[-3:]
    rows, width = value_ref.shape
    total = keep_ref[0:rows, :]
    for ref in refs[:-3]:
        total = total + ref[...].astype(F32)
    value_ref[...] = total[:, 0:width]
    step_ref[...] = total[:, width : width + PAD].T[0 : step_ref.shape[0], :]
    state_ref[...] = total[:, width + PAD :]


def sums_end_kernel(
    sums_ref, got_ref,
    prenorm_ref, taps_ref, shift_ref, staps_ref, sshift_ref, bias_ref, decay_ref, skip_ref, gain_ref,
):
    total = sums_ref[...] + got_ref[...]
    n2 = sshift_ref.shape[0]
    heads = bias_ref.shape[0]
    taps_ref[...] = total[0:4, :]
    shift_ref[...] = total[4, :]
    gain_ref[...] = total[5, :]
    bias_ref[...] = total[6, 0:PAD][0:heads]
    decay_ref[...] = total[6, PAD : 2 * PAD][0:heads]
    skip_ref[...] = total[6, 2 * PAD : 3 * PAD][0:heads]
    staps_ref[...] = total[8:12, 0:n2]
    sshift_ref[...] = total[12, 0:n2]
    prenorm_ref[...] = total[13, :]


def call(body, grid, in_specs, out_specs, out_shape, scratch=(), flops=0, vmem=24, aliases={}):
    return pl.pallas_call(
        body,
        grid=grid,
        in_specs=in_specs,
        out_specs=out_specs,
        out_shape=out_shape,
        scratch_shapes=list(scratch),
        input_output_aliases=aliases,
        compiler_params=pltpu.CompilerParams(
            vmem_limit_bytes=vmem * MIB, dimension_semantics=("arbitrary",) * len(grid)
        ),
        cost_estimate=pl.CostEstimate(flops=flops, bytes_accessed=10_000_000, transcendentals=0),
    )


def shape(dims, dtype=F32):
    return jax.ShapeDtypeStruct(dims, dtype)


def hbm(v):
    return pltpu.with_memory_space_constraint(v, pltpu.HBM)


def fixed(dims, *index):
    return pl.BlockSpec(dims, lambda *_: index)


ANYWHERE = pl.BlockSpec(memory_space=pl.ANY)
AXES = ("dp", "tensor")
TENSOR, CORE, CHIP = 1, 2, 4
FAR = 3


def swap(v, mask):
    count = lax.axis_size("dp") * lax.axis_size("tensor")
    return lax.ppermute(v, AXES, [(i, i ^ mask) for i in range(count)])


def far_masks():
    count = lax.axis_size("dp") * lax.axis_size("tensor")
    return [m << FAR for m in range(1, count >> FAR)]


def start_near(pack):
    return [pack] + [swap(pack, m) for m in far_masks()]


def start_far(v, rows):
    return [swap(v[(i + 1) * rows : (i + 2) * rows].astype(BF16), m) for i, m in enumerate(far_masks())]


def wide(*parts):
    return sum((part.astype(F32) for part in parts[1:]), parts[0].astype(F32))


def meet(*values):
    return lax.optimization_barrier(values)


def after(v, *others):
    return lax.optimization_barrier((v,) + others)[0]


def local(
    inputs,
    prenorm,
    gate_weight,
    value_weight,
    state_weight,
    step_weight,
    value_conv,
    value_shift,
    state_conv,
    state_shift,
    step_shift,
    decay_log,
    skip_scale,
    gated_gain,
    output_matrix,
    cotangent,
):
    length, width = inputs.shape[1:]
    rows, w = gate_weight.shape
    heads = step_weight.shape[1]
    n = state_weight.shape[1] // 2
    n2 = 2 * n
    blocks = length // BLOCK
    quarter = width // 4
    wp = w + PAD
    whole = lambda v: fixed(v.shape, *([0] * v.ndim))
    row_block = lambda dims: pl.BlockSpec(dims, lambda b: (b, 0))
    col_block = lambda dims: pl.BlockSpec(dims, lambda b: (0, b))
    tokens = pl.BlockSpec((1, BLOCK, width), lambda b: (0, b, 0))
    halves = lambda last: pl.BlockSpec((HALVES, BLOCK, last), lambda b: (0, b, 0))
    square = fixed((width, width), 0, 0)
    small_spec = fixed((8, w), 0, 0)
    sems = lambda count: pltpu.SemaphoreType.DMA((count,))

    to_pack = (
        value_conv, value_shift, skip_scale, gated_gain, step_shift, decay_log, prenorm, state_shift,
        gate_weight, value_weight, step_weight.T, output_matrix.T,
    )
    small, shared, vpack, gpack = call(
        pack_kernel,
        (1,),
        [whole(v) for v in to_pack],
        [small_spec, fixed((8, width), 0, 0), fixed((rows, wp), 0, 0), fixed((rows, 2 * w), 0, 0)],
        [shape((8, w)), shape((8, width)), shape((rows, wp), BF16), shape((rows, 2 * w), BF16)],
        flops=1_000_000,
    )(*(hbm(v) for v in to_pack))

    spot = jnp.arange(width)
    owner = lax.axis_index("dp") ^ (
        spot // (2 * quarter) + 2 * (spot // quarter % 2) + 4 * (spot % quarter // rows)
    )
    natural = owner * rows + spot % rows
    pm = (spot[:, None] == natural[None, :]).astype(BF16)
    pmt = (natural[:, None] == spot[None, :]).astype(BF16)

    near = jnp.concatenate(start_near(state_weight), axis=0)
    chip = swap(near, CHIP)
    chip, *value_near = meet(chip, *start_near(vpack))
    state_own = (near, chip, swap(near, CORE), swap(chip, CORE))
    value_near = jnp.concatenate(value_near, axis=0)
    value_chip, value_y = swap(value_near, CHIP), swap(value_near, TENSOR)
    gate_near = start_near(after(gpack, near))
    small_got = swap(small, TENSOR)

    normed, normed_t, state_in, state_c, maps, maps_t = call(
        maps_kernel,
        (blocks,),
        [tokens, square] + [ANYWHERE] * 4 + [fixed((4, n2), 0, 0), fixed((8, width), 0, 0)],
        [row_block((BLOCK, width)), col_block((width, BLOCK)), row_block((BLOCK, n2)), row_block((BLOCK, n2)),
         row_block((BLOCK, n2)), col_block((n2, BLOCK))],
        [shape((length, width), BF16), shape((width, length), BF16), shape((length, n2)), shape((length, n2)),
         shape((length, n2), BF16), shape((n2, length), BF16)],
        [pltpu.VMEM((BLOCK + 8, n2), F32), pltpu.VMEM((width, n2), BF16), sems(4)],
        flops=6_000_000_000,
    )(inputs, pm, *state_own, state_conv, shared)

    def forward(pieces, half, normed):
        return call(
            forward_kernel,
            (blocks,),
            [ANYWHERE] * len(pieces)
            + [row_block((BLOCK, width)), small_spec, row_block((BLOCK, n2)), col_block((n2, BLOCK))],
            [row_block((BLOCK, w))] * 3 + [pl.BlockSpec((1, n, w), lambda b: (b, 0, 0))]
            + [row_block((BLOCK, PAD)), col_block((16, BLOCK))],
            [pltpu.HBM((length, w), BF16), pltpu.HBM((length, w), F32), shape((length, w)),
             pltpu.HBM((blocks, n, w), F32), pltpu.HBM((length, PAD), F32), pltpu.HBM((16, length), F32)],
            [pltpu.VMEM((BLOCK + 8, w), F32), pltpu.VMEM((n, w), F32), pltpu.VMEM((width, wp), BF16),
             pltpu.VMEM((2 * PAD, w), BF16), sems(4)],
            flops=12_000_000_000,
        )(*pieces, normed, smalls[half], maps, maps_t)

    normed, value_chip, value_y, small_got, *gate_near = meet(normed, value_chip, value_y, small_got, *gate_near)
    smalls = (small, small_got)
    value_own = (value_near, value_chip, swap(value_near, CORE), swap(value_chip, CORE))
    value_yx = swap(value_chip, TENSOR)
    gate_near = jnp.concatenate(gate_near, axis=0)
    gate_y, gate_x = swap(gate_near[:, :w], TENSOR), swap(gate_near, CHIP)
    out_y = swap(gate_near[:, w:], TENSOR)
    scan_own = forward(value_own, 0, after(normed, gate_near))
    normed, value_y, value_yx, gate_x, gate_y, _ = meet(normed, value_y, value_yx, gate_x, gate_y, scan_own[2])
    gate_yx, out_yx = swap(gate_y, CHIP), swap(gate_x[:, w:], TENSOR)
    value_other = (value_y, value_yx, swap(value_y, CORE), swap(value_yx, CORE))
    scan_other = forward(value_other, 1, normed)
    scans = (scan_own, scan_other)

    both_w = (HALVES, width, w)
    out_y, gate_yx, out_yx, _ = meet(out_y, gate_yx, out_yx, scan_other[2])
    far = jnp.concatenate([jnp.concatenate([gate_y, out_y], axis=1), jnp.concatenate([gate_yx, out_yx], axis=1)], axis=0)
    gate_pieces = (gate_near, gate_x, far)
    gate_pieces += tuple(swap(v, CORE) for v in gate_pieces)
    given = (after(pmt, far), *value_own, *value_other, *state_own)
    turned = call(
        turn_value_kernel,
        (1,),
        [square] + [ANYWHERE] * 12,
        [fixed((wp, width), 0, 0), fixed((wp, width), 0, 0), fixed((n2, width), 0, 0)],
        [shape((wp, width), BF16), shape((wp, width), BF16), shape((n2, width), BF16)],
        [pltpu.VMEM((width, wp), BF16), pltpu.VMEM((width, wp), BF16), pltpu.VMEM((width, n2), BF16), sems(12)],
        flops=4_000_000_000,
    )(*given)
    half_rows = (HALVES, width // 2, 2 * w)
    turned = list(turned)
    turned[0], *gate_pieces = meet(turned[0], *gate_pieces)
    result, dy0, dy1, dgate, early_send, early_keep, gain_partial, gate_pre = call(
        gated_kernel,
        (blocks,),
        [tokens, tokens, row_block((BLOCK, width)), col_block((width, BLOCK)), row_block((BLOCK, w)),
         row_block((BLOCK, w)), small_spec, small_spec, square] + [ANYWHERE] * 6,
        [tokens, row_block((BLOCK, w)), row_block((BLOCK, w)), halves(w), fixed(half_rows, 0, 0, 0),
         fixed(half_rows, 0, 0, 0), fixed((HALVES, w), 0, 0), fixed((8, width), 0, 0)],
        [shape(inputs.shape, BF16), shape((length, w), BF16), shape((length, w), BF16),
         shape((HALVES, length, w), BF16), shape(half_rows, BF16), shape(half_rows), shape((HALVES, w)),
         shape((8, width))],
        [pltpu.VMEM(both_w, BF16), pltpu.VMEM(both_w, BF16), pltpu.VMEM(both_w, BF16), pltpu.VMEM(half_rows, F32),
         sems(16)],
        flops=25_000_000_000,
        vmem=48,
    )(inputs, cotangent, normed, normed_t, scans[0][2], scans[1][2], *smalls, pmt, *gate_pieces)

    seg_w = w // SEGMENTS
    seg_heads = heads // SEGMENTS

    def backward(half, segment, dy, dmaps=None, dstep=None):
        back = lambda dims, col=0: pl.BlockSpec(dims, lambda b: (blocks - 1 - b, col))
        value_in, value_c, _, states, steps, cumr = scans[half]
        extra = ([dmaps] if dmaps is not None else []) + ([dstep] if dstep is not None else [])
        return call(
            functools.partial(backward_kernel, segment * seg_heads, dmaps is not None, dstep is not None),
            (blocks,),
            [back((BLOCK, seg_w), segment)] * 3
            + [pl.BlockSpec((1, n, seg_w), lambda b: (blocks - 1 - b, 0, segment)), back((BLOCK, n2)),
               pl.BlockSpec((n2, BLOCK), lambda b: (0, blocks - 1 - b))] + [back((BLOCK, PAD))]
            + [pl.BlockSpec((16, BLOCK), lambda b: (0, blocks - 1 - b)), fixed((8, seg_w), 0, segment),
               fixed((8, PAD), 0, 1)] + [back((BLOCK, v.shape[1])) for v in extra],
            [back((BLOCK, seg_w)), back((BLOCK, n2)), back((BLOCK, PAD)), fixed((8, seg_w), 0, 0), fixed((8, PAD), 0, 0)],
            [shape((length, seg_w), BF16), shape((length, n2)), shape((length, PAD), BF16), shape((8, seg_w)),
             shape((8, PAD))],
            [pltpu.VMEM((BLOCK + 8, seg_w), F32), pltpu.VMEM((n, seg_w), F32), pltpu.VMEM((BLOCK, BLOCK), F32),
             pltpu.VMEM((BLOCK, seg_w), F32), pltpu.VMEM((BLOCK, seg_w), BF16),
             pltpu.VMEM((BLOCK, seg_w), BF16), pltpu.VMEM((2 * seg_w, PAD), BF16), pltpu.VMEM((BLOCK, BLOCK), BF16),
             pltpu.VMEM((2 * PAD, seg_w), BF16)],
            flops=12_000_000_000,
        )(hbm(value_c), hbm(value_in), dy, hbm(states), maps, maps_t, hbm(steps), hbm(cumr), smalls[half], smalls[half],
          *extra)

    core = width // 2
    lead = pl.BlockSpec((core, length), lambda b: (1 - b, 0))
    split_specs = lambda cols: [fixed((core, cols), 0, 0)] * 2
    split_shapes = lambda cols: [shape((core, cols)), shape((core, cols), BF16)]

    early_got = swap(early_send, CORE)
    other0 = backward(1, 0, dy1)
    early_keep, early_got, _ = meet(early_keep, early_got, other0[2])
    gate = wide(early_keep[:, :, :w], early_got[:, :, :w])
    out = wide(early_keep[:, :, w:], early_got[:, :, w:])
    gate_out, gate = gate[1].astype(BF16), gate[0]
    out_out, out = out[:, quarter:].astype(BF16), out[:, :quarter]
    gate_got, out_got = swap(gate_out, TENSOR), swap(out_out, CHIP)
    other1 = backward(1, 1, after(dy1, gate_out, gate, out_out, out), other0[1], other0[2])
    gate, out, gate_got, out_got, _ = meet(gate, out, gate_got, out_got, other1[2])
    gate, out = wide(gate, gate_got), wide(out, out_got)
    gate_out, gate = gate[quarter:].astype(BF16), gate[:quarter]
    out_out, out = out[1].astype(BF16), out[0]
    gate_got, out_got = swap(gate_out, CHIP), swap(out_out, TENSOR)
    groups = (other0[0], other1[0], after(other1[2], gate_out, gate, out_out, out))
    other_keep, other_send, other_pre = call(
        partial_kernel,
        (2,),
        [lead] + [whole(v) for v in groups] + [ANYWHERE] * 4,
        split_specs(wp) + [fixed((8, width), 0, 0)],
        split_shapes(wp) + [shape((8, width))],
        [pltpu.VMEM((width, wp), BF16), sems(4)],
        flops=3_000_000_000,
    )(normed_t, *groups, *value_other)
    other_got = swap(other_send, CORE)
    own0 = backward(0, 0, after(dy0, other_send), other1[1])
    gate, out, gate_got, out_got, other_keep, other_got, _ = meet(
        gate, out, gate_got, out_got, other_keep, other_got, own0[2]
    )
    other_out = wide(other_keep, other_got).astype(BF16)
    other_got = swap(other_out, TENSOR)
    early = jnp.concatenate([wide(gate, gate_got), wide(out, out_got)], axis=1)
    early_far = start_far(early, rows)
    own1 = backward(0, 1, after(dy0, other_out, early), own0[1], own0[2])

    def end(body, given, dims):
        return call(
            body, (1,), [whole(v) for v in given], [fixed(d, *([0] * len(d))) for d in dims], [shape(d) for d in dims],
            flops=1_000_000,
        )(*given)

    dmaps, other_got, early, *early_far = meet(own1[1], other_got, early, *early_far)
    gate_grad, out_grad = end(early_end_kernel, (early, *early_far), ((rows, w), (rows, w)))
    groups = (own0[0], own1[0], own1[2])
    parts = (own0, own1, other0, other1)
    given = (
        (dmaps, state_in, state_c, state_conv, pm, shared, gain_partial, gate_pre, other_pre)
        + tuple(part[3] for part in parts) + tuple(part[4] for part in parts) + groups
    )
    late_keep, late_send, dstate, sums = call(
        late_kernel,
        (2,),
        [lead] + [whole(v) for v in given] + [ANYWHERE] * 8,
        split_specs(wp + n2) + [fixed((length, n2), 0, 0), fixed((24, width), 0, 0)],
        split_shapes(wp + n2) + [shape((length, n2), BF16), shape((24, width))],
        [pltpu.VMEM((length + 8, n2), F32), pltpu.VMEM((width, wp + n2), BF16), pltpu.VMEM((8, width), F32), sems(8)],
        flops=4_000_000_000,
    )(normed_t, *given, *value_own, *state_own)
    late_got, sums_got = swap(late_send, CORE), swap(sums[:16], TENSOR)
    turned_gate = call(
        turn_gate_kernel,
        (1,),
        [square] + [ANYWHERE] * 6,
        [fixed(both_w, 0, 0, 0)],
        [shape(both_w, BF16)],
        [pltpu.VMEM(both_w, BF16), sems(16)],
        flops=2_000_000_000,
    )(after(pmt, late_send), *gate_pieces)[0]
    late_keep, late_got, other_got, sums, sums_got, turned_gate = meet(
        late_keep, late_got, other_got, sums, sums_got, turned_gate
    )
    late = wide(late_keep, late_got)
    late = jnp.concatenate([late[:, :wp] + other_got.astype(F32), late[:, wp:]], axis=1)
    late_out, late = late[quarter:].astype(BF16), late[:quarter]
    late_got = swap(late_out, CHIP)
    sums = jnp.concatenate([sums[16:] + sums_got[:8], sums[8:16] + sums_got[8:]], axis=0)
    sums_got = swap(sums, CORE)

    def input_part(dgate, first, grad=None):
        token = pl.BlockSpec((1, BLOCK, width), lambda b: (0, b + first, 0))
        tall = lambda cols: pl.BlockSpec((BLOCK, cols), lambda b: (b + first, 0))
        given = (
            (inputs, cotangent, shared, dgate, dstate, turned_gate, *turned)
            + tuple(part[0] for part in parts) + (own1[2], other1[2])
        )
        return call(
            input_kernel,
            (blocks // 2,),
            [token, token, fixed((8, width), 0, 0), pl.BlockSpec((HALVES, BLOCK, w), lambda b: (0, b + first, 0)), tall(n2),
             fixed(both_w, 0, 0, 0)] + [whole(v) for v in turned] + [tall(seg_w)] * len(parts) + [tall(PAD)] * HALVES
            + ([] if grad is None else [ANYWHERE]),
            [token],
            [shape(inputs.shape)],
            flops=6_000_000_000,
            aliases={} if grad is None else {len(given): 0},
        )(*given, *(() if grad is None else (grad,)))[0]

    input_grad = input_part(after(dgate, late_out, late, sums), 0)
    sums, sums_got, input_grad = meet(sums, sums_got, input_grad)
    sums = sums + sums_got
    bits = [1 << FAR]
    while 2 * bits[-1] < lax.axis_size("dp") * lax.axis_size("tensor"):
        bits.append(2 * bits[-1])
    bits.append(CHIP)
    sums_got = swap(sums, bits[0])
    late, sums, sums_got, late_got = meet(late, sums, sums_got, late_got)
    late = wide(late, late_got)
    late_far = start_far(late, rows)
    sums = sums + sums_got
    sums_got = swap(sums, bits[1])
    input_grad = input_part(after(dgate, late, sums), blocks // 2, input_grad)
    sums, sums_got, input_grad = meet(sums, sums_got, input_grad)
    for bit in bits[2:]:
        sums = sums + sums_got
        sums_got = swap(sums, bit)

    value_grad, step_grad, state_grad = end(
        late_end_kernel, (late, *late_far), ((rows, w), (heads, rows), (rows, n2))
    )
    state_grad = state_grad + swap(state_grad, TENSOR)
    prenorm_grad, taps, shift, state_taps, state_bias, bias, decay, skip, gain = end(
        sums_end_kernel,
        (sums, sums_got),
        ((width,), (4, w), (w,), (4, n2), (n2,), (heads,), (heads,), (heads,), (w,)),
    )
    return (
        result, input_grad, prenorm_grad, gate_grad, value_grad, state_grad, step_grad.T, taps, shift, state_taps,
        state_bias, bias, decay, skip, gain, out_grad.T,
    )


def solution(mesh):
    in_specs = (
        P(("dp", "tensor"), None, None),
        P(),
        P("dp", "tensor"),
        P("dp", "tensor"),
        P("dp", None),
        P("dp", "tensor"),
        P(None, "tensor"),
        P("tensor"),
        P(),
        P(),
        P("tensor"),
        P("tensor"),
        P("tensor"),
        P("tensor"),
        P("tensor", "dp"),
        P(("dp", "tensor"), None, None),
    )
    out_specs = (
        P(("dp", "tensor"), None, None),
        P(("dp", "tensor"), None, None),
        P(),
        P("dp", "tensor"),
        P("dp", "tensor"),
        P("dp", None),
        P("dp", "tensor"),
        P(None, "tensor"),
        P("tensor"),
        P(),
        P(),
        P("tensor"),
        P("tensor"),
        P("tensor"),
        P("tensor"),
        P("tensor", "dp"),
    )
    return jax.shard_map(local, mesh=mesh, in_specs=in_specs, out_specs=out_specs, check_vma=False)
```
